32 devices in a mesh: dp: 16 (over z, y, core), tensor: 2 (over x).
Axes of the slice: x: 2, y: 2, z: 4, core: 2. Of those that a mesh axis runs over, the one named last changes fastest.
Arguments:
- block_input: bfloat16 [4096, 2560], P(('dp', 'tensor')), may hold values from -6 to 6
- starts: int32 [4096], P('dp'), may hold values from 0 to 1, as said below
- cotangent: bfloat16 [4096, 2560], P(('dp', 'tensor')), may hold values from -6 to 6
- gain_mixer: bfloat16 [2560], P('dp'), may hold values from 0.5 to 1.5
- w_branch: bfloat16 [2560, 2560], P(None, ('tensor', 'dp')), may hold values from -0.125 to 0.125
- w_signal: bfloat16 [2560, 2560], P(None, ('tensor', 'dp')), may hold values from -0.125 to 0.125
- w_input_gate: bfloat16 [10, 256, 256], P('tensor', 'dp'), may hold values from -0.375 to 0.375
- w_decay_gate: bfloat16 [10, 256, 256], P('tensor', 'dp'), may hold values from -0.375 to 0.375
- conv_taps: bfloat16 [2560, 4], P(('tensor', 'dp')), may hold values from -3 to 3
- decay_param: bfloat16 [2560], P(('tensor', 'dp')), may hold values from -9 to -2
- w_mixout: bfloat16 [2560, 2560], P(('tensor', 'dp')), may hold values from -0.5 to 0.5
- gain_dense: bfloat16 [2560], P('dp'), may hold values from 0.5 to 1.5
- w_gate: bfloat16 [2560, 7680], P(None, ('tensor', 'dp')), may hold values from -0.125 to 0.125
- w_up: bfloat16 [2560, 7680], P(None, ('tensor', 'dp')), may hold values from -0.125 to 0.125
- w_down: bfloat16 [7680, 2560], P(('tensor', 'dp')), may hold values from -0.125 to 0.125
Outputs:
- block_output: bfloat16 [4096, 2560], P(('dp', 'tensor'))
- grad_input: float32 [4096, 2560], P(('dp', 'tensor'))
- grad_gain_mixer: float32 [2560], P('dp')
- grad_w_branch: float32 [2560, 2560], P(None, ('tensor', 'dp'))
- grad_w_signal: float32 [2560, 2560], P(None, ('tensor', 'dp'))
- grad_input_gate: float32 [10, 256, 256], P('tensor', 'dp')
- grad_decay_gate: float32 [10, 256, 256], P('tensor', 'dp')
- grad_conv_taps: float32 [2560, 4], P(('tensor', 'dp'))
- grad_decay_param: float32 [2560], P(('tensor', 'dp'))
- grad_w_mixout: float32 [2560, 2560], P(('tensor', 'dp'))
- grad_gain_dense: float32 [2560], P('dp')
- grad_w_gate: float32 [2560, 7680], P(None, ('tensor', 'dp'))
- grad_w_up: float32 [2560, 7680], P(None, ('tensor', 'dp'))
- grad_w_down: float32 [7680, 2560], P(('tensor', 'dp'))
The draws below stay inside these ranges and needn't reach their ends.
Inputs may be any that keep to these rules, and one draw needn't show every extreme that they name: starts[0] is 1; the distance between consecutive ones, and from the last one to the end, is at most 1024, and one distance equals 1024 exactly.
All inputs are finite; a program needn't handle non-finite values.
Results may differ from the reference program's by a relative error of at most 0.02.
Values may be sent and summed in bfloat16 or wider, within the bound.
No kernel may reach another device: no remote copies, remote signals or barrier semaphores. Data moves between devices by JAX's collectives and lax.ppermute only.
A program may use at most 320 MiB of HBM per device.

```python
import jax
import jax.numpy as jnp
from jax import lax

D = 2560
FF = 7680
HEADS = 10
BLOCK = 256
CONV = 4
MAXLEN = 1024
LRU = 2560
TOKENS = 4096


def draw_starts(key, part):
    key_len, key_place = jax.random.split(jax.random.fold_in(key, 17))
    lowest = MAXLEN // 32 + 1
    lengths = jax.random.randint(key_len, (TOKENS,), lowest, MAXLEN + 1)
    place = jax.random.randint(key_place, (), 0, max(TOKENS // MAXLEN - 1, 1))
    lengths = jnp.where(jnp.arange(TOKENS) == place, MAXLEN, lengths)
    offsets = jnp.cumsum(lengths) - lengths
    return jnp.zeros((TOKENS,), jnp.int32).at[offsets].set(1, mode='drop')


def with_spikes(drawn, key, source, target, parts, factor):
    owner, partner = [(jnp.arange(drawn.shape[dim]) // (drawn.shape[dim] // parts)).reshape([-1 if axis == dim else 1 for axis in range(drawn.ndim)]) for dim in (source, target)]
    chosen = jax.random.permutation(key, parts)[partner]
    strong = (owner == chosen) | (owner == (partner + parts // 2) % parts)
    return jnp.where(strong, factor * drawn, drawn)


def levels(key, dims, shards, low, largest):
    loudness = 1.0
    for axis_at, parts in shards:
        steps = jax.random.uniform(jax.random.fold_in(jax.random.fold_in(key, 6), axis_at), (parts,), jnp.float32, low / len(shards), largest / len(shards))
        loudness = loudness * jnp.repeat(jnp.exp(steps), dims[axis_at] // parts).reshape((-1,) + (1,) * (len(dims) - 1 - axis_at))
    return loudness


def gaussian(stream_key, dims, scale, reach, cuts=(), held_as=jnp.bfloat16):
    entries = scale * jax.random.normal(stream_key, dims, jnp.float32)
    if cuts:
        entries = entries * levels(stream_key, dims, cuts, -0.22, 0.18)
    return jnp.clip(entries, -reach, reach).astype(held_as)


def gaussian_with(stream_key, shape, deviation, reach, shards, heavy, kind=jnp.bfloat16):
    array = deviation * jax.random.normal(stream_key, shape, jnp.float32)
    if shards:
        array = array * levels(stream_key, shape, shards, -0.22, 0.18)
    return jnp.clip(with_spikes(array, jax.random.fold_in(stream_key, 3), *heavy), -reach, reach).astype(kind)


def setup_inputs(seed: int = 0) -> dict:
    arg_keys = jax.random.split(jax.random.key(seed), 16)
    block_input = gaussian_with(arg_keys[0], (TOKENS, D), 1.0, 6.0, ((0, 32),), (0, 1, 32, 2.75))
    starts = draw_starts(jax.random.fold_in(arg_keys[15], 71), 0)
    cotangent = gaussian(arg_keys[2], (TOKENS, D), 1.0, 6.0, ((0, 32),))
    gain_mixer = jnp.clip(1.0 + 0.1 * jax.random.normal(arg_keys[3], (D,), jnp.float32), 0.5, 1.5).astype(jnp.bfloat16)
    w_branch = gaussian(arg_keys[4], (D, LRU), D ** -0.5, 0.125, ((1, 32),))
    w_signal = gaussian(arg_keys[5], (D, LRU), D ** -0.5, 0.125, ((1, 32),))
    w_input_gate = gaussian(arg_keys[6], (HEADS, BLOCK, BLOCK), BLOCK ** -0.5, 0.375, ((0, 2), (1, 16)))
    w_decay_gate = gaussian(arg_keys[7], (HEADS, BLOCK, BLOCK), BLOCK ** -0.5, 0.375, ((0, 2), (1, 16)))
    conv_taps = gaussian(arg_keys[8], (LRU, CONV), CONV ** -0.5, 3.0, ((0, 32),))
    decay_param = jnp.clip(-9.0 + 7.0 * jax.random.uniform(arg_keys[9], (LRU,), jnp.float32) ** levels(arg_keys[9], (LRU,), ((0, 32),), -0.2, 0.2), -9.0, -2.0).astype(jnp.bfloat16)
    w_mixout = gaussian(arg_keys[10], (LRU, D), (LRU // 16) ** -0.5, 0.5, ((0, 32),))
    gain_dense = jnp.clip(1.0 + 0.1 * jax.random.normal(arg_keys[11], (D,), jnp.float32), 0.5, 1.5).astype(jnp.bfloat16)
    w_gate = gaussian(arg_keys[12], (D, FF), D ** -0.5, 0.125, ((1, 32),))
    w_up = gaussian(arg_keys[13], (D, FF), D ** -0.5, 0.125, ((1, 32),))
    w_down = gaussian(arg_keys[14], (FF, D), (FF // 4) ** -0.5, 0.125, ((0, 32),))
    return {"block_input": block_input, "starts": starts, "cotangent": cotangent, "gain_mixer": gain_mixer, "w_branch": w_branch, "w_signal": w_signal, "w_input_gate": w_input_gate, "w_decay_gate": w_decay_gate, "conv_taps": conv_taps, "decay_param": decay_param, "w_mixout": w_mixout, "gain_dense": gain_dense, "w_gate": w_gate, "w_up": w_up, "w_down": w_down}


EPS = 1e-06
HIGH = lax.Precision.HIGHEST

@jax.custom_vjp
def low(v):
    return lax.optimization_barrier(v.astype(jnp.bfloat16)).astype(jnp.float32)

@jax.custom_vjp
def low_back(v):
    return v

def low_keep(v):
    return (low(v), None)

def low_pass(kept, grad):
    return (grad,)

def back_keep(v):
    return (v, None)

def back_low(kept, grad):
    return (low(grad),)
low.defvjp(low_keep, low_pass)
low_back.defvjp(back_keep, back_low)

def normed(value, gain):
    return value * lax.rsqrt(lax.optimization_barrier(jnp.mean(value * value, axis=-1, keepdims=True)) + EPS) * gain

def gelu_tanh(value):
    return jax.nn.gelu(value, approximate=True)

def affine(first, second):
    return (first[0] * second[0], second[0] * first[1] + second[1])

def lru_coeffs(ga_pre, gx_pre, conv_out, param, reset):
    gate_a = jax.nn.sigmoid(ga_pre)
    gate_x = jax.nn.sigmoid(gx_pre)
    log_a = -8.0 * gate_a * jax.nn.softplus(param)
    keep = 1.0 - reset
    decay = jnp.exp(log_a) * keep
    multiplier = jnp.sqrt(-jnp.expm1(2.0 * log_a)) * keep + reset
    return (decay, gate_x * conv_out * multiplier)

def conv_mix(padded, taps, masks):
    lag = CONV - 1
    count = masks.shape[0]
    total = taps[:, 0] * padded[lag:lag + count] * masks[:, 0:1]
    for shift_k in range(1, CONV):
        total = total + taps[:, shift_k] * padded[lag - shift_k:lag - shift_k + count] * masks[:, shift_k:shift_k + 1]
    return total

def reference(block_input, starts, cotangent, gain_mixer, w_branch, w_signal, w_input_gate, w_decay_gate, conv_taps, decay_param, w_mixout, gain_dense, w_gate, w_up, w_down):
    lag = CONV - 1
    count = starts.shape[0]
    reset = starts.astype(jnp.float32)[:, None]
    cumulative = jnp.cumsum(starts).astype(jnp.int32)
    padded_cum = jnp.concatenate([jnp.zeros((lag,), jnp.int32), cumulative])
    masks = jnp.stack([(cumulative - padded_cum[lag - k:lag - k + count] == 0).astype(jnp.float32) for k in range(CONV)], axis=1)

    def forward(x, gain_one, wb, ws, wig, wdg, taps, param, wo, gain_two, wg, wu, wd):
        h_one = low(normed(x, gain_one))
        branch = gelu_tanh(low_back(jnp.dot(h_one, wb, precision=HIGH)))
        signal = low(low_back(jnp.dot(h_one, ws, precision=HIGH)))
        padded = jnp.concatenate([jnp.zeros((lag, signal.shape[1]), jnp.float32), signal])
        mixed = low(conv_mix(padded, taps, masks))
        grouped = mixed.reshape(count, HEADS, BLOCK)
        gx_pre = low_back(jnp.einsum('thb,hbc->thc', grouped, wig, precision=HIGH).reshape(mixed.shape))
        ga_pre = low_back(jnp.einsum('thb,hbc->thc', grouped, wdg, precision=HIGH).reshape(mixed.shape))
        decay, drive = lru_coeffs(ga_pre, gx_pre, mixed, param, reset)
        prods, state = lax.associative_scan(affine, (decay, drive), axis=0)
        merged = low(state * branch)
        x_one = x + low_back(jnp.dot(merged, wo, precision=HIGH))
        h_two = low(normed(x_one, gain_two))
        gate_pre = low_back(jnp.dot(h_two, wg, precision=HIGH))
        up_val = low_back(jnp.dot(h_two, wu, precision=HIGH))
        act = low(gelu_tanh(gate_pre) * up_val)
        return x_one + low_back(jnp.dot(act, wd, precision=HIGH))
    floats = [a.astype(jnp.float32) for a in (block_input, gain_mixer, w_branch, w_signal, w_input_gate, w_decay_gate, conv_taps, decay_param, w_mixout, gain_dense, w_gate, w_up, w_down)]
    result, pullback = jax.vjp(forward, *floats)
    g_x, g_g1, g_wb, g_ws, g_wig, g_wdg, g_taps, g_param, g_wo, g_g2, g_wg, g_wu, g_wd = pullback(cotangent.astype(jnp.float32))
    return (result.astype(jnp.bfloat16), g_x, g_g1, g_wb, g_ws, g_wig, g_wdg, g_taps, g_param, g_wo, g_g2, g_wg, g_wu, g_wd)
```

```python
import functools

import jax
import jax.numpy as jnp
from jax import lax
from jax.experimental import pallas as pl
from jax.experimental.pallas import tpu as pltpu
from jax.sharding import PartitionSpec as P

BLOCK = 256
CONV = 4
MAXLEN = 1024
EPS = 1e-06
BF16 = jnp.bfloat16
F32 = jnp.float32


def ring_order(chips):
    return list(range(0, chips, 2)) + list(range(chips - 1, 0, -2))


class Ring:
    def __init__(self):
        count = lax.axis_size("dp")
        self.chips = count // 2
        self.reach = self.chips // 2
        order = ring_order(self.chips)
        self.up_route = [
            (order[p] * 2 + c, order[(p + 1) % self.chips] * 2 + c)
            for p in range(self.chips)
            for c in range(2)
        ]
        self.down_route = [(b, a) for a, b in self.up_route]
        place = [0] * self.chips
        for p, chip in enumerate(order):
            place[chip] = p
        me = lax.axis_index("dp")
        self.core = lax.rem(me, 2)
        self.order = jnp.array(order, jnp.int32)
        self.place = jnp.array(place, jnp.int32)[me // 2]

    def chip_at(self, distance):
        return self.order[lax.rem(self.place - distance + self.chips, self.chips)]

    def up(self, value):
        return lax.ppermute(value, "dp", self.up_route)

    def down(self, value):
        return lax.ppermute(value, "dp", self.down_route)

    def gather(self, value):
        half = value.shape[0] // 2
        u = d = value
        pairs = []
        for _ in range(self.reach - 1):
            u, d = self.up(u), self.down(d)
            pairs.append((u, d))
        far = jnp.concatenate([self.up(u[:half]), self.down(d[half:])])
        return pairs, far

    def scatter(self, own, pairs, far):
        half = far.shape[0] // 2
        to_down = self.down(far[:half])
        to_up = self.up(far[half:])
        first = True
        for u, d in reversed(pairs):
            if first:
                u = jnp.concatenate([plus(u[:half], to_down), u[half:].astype(BF16)])
                d = jnp.concatenate([d[:half].astype(BF16), plus(d[half:], to_up)])
                first = False
            else:
                u, d = plus(u, to_down), plus(d, to_up)
            to_down, to_up = self.down(u), self.up(d)
        return own.astype(F32) + to_down.astype(F32) + to_up.astype(F32)


def plus(a, b):
    return (a.astype(F32) + b.astype(F32)).astype(BF16)


def core_swap(value):
    count = lax.axis_size("dp")
    return lax.ppermute(value, "dp", [(i, i ^ 1) for i in range(count)])


def tensor_swap(value):
    return lax.ppermute(value, "tensor", [(0, 1), (1, 0)])


def after(value, other):
    return lax.optimization_barrier((value, other))[0]


def from_behind(block, distance):
    devices = range(lax.axis_size("dp"))
    route = [(i - distance, i) for i in devices if i - distance in devices]
    return lax.ppermute(block, "dp", route)


def entering(prods, state, hops, reverse):
    part = jnp.stack([prods, state])
    total = jnp.zeros_like(state)
    sign = -1 if reverse else 1
    got = [from_behind(part, sign * hop) for hop in range(1, hops + 1)]
    for value in reversed(got):
        total = value[0] * total + value[1]
    return total


def normed(value, gain):
    return value * lax.rsqrt(jnp.mean(value * value, axis=-1, keepdims=True) + EPS) * gain


def gelu_tanh(value):
    return jax.nn.gelu(value, approximate=True)


def lru_coeffs(ga_pre, gx_pre, conv_out, param, reset):
    gate_a = jax.nn.sigmoid(ga_pre)
    gate_x = jax.nn.sigmoid(gx_pre)
    log_a = -8.0 * gate_a * jax.nn.softplus(param)
    keep = 1.0 - reset
    decay = jnp.exp(log_a) * keep
    multiplier = jnp.sqrt(-jnp.expm1(2.0 * log_a)) * keep + reset
    return (decay, gate_x * conv_out * multiplier)


def conv_mix(padded, taps, masks):
    lag = CONV - 1
    count = masks.shape[0]
    total = taps[:, 0] * padded[lag : lag + count] * masks[:, 0:1]
    for shift_k in range(1, CONV):
        total = (
            total
            + taps[:, shift_k]
            * padded[lag - shift_k : lag - shift_k + count]
            * masks[:, shift_k : shift_k + 1]
        )
    return total


def rows_inner(left, right):
    return lax.dot_general(
        left, right, (((0,), (0,)), ((), ())), preferred_element_type=F32
    )


def cols_inner(left, right):
    return lax.dot_general(
        left, right, (((1,), (1,)), ((), ())), preferred_element_type=F32
    )


def scan_body(reverse, a_ref, b_ref, p_ref, s_ref):
    rows, width = a_ref.shape
    blocks = rows // 8
    row = lax.broadcasted_iota(jnp.int32, (8, width), 0)

    def step(i, carry):
        p_in, s_in = carry
        at = (blocks - 1 - i) if reverse else i
        here = pl.ds(pl.multiple_of(at * 8, 8), 8)
        a = a_ref[here, :]
        b = b_ref[here, :]
        for shift in (1, 2, 4):
            turn = 8 - shift if reverse else shift
            inside = (row < 8 - shift) if reverse else (row >= shift)
            a_prev = jnp.where(inside, pltpu.roll(a, turn, 0), 1.0)
            b_prev = jnp.where(inside, pltpu.roll(b, turn, 0), 0.0)
            b = a * b_prev + b
            a = a * a_prev
        b = b + a * s_in
        a = a * p_in
        p_ref[here, :] = a
        s_ref[here, :] = b
        last = 0 if reverse else 7
        return (a[last : last + 1], b[last : last + 1])

    lax.fori_loop(
        0, blocks, step, (jnp.ones((1, width), F32), jnp.zeros((1, width), F32))
    )


def local_scan(coeff, value, reverse):
    shape = jax.ShapeDtypeStruct(value.shape, F32)
    return pl.pallas_call(
        functools.partial(scan_body, reverse),
        out_shape=(shape, shape),
        in_specs=[pl.BlockSpec(memory_space=pltpu.VMEM)] * 2,
        out_specs=(pl.BlockSpec(memory_space=pltpu.VMEM),) * 2,
        cost_estimate=pl.CostEstimate(
            flops=20 * value.size, bytes_accessed=16 * value.size, transcendentals=0
        ),
        compiler_params=pltpu.CompilerParams(vmem_limit_bytes=32 << 20),
    )(coeff, value)


def gather_absolute(ring, shard, sizes, wait=None):
    count = 2 * ring.chips
    width = shard.shape[1]
    if wait is not None:
        shard = after(shard, wait)
    pairs, far = ring.gather(shard)
    chunks = [(0, shard)]
    for k, (u, d) in enumerate(pairs, 1):
        chunks += [(k, u), (-k, d)]
    chunks.append((ring.reach, far))
    outs = [jnp.zeros((count, size, width), shard.dtype) for size in sizes]
    for distance, chunk in chunks:
        other = core_swap(chunk)
        first = jnp.where(ring.core == 0, chunk, other)
        second = jnp.where(ring.core == 0, other, chunk)
        both = jnp.stack([first, second])
        at = ring.chip_at(distance) * 2
        start = 0
        for i, size in enumerate(sizes):
            outs[i] = lax.dynamic_update_slice(
                outs[i], both[:, start : start + size], (at, 0, 0)
            )
            start += size
    return outs, pairs[-1]


def scatter_absolute(ring, parts):
    count = 2 * ring.chips
    split = [p.astype(BF16).reshape(ring.chips, 2, p.shape[1], p.shape[2]) for p in parts]
    split = jnp.concatenate(split, axis=2)
    theirs = core_swap(lax.dynamic_index_in_dim(split, 1 - ring.core, 1, False))
    mine = plus(lax.dynamic_index_in_dim(split, ring.core, 1, False), theirs)

    def part(distance):
        return lax.dynamic_index_in_dim(mine, ring.chip_at(distance), 0, False)

    pairs = [(part(k), part(-k)) for k in range(1, ring.reach)]
    return ring.scatter(part(0), pairs, part(ring.reach))


def fetch_hidden(shard):
    mine = jnp.concatenate([shard, tensor_swap(shard)])
    return jnp.concatenate([mine, core_swap(mine)])


def reduce_hidden(grad):
    size = grad.shape[0] // 4
    mine = grad[: 2 * size] + core_swap(grad[2 * size :].astype(BF16)).astype(F32)
    return mine[:size] + tensor_swap(mine[size:].astype(BF16)).astype(F32)


def ordered(ring_tensor, own, other):
    first = jnp.where(ring_tensor == 0, own, other)
    second = jnp.where(ring_tensor == 0, other, own)
    return jnp.concatenate([first, second])


def per_device(
    block_input,
    starts,
    cotangent,
    gain_mixer,
    w_branch,
    w_signal,
    w_input_gate,
    w_decay_gate,
    conv_taps,
    decay_param,
    w_mixout,
    gain_dense,
    w_gate,
    w_up,
    w_down,
):
    ring = Ring()
    side = lax.axis_index("tensor")
    count = lax.axis_size("dp")
    group = starts.shape[0]
    rows, width = block_input.shape
    shard = w_branch.shape[1]
    channels = shard * count
    lag = CONV - 1
    hops = -(-MAXLEN // group)
    heads_here = w_input_gate.shape[0]

    small = jnp.concatenate(
        [gain_mixer, gain_dense, conv_taps.reshape(-1), decay_param]
    )
    n_small = small.shape[0]
    small = jnp.pad(small, (0, width - n_small)).reshape(1, width)
    gates = jnp.concatenate(
        [w_input_gate.reshape(-1, width), w_decay_gate.reshape(-1, width)]
    )
    n_gate = gates.shape[0]
    pack = jnp.concatenate([w_signal.T, gates, small])
    pad = -pack.shape[0] % 16
    pack = jnp.pad(pack, ((0, pad), (0, 0)))
    (wide_s, wide_gates, wide_small), done = gather_absolute(
        ring, pack, (shard, n_gate, 1)
    )
    (wide_b,), done = gather_absolute(ring, w_branch.T, (shard,), done)
    (wide_o,), done = gather_absolute(ring, w_mixout, (shard,), done)
    wide_s = wide_s.reshape(channels, width)
    wide_b = wide_b.reshape(channels, width)
    wide_o = wide_o.reshape(channels, width)
    wide_gates = wide_gates.reshape(count, 2, heads_here, BLOCK // count, BLOCK)
    wide_ig = jnp.swapaxes(wide_gates[:, 0], 0, 1).reshape(heads_here, BLOCK, BLOCK)
    wide_dg = jnp.swapaxes(wide_gates[:, 1], 0, 1).reshape(heads_here, BLOCK, BLOCK)
    wide_small = wide_small[:, 0]
    n_gain = gain_mixer.shape[0]
    gain_one = wide_small[:, :n_gain].reshape(width).astype(F32)
    gain_two = wide_small[:, n_gain : 2 * n_gain].reshape(width).astype(F32)
    taps = wide_small[:, 2 * n_gain : 2 * n_gain + shard * CONV]
    taps = taps.reshape(channels, CONV).astype(F32)
    param = wide_small[:, 2 * n_gain + shard * CONV : n_small].reshape(channels).astype(F32)

    x_other = tensor_swap(block_input)
    dy_pairs, dy_far = ring.gather(after(cotangent, done))
    hid_g = fetch_hidden(after(w_gate.T, x_other))
    hid_u = fetch_hidden(after(w_up.T, hid_g))
    hid_d = fetch_hidden(after(w_down, hid_u))

    x_val = block_input.astype(F32)
    x_both = ordered(side, block_input, x_other).astype(F32)
    h_one = normed(x_both, gain_one).astype(BF16)
    signal = cols_inner(h_one, wide_s).astype(BF16)
    branch_pre = cols_inner(h_one, wide_b)
    branch, branch_back = jax.vjp(gelu_tanh, branch_pre)
    reset = starts.astype(F32)[:, None]
    cumulative = jnp.cumsum(starts)
    padded_cum = jnp.concatenate([jnp.zeros((lag,), jnp.int32), cumulative])
    masks = jnp.stack(
        [
            (cumulative - padded_cum[lag - k : lag - k + group] == 0).astype(F32)
            for k in range(CONV)
        ],
        axis=1,
    )
    tail_keep = (cumulative[group - 1] - cumulative[group - lag :] == 0)[:, None]
    rim = from_behind(signal[group - lag :] * tail_keep.astype(BF16), 1)
    padded = jnp.concatenate([rim, signal]).astype(F32)

    def conv_local(padded_in, taps_in):
        return conv_mix(padded_in, taps_in, masks)

    mixed_full, conv_back = jax.vjp(conv_local, padded, taps)
    mixed = mixed_full.astype(BF16)
    grouped = mixed.reshape(group, heads_here, BLOCK)
    gx_pre = jnp.einsum(
        "ghb,hbc->ghc", grouped, wide_ig, preferred_element_type=F32
    ).reshape(group, channels)
    ga_pre = jnp.einsum(
        "ghb,hbc->ghc", grouped, wide_dg, preferred_element_type=F32
    ).reshape(group, channels)

    def coeff_local(ga_in, gx_in, conv_in, param_in):
        return lru_coeffs(ga_in, gx_in, conv_in, param_in, reset)

    (decay, drive), coeff_back = jax.vjp(
        coeff_local, ga_pre, gx_pre, mixed.astype(F32), param
    )
    prods, local_state = local_scan(decay, drive, False)
    incoming = entering(prods[group - 1], local_state[group - 1], hops, False)
    state = local_state + prods * incoming[None, :]
    merged = (state * branch).astype(BF16)
    mine_at, theirs_at = side * rows, (1 - side) * rows
    mix_theirs = jnp.dot(
        lax.dynamic_slice_in_dim(merged, theirs_at, rows, 0),
        wide_o,
        preferred_element_type=F32,
    )
    mix_got = tensor_swap(mix_theirs.astype(BF16))
    mix_mine = jnp.dot(
        lax.dynamic_slice_in_dim(merged, mine_at, rows, 0),
        wide_o,
        preferred_element_type=F32,
    )
    x_one = x_val + mix_mine + mix_got.astype(F32)
    n_two, norm_two_back = jax.vjp(normed, x_one, gain_two)

    h_own = n_two.astype(BF16)
    h_pairs, h_far = ring.gather(h_own)

    def pieces(own, pairs, far):
        return [
            jnp.concatenate([own, *pairs[0]]),
            *(jnp.concatenate(pair) for pair in pairs[1:]),
            far,
        ]

    h_list = pieces(h_own, h_pairs, h_far)
    dy_list = pieces(cotangent, dy_pairs, dy_far)
    acts, d_gates, d_ups, d_hs, downs = [], [], [], [], []
    for h_piece, dy_piece in zip(h_list, dy_list):
        gate_pre = cols_inner(h_piece, hid_g)
        up_val = cols_inner(h_piece, hid_u)
        gate_act, gate_back = jax.vjp(gelu_tanh, gate_pre)
        acts.append((gate_act * up_val).astype(BF16))
        d_act = cols_inner(dy_piece, hid_d)
        d_gate = gate_back(d_act * up_val)[0].astype(BF16)
        d_up = (d_act * gate_act).astype(BF16)
        d_gates.append(d_gate)
        d_ups.append(d_up)
        d_hs.append(
            (
                jnp.dot(d_gate, hid_g, preferred_element_type=F32)
                + jnp.dot(d_up, hid_u, preferred_element_type=F32)
            ).astype(BF16)
        )
        downs.append(jnp.dot(acts[-1], hid_d, preferred_element_type=F32).astype(BF16))

    def chunks(parts):
        own = parts[0][:rows]
        pairs = [(parts[0][rows : 2 * rows], parts[0][2 * rows :])]
        pairs += [(p[:rows], p[rows:]) for p in parts[1:-1]]
        return own, pairs, parts[-1]

    d_h_two = ring.scatter(*chunks(d_hs))
    downs = after(downs, d_h_two)
    block_output = (x_one + ring.scatter(*chunks(downs))).astype(BF16)
    h_all = jnp.concatenate(h_list)
    dy_all = jnp.concatenate(dy_list)
    s_gate = reduce_hidden(rows_inner(jnp.concatenate(d_gates), h_all)).T
    s_up = reduce_hidden(rows_inner(jnp.concatenate(d_ups), h_all)).T
    s_down = reduce_hidden(rows_inner(jnp.concatenate(acts), dy_all))

    d_x_norm_two, g_gain_two = norm_two_back(d_h_two)
    d_x_one = cotangent.astype(F32) + d_x_norm_two
    dz_own = d_x_one.astype(BF16)
    d_mix = ordered(side, dz_own, tensor_swap(dz_own))
    g_mixout = rows_inner(merged, d_mix)
    s_mixout = scatter_absolute(ring, [g_mixout.reshape(count, shard, width)])
    d_merged = cols_inner(d_mix, wide_o)
    d_state = d_merged * branch
    d_branch = branch_back(d_merged * state)[0].astype(BF16)
    g_branch_rows = rows_inner(d_branch, h_one)
    s_branch = scatter_absolute(ring, [g_branch_rows.reshape(count, shard, width)]).T
    shifted = jnp.concatenate([decay[1:], jnp.ones((1, channels), F32)])
    rev_prods, rev_state = local_scan(shifted, d_state, True)
    later = entering(decay[0] * rev_prods[0], decay[0] * rev_state[0], hops, True)
    d_total = rev_state + rev_prods * later[None, :]
    previous = jnp.concatenate([incoming[None, :], state[:-1]])
    d_ga, d_gx, d_mixed_direct, g_param = coeff_back((d_total * previous, d_total))
    d_ga_low = d_ga.astype(BF16).reshape(group, heads_here, BLOCK)
    d_gx_low = d_gx.astype(BF16).reshape(group, heads_here, BLOCK)
    g_input_rows = jnp.einsum("ghb,ghc->bhc", grouped, d_gx_low, preferred_element_type=F32)
    g_decay_rows = jnp.einsum("ghb,ghc->bhc", grouped, d_ga_low, preferred_element_type=F32)
    d_back_gates = jnp.einsum(
        "ghc,hbc->ghb", d_gx_low, wide_ig, preferred_element_type=F32
    ) + jnp.einsum("ghc,hbc->ghb", d_ga_low, wide_dg, preferred_element_type=F32)
    d_mixed = d_mixed_direct + d_back_gates.reshape(group, channels)
    d_padded, g_taps = conv_back(d_mixed)
    back_rim = from_behind(d_padded[:lag], -1)
    d_sig_full = d_padded[lag:]
    d_sig_full = jnp.concatenate(
        [
            d_sig_full[: group - lag],
            d_sig_full[group - lag :] + back_rim * tail_keep.astype(F32),
        ]
    )
    d_signal = d_sig_full.astype(BF16)

    def d_h_rows(at):
        return jnp.dot(
            lax.dynamic_slice_in_dim(d_branch, at, rows, 0), wide_b, preferred_element_type=F32
        ) + jnp.dot(
            lax.dynamic_slice_in_dim(d_signal, at, rows, 0), wide_s, preferred_element_type=F32
        )

    d_h_got = tensor_swap(d_h_rows(theirs_at).astype(BF16))
    d_h_one = d_h_rows(mine_at) + d_h_got.astype(F32)
    _, norm_one_back = jax.vjp(normed, x_val, gain_one)
    d_x_norm_one, g_gain_one = norm_one_back(d_h_one)
    grad_input = d_x_one + d_x_norm_one

    g_signal_rows = rows_inner(d_signal, h_one).reshape(count, shard, width)
    gate_rows = jnp.concatenate(
        [
            g_input_rows.reshape(count, BLOCK // count, heads_here, BLOCK)
            .swapaxes(1, 2)
            .reshape(count, n_gate // 2, width),
            g_decay_rows.reshape(count, BLOCK // count, heads_here, BLOCK)
            .swapaxes(1, 2)
            .reshape(count, n_gate // 2, width),
        ],
        axis=1,
    )
    small_rows = jnp.concatenate(
        [g_taps.reshape(count, shard * CONV), g_param.reshape(count, shard)], axis=1
    )
    n_rows = small_rows.shape[1]
    small_rows = jnp.pad(small_rows, ((0, 0), (0, width - n_rows)))[:, None]
    last = scatter_absolute(ring, [g_signal_rows, gate_rows, small_rows])
    s_signal = last[:shard].T
    s_gates = last[shard : shard + n_gate].reshape(2, *w_input_gate.shape)
    s_taps = last[shard + n_gate, : shard * CONV].reshape(shard, CONV)
    s_param = last[shard + n_gate, shard * CONV : n_rows]
    gains = jnp.stack([g_gain_one, g_gain_two])
    gains = gains + tensor_swap(gains)
    gains = lax.psum_scatter(gains, "dp", scatter_dimension=1, tiled=True)
    return (
        block_output,
        grad_input,
        gains[0],
        s_branch,
        s_signal,
        s_gates[0],
        s_gates[1],
        s_taps,
        s_param,
        s_mixout,
        gains[1],
        s_gate,
        s_up,
        s_down,
    )


def solution(mesh):
    placed = (
        P(("dp", "tensor"), None),
        P("dp"),
        P(("dp", "tensor"), None),
        P("dp"),
        P(None, ("tensor", "dp")),
        P(None, ("tensor", "dp")),
        P("tensor", "dp", None),
        P("tensor", "dp", None),
        P(("tensor", "dp"), None),
        P(("tensor", "dp")),
        P(("tensor", "dp"), None),
        P("dp"),
        P(None, ("tensor", "dp")),
        P(None, ("tensor", "dp")),
        P(("tensor", "dp"), None),
    )
    return jax.shard_map(
        per_device,
        mesh=mesh,
        in_specs=placed,
        out_specs=(
            P(("dp", "tensor"), None),
            P(("dp", "tensor"), None),
            P("dp"),
            P(None, ("tensor", "dp")),
            P(None, ("tensor", "dp")),
            P("tensor", "dp", None),
            P("tensor", "dp", None),
            P(("tensor", "dp"), None),
            P(("tensor", "dp")),
            P(("tensor", "dp"), None),
            P("dp"),
            P(None, ("tensor", "dp")),
            P(None, ("tensor", "dp")),
            P(("tensor", "dp"), None),
        ),
        check_vma=False,
    )
```

```python
import functools

import jax
import jax.numpy as jnp
from jax import lax
from jax.experimental import pallas as pl
from jax.experimental.pallas import tpu as pltpu
from jax.sharding import PartitionSpec as P

BLOCK = 256
CONV = 4
MAXLEN = 1024
EPS = 1e-06
HALO = 16
BF16 = jnp.bfloat16
F32 = jnp.float32


def ring_order(chips):
    return list(range(0, chips, 2)) + list(range(chips - 1, 0, -2))


class Ring:
    def __init__(self):
        count = lax.axis_size("dp")
        self.chips = count // 2
        self.reach = self.chips // 2
        order = ring_order(self.chips)
        self.up_route = [
            (order[p] * 2 + c, order[(p + 1) % self.chips] * 2 + c)
            for p in range(self.chips)
            for c in range(2)
        ]
        self.down_route = [(b, a) for a, b in self.up_route]
        me = lax.axis_index("dp")
        chip = me // 2
        self.core = lax.rem(me, 2)
        self.place = jnp.where(
            lax.rem(chip, 2) == 0, chip // 2, self.chips - 1 - chip // 2
        )

    def chip_at(self, distance):
        p = lax.rem(self.place - distance + self.chips, self.chips)
        return jnp.where(p < self.reach, 2 * p, 2 * (self.chips - 1 - p) + 1)

    def up(self, value):
        return lax.ppermute(value, "dp", self.up_route)

    def down(self, value):
        return lax.ppermute(value, "dp", self.down_route)


class Order:
    def __init__(self):
        self.token = None

    def tie(self, *values):
        if self.token is not None:
            values = lax.optimization_barrier((values, self.token))[0]
        return values if len(values) > 1 else values[0]

    def arrive(self, *values):
        values = lax.optimization_barrier((values, self.token))[0]
        self.token = values[-1]
        return values if len(values) > 1 else values[0]

    def run(self, function, *values):
        values = self.tie(*values)
        out = function(*values) if isinstance(values, tuple) else function(values)
        self.token = jax.tree.leaves(out)[-1]
        return out


SHOWN = 4


class Gather:
    def __init__(self, ring, order, value, both_cores=False):
        self.ring, self.order = ring, order
        self.own = value
        self.half = value.shape[0] // 32 * 16 or value.shape[0] // 2
        self.flight = (value, value)
        self.pairs, self.far = [], None
        self.theirs = [] if both_cores else None
        self.steps = 0

    def start(self):
        if self.theirs is not None:
            self.theirs.append((core_swap(self.own),))
        self.send()
        for _ in range(self.ring.reach - SHOWN):
            self.next()

    def send(self):
        self.steps += 1
        u, d = self.order.tie(*self.flight)
        if self.steps == self.ring.reach:
            u, d = u[: self.half], d[self.half :]
        self.flight = (self.ring.up(u), self.ring.down(d))

    def land(self):
        self.flight = self.order.arrive(*self.flight)
        if self.theirs is not None:
            self.theirs.append(tuple(core_swap(v) for v in self.flight))

    def next(self):
        self.land()
        self.pairs.append(self.flight)
        self.send()

    def finish(self):
        self.land()
        self.far = self.flight


class Scatter:
    def __init__(self, ring, order, parts, half):
        self.ring, self.order = ring, order
        self.parts, self.half = list(parts), half
        self.steps = 0

    def start(self):
        far = self.parts.pop()
        self.flight = self.order.run(
            lambda *v: (far(v, 0, self.half), far(v, self.half, None)), *far.values
        )
        self.send()
        for _ in range(self.ring.reach - SHOWN):
            self.next()

    def send(self):
        self.steps += 1
        u, d = self.order.tie(*self.flight)
        self.flight = (self.ring.down(u), self.ring.up(d))

    def next(self):
        ahead, behind = self.parts.pop(), self.parts.pop()
        half, first = self.half, self.steps == 1

        def add(to_down, to_up, *values):
            u_values, d_values = values[: len(behind.values)], values[len(behind.values) :]
            if first:
                return (
                    jnp.concatenate(
                        [behind(u_values, 0, half, to_down), behind(u_values, half, None)]
                    ),
                    jnp.concatenate(
                        [ahead(d_values, 0, half), ahead(d_values, half, None, to_up)]
                    ),
                )
            return behind(u_values, 0, None, to_down), ahead(d_values, 0, None, to_up)

        self.flight = self.order.run(add, *self.flight, *behind.values, *ahead.values)
        self.send()

    def finish(self, function=None, *more):
        own = self.parts.pop()

        def total(to_down, to_up, *values):
            count = len(own.values)
            out = own(values[:count], 0, None, to_down, to_up, F32)
            return function(out, *values[count:]) if function else out

        return self.order.run(total, *self.flight, *own.values, *more)


class Part:
    def __init__(self, cut, *values):
        self.cut, self.values = cut, values

    def __call__(self, values, first, last, *others):
        dtype = BF16
        if others and others[-1] is F32:
            others, dtype = others[:-1], F32
        total = self.cut(*values)[first:last]
        for other in others:
            total = total + other.astype(F32)
        return total.astype(dtype)


def plain_parts(values):
    return [Part(lambda v: v.astype(F32), value) for value in values]


def plus(a, b):
    return (a.astype(F32) + b.astype(F32)).astype(BF16)


def core_swap(value):
    count = lax.axis_size("dp")
    return lax.ppermute(value, "dp", [(i, i ^ 1) for i in range(count)])


def tensor_swap(value):
    return lax.ppermute(value, "tensor", [(0, 1), (1, 0)])


def from_behind(block, distance):
    devices = range(lax.axis_size("dp"))
    route = [(i - distance, i) for i in devices if i - distance in devices]
    return lax.ppermute(block, "dp", route)


class Entering:
    def __init__(self, order, window, hops, reverse):
        self.order, self.sign = order, (-1 if reverse else 1)
        size = 1
        while 4 * size < hops:
            window = follow(from_behind(window, self.sign * size), window)
            size *= 2
        self.size, self.hops, self.window = size, hops, window
        if size < hops:
            self.behind = from_behind(window, self.sign * size)

    def next(self):
        if 2 * self.size < self.hops:
            self.window = self.order.run(follow, self.behind, self.window)
            self.size *= 2
        self.near = from_behind(self.window, self.sign)
        if self.size < self.hops:
            self.rest = from_behind(self.window, self.sign * (1 + self.size))

    def finish(self):
        if self.size >= self.hops:
            return self.order.arrive(self.near)[1:]
        return self.order.run(lambda n, r: n[:1] * r[1:] + n[1:], self.near, self.rest)


def follow(first, second):
    return jnp.stack([first[0] * second[0], second[0] * first[1] + second[1]])


def normed(value, gain):
    return value * lax.rsqrt(jnp.mean(value * value, axis=-1, keepdims=True) + EPS) * gain


def gelu_tanh(value):
    return jax.nn.gelu(value, approximate=True)


GELU_IN = 0.7978845608028654
GELU_CUBE = 0.044715


def gelu_and_slope(value):
    square = value * value
    t = jnp.tanh(GELU_IN * (value + GELU_CUBE * (square * value)))
    half = 0.5 * (1.0 + t)
    slope = half + 0.5 * value * (1.0 - t * t) * (GELU_IN * (1.0 + 3.0 * GELU_CUBE * square))
    return value * half, slope


def rows_inner(left, right):
    return lax.dot_general(
        left, right, (((0,), (0,)), ((), ())), preferred_element_type=F32
    )


def cols_inner(left, right):
    return lax.dot_general(
        left, right, (((1,), (1,)), ((), ())), preferred_element_type=F32
    )


def scan_rows(reverse, a_ref, b_ref, p_ref, s_ref):
    rows, width = a_ref.shape
    blocks = rows // 8
    row = lax.broadcasted_iota(jnp.int32, (8, width), 0)

    def step(i, carry):
        p_in, s_in = carry
        at = (blocks - 1 - i) if reverse else i
        here = pl.ds(pl.multiple_of(at * 8, 8), 8)
        a = a_ref[here, :]
        b = b_ref[here, :]
        for shift in (1, 2, 4):
            turn = 8 - shift if reverse else shift
            inside = (row < 8 - shift) if reverse else (row >= shift)
            a_prev = jnp.where(inside, pltpu.roll(a, turn, 0), 1.0)
            b_prev = jnp.where(inside, pltpu.roll(b, turn, 0), 0.0)
            b = a * b_prev + b
            a = a * a_prev
        b = b + a * s_in
        a = a * p_in
        p_ref[here, :] = a
        s_ref[here, :] = b
        last = 0 if reverse else 7
        return (a[last : last + 1], b[last : last + 1])

    return lax.fori_loop(
        0, blocks, step, (jnp.ones((1, width), F32), jnp.zeros((1, width), F32))
    )


def lru_gates(mixed, w_ig, w_dg, param):
    gx_pre = jnp.dot(mixed, w_ig, preferred_element_type=F32)
    ga_pre = jnp.dot(mixed, w_dg, preferred_element_type=F32)
    return jax.nn.sigmoid(gx_pre), jax.nn.sigmoid(ga_pre), jax.nn.softplus(param)


def one_minus_square(log_a, e):
    x = 2.0 * log_a
    series = -x * (
        1.0 + x * (1 / 2 + x * (1 / 6 + x * (1 / 24 + x * (1 / 120 + x * (1 / 720)))))
    )
    return jnp.where(x > -0.3, series, 1.0 - e * e)


def mix_body(pad_ref, marks_ref, params_ref, ig_ref, dg_ref, *refs):
    mixed_ref, decay_ref, prods_ref, state_ref, ends_ref, a_scr, b_scr = refs
    block = pl.program_id(0)
    rows = mixed_ref.shape[0]
    pad = pad_ref[...].astype(F32)
    total = params_ref[0:1, :] * pad[HALO:] * marks_ref[:, 0:1]
    for k in range(1, CONV):
        behind = pltpu.roll(pad, k, 0)[HALO:]
        total = total + params_ref[k : k + 1, :] * behind * marks_ref[:, k : k + 1]
    mixed = total.astype(BF16)
    mixed_ref[...] = mixed
    gate_x, gate_a, soft = lru_gates(mixed, ig_ref[...], dg_ref[...], params_ref[CONV : CONV + 1, :])
    reset = marks_ref[:, CONV : CONV + 1]
    keep = 1.0 - reset
    log_a = -8.0 * gate_a * soft
    e = jnp.exp(log_a)
    decay = e * keep
    multiplier = jnp.sqrt(one_minus_square(log_a, e)) * keep + reset
    decay_ref[...] = decay
    here = pl.ds(pl.multiple_of(block * BLOCK, BLOCK), BLOCK)
    a_scr[:, here] = decay
    b_scr[:, here] = gate_x * mixed.astype(F32) * multiplier

    @pl.when(block == pl.num_programs(0) - 1)
    def _():
        p_end, s_end = scan_rows(False, a_scr, b_scr, prods_ref, state_ref)
        ends_ref[0:1, :] = p_end
        ends_ref[1:2, :] = s_end


def back_scan_body(dz_ref, wide_ref, pre_ref, decay_ref, prods_ref, state_ref, in_ref, *refs):
    branch_ref, rev_p_ref, rev_s_ref, ends_ref, a_scr, b_scr, first_scr = refs
    block = pl.program_id(0)
    rows = pre_ref.shape[0]
    d_merged = lax.dot_general(
        dz_ref[...], wide_ref[...], (((1,), (1,)), ((), ())), preferred_element_type=F32
    )
    branch, slope = gelu_and_slope(pre_ref[...])
    state = state_ref[...] + prods_ref[...] * in_ref[...]
    branch_ref[...] = (d_merged * state * slope).astype(BF16)
    decay = decay_ref[...]
    row = lax.broadcasted_iota(jnp.int32, decay.shape, 0)
    ahead = jnp.where(row == rows - 1, 1.0, pltpu.roll(decay, rows - 1, 0))
    here = pl.ds(pl.multiple_of(block * BLOCK, BLOCK), BLOCK)
    a_scr[:, here] = ahead
    b_scr[:, here] = d_merged * branch
    first_scr[:, here] = decay[0:8]

    @pl.when(block == pl.num_programs(0) - 1)
    def _():
        p_end, s_end = scan_rows(True, a_scr, b_scr, rev_p_ref, rev_s_ref)
        first = first_scr[0:1, :]
        ends_ref[0:1, :] = first * p_end
        ends_ref[1:2, :] = first * s_end


def back_mix_body(*refs):
    (rev_p_ref, rev_s_ref, later_ref, prods_ref, state_ref, in_ref) = refs[:6]
    (mixed_ref, pad_ref, marks_ref, params_ref, ig_ref, dg_ref) = refs[6:12]
    sig_ref, tail_ref, rim_ref, sums_ref, gates_ref = refs[12:]
    rows = mixed_ref.shape[0]
    g = rev_s_ref[...] + rev_p_ref[...] * later_ref[...]
    entering_row = in_ref[...]
    state = state_ref[...] + prods_ref[...] * entering_row
    row = lax.broadcasted_iota(jnp.int32, state.shape, 0)
    previous = jnp.where(row == 0, entering_row, pltpu.roll(state, 1, 0))
    mixed = mixed_ref[...]
    mixed_f = mixed.astype(F32)
    param = params_ref[CONV : CONV + 1, :]
    gate_x, gate_a, soft = lru_gates(mixed, ig_ref[...], dg_ref[...], param)
    reset = marks_ref[:, CONV : CONV + 1]
    keep = 1.0 - reset
    log_a = -8.0 * gate_a * soft
    e = jnp.exp(log_a)
    root = jnp.sqrt(one_minus_square(log_a, e))
    multiplier = root * keep + reset
    d_multiplier = g * gate_x * mixed_f
    d_log_a = keep * (g * previous * e - d_multiplier * (e * e) / root)
    d_gate_a = d_log_a * (-8.0 * soft)
    d_param = jnp.sum(d_log_a * (-8.0 * gate_a), axis=0, keepdims=True) * jax.nn.sigmoid(param)
    d_ga = (d_gate_a * gate_a * (1.0 - gate_a)).astype(BF16)
    d_gx = (g * mixed_f * multiplier * gate_x * (1.0 - gate_x)).astype(BF16)
    for half, d_pre in enumerate((d_gx, d_ga)):
        at = (half * pl.num_programs(0) + pl.program_id(0)) * BLOCK
        gates_ref[:, pl.ds(pl.multiple_of(at, BLOCK), BLOCK)] = lax.dot_general(
            mixed, d_pre, (((0,), (0,)), ((), ())), preferred_element_type=F32
        ).astype(BF16)
    d_mixed = (
        g * gate_x * multiplier
        + lax.dot_general(d_gx, ig_ref[...], (((1,), (1,)), ((), ())), preferred_element_type=F32)
        + lax.dot_general(d_ga, dg_ref[...], (((1,), (1,)), ((), ())), preferred_element_type=F32)
    )
    pad = pad_ref[...].astype(F32)
    front = jnp.zeros((HALO, BLOCK), F32)
    d_pad = None
    for k in range(CONV):
        masked = d_mixed * marks_ref[:, k : k + 1]
        behind = pad if k == 0 else pltpu.roll(pad, k, 0)
        sums_ref[k : k + 1, :] = jnp.sum(masked * behind[HALO:], axis=0, keepdims=True)
        term = jnp.concatenate([front, masked * params_ref[k : k + 1, :]])
        if k:
            term = pltpu.roll(term, rows + HALO - k, 0)
        d_pad = term if d_pad is None else d_pad + term
    sums_ref[CONV : CONV + 1, :] = d_param
    sums_ref[CONV + 1 : 8, :] = jnp.zeros((8 - CONV - 1, BLOCK), F32)
    rim_ref[...] = d_pad[HALO - 8 : HALO]
    sig_ref[...] = d_pad[HALO:].astype(BF16)
    tail_ref[...] = d_pad[HALO + rows - 8 :]


def rows_spec(rows):
    return pl.BlockSpec((rows, BLOCK), lambda h: (0, h))


def whole_spec(*shape):
    return pl.BlockSpec(shape, lambda h: (0,) * len(shape))


def gate_specs(heads):
    return [
        pl.BlockSpec((BLOCK, BLOCK), lambda h: (0, h)),
        pl.BlockSpec((BLOCK, BLOCK), lambda h: (0, heads + h)),
    ]


BIG = pltpu.CompilerParams(vmem_limit_bytes=48 << 20)


def shaped(rows, width, dtype=F32):
    return jax.ShapeDtypeStruct((rows, width), dtype)


def mix(padded, marks, params, w_gates):
    rows, width = padded.shape[0] - HALO, padded.shape[1]
    return pl.pallas_call(
        mix_body,
        grid=(width // BLOCK,),
        in_specs=[
            rows_spec(rows + HALO),
            whole_spec(rows, 8),
            rows_spec(8),
            *gate_specs(width // BLOCK),
        ],
        out_specs=[
            rows_spec(rows),
            rows_spec(rows),
            whole_spec(rows, width),
            whole_spec(rows, width),
            whole_spec(2, width),
        ],
        out_shape=[
            shaped(rows, width, BF16),
            shaped(rows, width),
            shaped(rows, width),
            shaped(rows, width),
            shaped(2, width),
        ],
        scratch_shapes=[pltpu.VMEM((rows, width), F32)] * 2,
        cost_estimate=pl.CostEstimate(
            flops=4 * rows * width * BLOCK,
            bytes_accessed=18 * rows * width,
            transcendentals=6 * rows * width,
        ),
        compiler_params=BIG,
    )(padded, marks, params, w_gates, w_gates)


def back_scan(dz, wide, pre, decay, prods, state, incoming):
    rows, width = pre.shape
    depth = dz.shape[1]
    return pl.pallas_call(
        back_scan_body,
        grid=(width // BLOCK,),
        in_specs=[
            whole_spec(rows, depth),
            pl.BlockSpec((BLOCK, depth), lambda h: (h, 0)),
            rows_spec(rows),
            rows_spec(rows),
            rows_spec(rows),
            rows_spec(rows),
            rows_spec(1),
        ],
        out_specs=[
            rows_spec(rows),
            whole_spec(rows, width),
            whole_spec(rows, width),
            whole_spec(2, width),
        ],
        out_shape=[
            shaped(rows, width, BF16),
            shaped(rows, width),
            shaped(rows, width),
            shaped(2, width),
        ],
        scratch_shapes=[
            pltpu.VMEM((rows, width), F32),
            pltpu.VMEM((rows, width), F32),
            pltpu.VMEM((8, width), F32),
        ],
        cost_estimate=pl.CostEstimate(
            flops=2 * rows * width * depth,
            bytes_accessed=2 * (rows + width) * depth + 26 * rows * width,
            transcendentals=rows * width,
        ),
        compiler_params=BIG,
    )(dz, wide, pre, decay, prods, state, incoming)


def back_mix(rev_p, rev_s, later, prods, state, incoming, mixed, padded, marks, params, w_gates):
    rows, width = mixed.shape
    heads = width // BLOCK
    return pl.pallas_call(
        back_mix_body,
        grid=(heads,),
        in_specs=[
            rows_spec(rows),
            rows_spec(rows),
            rows_spec(1),
            rows_spec(rows),
            rows_spec(rows),
            rows_spec(1),
            rows_spec(rows),
            rows_spec(rows + HALO),
            whole_spec(rows, 8),
            rows_spec(8),
            *gate_specs(heads),
        ],
        out_specs=[
            rows_spec(rows),
            rows_spec(8),
            rows_spec(8),
            rows_spec(8),
            whole_spec(BLOCK, 2 * width),
        ],
        out_shape=[
            shaped(rows, width, BF16),
            shaped(8, width),
            shaped(8, width),
            shaped(8, width),
            shaped(BLOCK, 2 * width, BF16),
        ],
        cost_estimate=pl.CostEstimate(
            flops=12 * rows * width * BLOCK,
            bytes_accessed=24 * rows * width,
            transcendentals=6 * rows * width,
        ),
        compiler_params=BIG,
    )(rev_p, rev_s, later, prods, state, incoming, mixed, padded, marks, params, w_gates, w_gates)


def assemble_body(sizes, runs, places, at_ref, *refs):
    count = len(runs)
    chunks = refs[:count]
    outs = refs[count : count + len(sizes)]
    scratch, in_sems, out_sems = refs[count + len(sizes) :]
    loads = [
        pltpu.make_async_copy(
            chunk, scratch.at[slot, pl.ds(first, rows)], in_sems.at[i]
        )
        for i, (chunk, (slot, first, rows)) in enumerate(zip(chunks, runs))
    ]
    for load in loads:
        load.start()
    stores = []
    for slot in range(places):
        for load, run in zip(loads, runs):
            if run[0] == slot:
                load.wait()
        base = 0
        for out, size in zip(outs, sizes):
            target = pl.ds(pl.multiple_of(at_ref[slot] * size, 16), size)
            stores.append(
                pltpu.make_async_copy(
                    scratch.at[slot, pl.ds(base, size)],
                    out.at[target],
                    out_sems.at[len(stores)],
                )
            )
            stores[-1].start()
            base += size
    for store in stores:
        store.wait()


def assemble(ring, sizes, gathered):
    near = [(0, (gathered.own,))]
    for k, (u, d) in enumerate(gathered.pairs, 1):
        near += [(k, (u,)), (-k, (d,))]
    near.append((ring.reach, gathered.far))
    their = [gathered.theirs[0]]
    for pair in gathered.theirs[1:-1]:
        their += [(v,) for v in pair]
    their.append(gathered.theirs[-1])
    rows, width = gathered.own.shape
    slots = []
    for (distance, mine), theirs in zip(near, their):
        chip = ring.chip_at(distance)
        slots += [(2 * chip + ring.core, mine), (2 * chip + 1 - ring.core, theirs)]
    at = jnp.stack([place for place, _ in slots]).astype(jnp.int32)
    places = len(slots)
    if any(size % 16 for size in sizes):
        every = jnp.stack([jnp.concatenate(v) if len(v) > 1 else v[0] for _, v in slots])
        every = jnp.zeros_like(every).at[at].set(every)
        cuts = [sum(sizes[:i]) for i in range(len(sizes) + 1)]
        return [every[:, a:b].reshape(-1, width) for a, b in zip(cuts, cuts[1:])]
    chunks, runs = [], []
    for slot, (_, values) in enumerate(slots):
        first = 0
        for value in values:
            chunks.append(value)
            runs.append((slot, first, value.shape[0]))
            first += value.shape[0]
    anywhere = pl.BlockSpec(memory_space=pl.ANY)
    return pl.pallas_call(
        functools.partial(assemble_body, sizes, runs, places),
        out_shape=[shaped(places * size, width, BF16) for size in sizes],
        in_specs=[pl.BlockSpec(memory_space=pltpu.SMEM)] + [anywhere] * len(chunks),
        out_specs=[anywhere] * len(sizes),
        scratch_shapes=[
            pltpu.VMEM((places, rows, width), BF16),
            pltpu.SemaphoreType.DMA((len(chunks),)),
            pltpu.SemaphoreType.DMA((places * len(sizes),)),
        ],
        cost_estimate=pl.CostEstimate(
            flops=0, bytes_accessed=4 * places * rows * width, transcendentals=0
        ),
        compiler_params=BIG,
    )(at, *chunks)


def ring_distances(ring):
    out = [0]
    for k in range(1, ring.reach):
        out += [k, -k]
    return out + [ring.reach]


def ring_grads_body(shard, chips, pairs, extra, at_ref, *refs):
    lefts, rights = refs[:pairs], refs[pairs : 2 * pairs]
    rest = refs[2 * pairs :]
    if extra:
        extra_ref, rest = rest[0], rest[1:]
    mine_ref, theirs_ref, turned, full, sems = rest
    core = at_ref[chips]
    width = full.shape[2]
    copies = []

    def send(source, size, base):
        for slot in range(chips):
            for out, c in ((mine_ref, core), (theirs_ref, 1 - core)):
                first = pl.multiple_of((2 * at_ref[slot] + c) * size, 16)
                copies.append(
                    pltpu.make_async_copy(
                        source.at[pl.ds(first, size)],
                        out.at[slot, pl.ds(base, size)],
                        sems.at[len(copies)],
                    )
                )
                copies[-1].start()

    if extra:
        send(extra_ref, extra, pairs * shard)
    for pair in range(pairs):
        turned[...] = lefts[pair][...].astype(F32).T.astype(BF16)

        def column(n, _):
            here = pl.ds(pl.multiple_of(n * BLOCK, BLOCK), BLOCK)
            full[pair, :, here] = jnp.dot(
                turned[...], rights[pair][:, here], preferred_element_type=F32
            ).astype(BF16)
            return 0

        lax.fori_loop(0, width // BLOCK, column, 0)
        send(full.at[pair], shard, pair * shard)
    for copy in copies:
        copy.wait()


def ring_grads(ring, shard, lefts, rights, extra=None):
    pairs, chips = len(lefts), ring.chips
    rows, channels = lefts[0].shape
    width = rights[0].shape[1]
    more = 0 if extra is None else extra.shape[0] // (2 * chips)
    at = [ring.chip_at(distance) for distance in ring_distances(ring)]
    if shard % 16 or more % 16:
        values = [rows_inner(a, b).astype(BF16) for a, b in zip(lefts, rights)]
        values += [] if extra is None else [extra]
        values = jnp.concatenate([v.reshape(chips, 2, -1, width) for v in values], axis=2)
        values = values[jnp.stack(at)]
        return (
            lax.dynamic_index_in_dim(values, ring.core, 1, False),
            lax.dynamic_index_in_dim(values, 1 - ring.core, 1, False),
        )
    in_vmem = pl.BlockSpec(memory_space=pltpu.VMEM)
    anywhere = pl.BlockSpec(memory_space=pl.ANY)
    out = jax.ShapeDtypeStruct((chips, pairs * shard + more, width), BF16)
    return pl.pallas_call(
        functools.partial(ring_grads_body, shard, chips, pairs, more),
        out_shape=[out, out],
        in_specs=[pl.BlockSpec(memory_space=pltpu.SMEM)]
        + [in_vmem] * (2 * pairs + (extra is not None)),
        out_specs=[anywhere, anywhere],
        scratch_shapes=[
            pltpu.VMEM((channels, rows), BF16),
            pltpu.VMEM((pairs, channels, width), BF16),
            pltpu.SemaphoreType.DMA((2 * chips * (pairs + (extra is not None)),)),
        ],
        cost_estimate=pl.CostEstimate(
            flops=2 * pairs * rows * channels * width,
            bytes_accessed=2 * pairs * (channels * width + rows * (channels + width)),
            transcendentals=0,
        ),
        compiler_params=BIG,
    )(
        jnp.stack(at + [ring.core]).astype(jnp.int32),
        *lefts,
        *rights,
        *(() if extra is None else (extra,)),
    )


def ring_parts(mine, theirs):
    def part(k):
        return Part(lambda a, b: a[k].astype(F32) + b[k].astype(F32), mine, theirs)

    return [part(k) for k in range(mine.shape[0])]


def ordered(ring_tensor, own, other):
    first = jnp.where(ring_tensor == 0, own, other)
    second = jnp.where(ring_tensor == 0, other, own)
    return jnp.concatenate([first, second])


def per_device(
    block_input,
    starts,
    cotangent,
    gain_mixer,
    w_branch,
    w_signal,
    w_input_gate,
    w_decay_gate,
    conv_taps,
    decay_param,
    w_mixout,
    gain_dense,
    w_gate,
    w_up,
    w_down,
):
    ring = Ring()
    side = lax.axis_index("tensor")
    count = lax.axis_size("dp")
    group = starts.shape[0]
    rows, width = block_input.shape
    shard = w_branch.shape[1]
    channels = shard * count
    lag = CONV - 1
    hops = -(-MAXLEN // group)
    heads_here = w_input_gate.shape[0]

    order = Order()
    mine_at, theirs_at = side * rows, (1 - side) * rows

    small = jnp.concatenate(
        [gain_mixer, gain_dense, conv_taps.reshape(-1), decay_param]
    )
    n_small = small.shape[0]
    small = jnp.pad(small, (0, 16 * width - n_small)).reshape(16, width)
    n_gate = w_input_gate.shape[1]
    gates = jnp.concatenate(
        [jnp.swapaxes(w, 0, 1).reshape(n_gate, channels) for w in (w_input_gate, w_decay_gate)],
        axis=1,
    )
    x_other = tensor_swap(block_input)
    one = Gather(ring, order, jnp.concatenate([w_signal.T, gates, small]), True)
    order.token = one.own
    one.start()
    hid_own = order.run(lambda *w: jnp.stack(w), w_gate.T, w_up.T, w_down)
    pack_two = order.run(lambda *w: jnp.concatenate(w), w_branch.T, w_mixout)
    cumulative = jnp.cumsum(starts)
    padded_cum = jnp.concatenate([jnp.zeros((lag,), jnp.int32), cumulative])
    masks = [
        (cumulative - padded_cum[lag - k : lag - k + group] == 0).astype(F32)
        for k in range(CONV)
    ]
    marks = jnp.stack(masks + [starts.astype(F32)] * (8 - CONV), axis=1)
    tail_keep = (cumulative[group - 1] - cumulative[group - HALO :] == 0)[:, None]
    x_low = order.run(functools.partial(ordered, side), block_input, x_other)
    halo = from_behind(x_low[group - HALO :] * tail_keep.astype(BF16), 1)
    hid_other = tensor_swap(order.tie(hid_own))
    one.next()
    one.next()
    one.next()

    two = Gather(ring, order, pack_two, True)
    two.start()
    one.finish()
    wide_s, wide_gates, wide_small = order.run(
        lambda *_: assemble(ring, (shard, n_gate, 16), one), one.theirs[-1][0]
    )
    wide_small = wide_small.reshape(count, 16, width)[:, 0]
    n_gain = gain_mixer.shape[0]
    gain_one = wide_small[:, :n_gain].reshape(width).astype(F32)
    gain_two = wide_small[:, n_gain : 2 * n_gain].reshape(width).astype(F32)
    taps = wide_small[:, 2 * n_gain : 2 * n_gain + shard * CONV]
    taps = taps.reshape(channels, CONV)
    param = wide_small[:, 2 * n_gain + shard * CONV : n_small].reshape(channels, 1)
    params = jnp.concatenate([taps] + [param] * (8 - CONV), axis=1).T.astype(F32)
    h_pad = order.run(
        lambda x, g: normed(x.astype(F32), g).astype(BF16),
        jnp.concatenate([halo, x_low]),
        gain_one,
    )
    h_one = h_pad[HALO:]
    two.next()
    padded = order.run(lambda h, w: cols_inner(h, w).astype(BF16), h_pad, wide_s)
    mixed, decay, prods, local_state, ends = order.run(
        mix, padded, marks, params, wide_gates
    )
    enter = Entering(order, ends, hops, False)
    two.next()
    enter.next()
    two.next()
    dy = Gather(ring, order, cotangent)
    dy.start()
    incoming = enter.finish()
    hid_other = order.arrive(hid_other)
    hid_theirs = core_swap(hid_own), core_swap(hid_other)
    two.finish()
    wide_b, wide_o = order.run(
        lambda *_: assemble(ring, (shard, shard), two), two.theirs[-1][0]
    )
    dy.next()

    def merge(h, w, local, p, inc):
        pre = cols_inner(h, w)
        return pre, ((local + p * inc) * gelu_tanh(pre)).astype(BF16)

    branch_pre, merged = order.run(merge, h_one, wide_b, local_state, prods, incoming)

    def mix_out(m, w, at):
        return jnp.dot(
            lax.dynamic_slice_in_dim(m, at, rows, 0), w, preferred_element_type=F32
        )

    mix_theirs = order.run(lambda m, w: mix_out(m, w, theirs_at).astype(BF16), merged, wide_o)
    mix_got = tensor_swap(mix_theirs)
    mix_mine = order.run(lambda m, w: mix_out(m, w, mine_at), merged, wide_o)
    dy.next()
    hidden = order.run(
        lambda *parts: jnp.concatenate(parts, axis=1), hid_own, hid_other, *hid_theirs
    )
    hid_g, hid_u, hid_d = hidden[0], hidden[1], hidden[2]
    x_val = block_input.astype(F32)
    x_one = order.run(lambda x, m, t: x + m + t.astype(F32), x_val, mix_mine, mix_got)
    n_two, norm_two_back = jax.vjp(normed, x_one, gain_two)
    h_own = n_two.astype(BF16)

    ff = Gather(ring, order, h_own)
    ff.start()
    dy.next()
    acts, d_gates, d_ups, d_hs, h_list, dy_list = [], [], [], [], [], []

    def piece(h_piece, dy_piece, w_g, w_u, w_d):
        gate_pre = cols_inner(h_piece, w_g)
        up_val = cols_inner(h_piece, w_u)
        gate_act, slope = gelu_and_slope(gate_pre)
        act = (gate_act * up_val).astype(BF16)
        d_act = cols_inner(dy_piece, w_d)
        d_gate = (d_act * up_val * slope).astype(BF16)
        d_up = (d_act * gate_act).astype(BF16)
        d_h = jnp.dot(d_gate, w_g, preferred_element_type=F32) + jnp.dot(
            d_up, w_u, preferred_element_type=F32
        )
        return act, d_gate, d_up, d_h.astype(BF16)

    def do_piece(h_piece, dy_piece):
        out = order.run(piece, h_piece, dy_piece, hid_g, hid_u, hid_d)
        for kept, value in zip((acts, d_gates, d_ups, d_hs, h_list, dy_list), (*out, h_piece, dy_piece)):
            kept.append(value)

    do_piece(h_own, cotangent)
    for step in range(ring.reach - SHOWN, ring.reach - 1):
        ff.next()
        if step == ring.reach - SHOWN:
            first = 0
        else:
            first = step
        if step == ring.reach - 3:
            dy.finish()
        for k in range(first, step + 1):
            do_piece(jnp.concatenate(ff.pairs[k]), jnp.concatenate(dy.pairs[k]))
    ff.finish()
    do_piece(jnp.concatenate(ff.far), jnp.concatenate(dy.far))

    def chunks(parts):
        out = plain_parts(parts[:1])
        for pair in parts[1:-1]:
            out += [Part(lambda v: v[:rows].astype(F32), pair)]
            out += [Part(lambda v: v[rows:].astype(F32), pair)]
        return out + plain_parts(parts[-1:])

    back = Scatter(ring, order, chunks(d_hs), rows // 2)
    back.start()
    downs = [
        order.run(lambda a, w: jnp.dot(a, w, preferred_element_type=F32).astype(BF16), a, hid_d)
        for a in acts
    ]

    def hidden_grad(lefts, rights):
        return order.run(
            lambda a, b: rows_inner(a, b).astype(BF16),
            jnp.concatenate(lefts),
            jnp.concatenate(rights),
        )

    back.next()
    g_gate = hidden_grad(d_gates, h_list)
    back.next()
    g_up = hidden_grad(d_ups, h_list)
    back.next()
    g_down = hidden_grad(acts, dy_list)
    unit = g_gate.shape[0] // 4
    hid_back = [core_swap(g[2 * unit :]) for g in (g_gate, g_up, g_down)]

    def dense_back(d_h, dy_own):
        d_x, g_gain = norm_two_back(d_h)
        d_x = dy_own.astype(F32) + d_x
        return d_x, g_gain, d_x.astype(BF16)

    d_x_one, g_gain_two, dz_own = back.finish(dense_back, cotangent)
    dz_other = tensor_swap(dz_own)
    down = Scatter(ring, order, chunks(downs), rows // 2)
    down.start()
    hid_mine, hid_got = [], []

    def hidden_add(g, t):
        mine, send = order.run(
            lambda a, b: (
                a[:unit].astype(F32) + b[:unit].astype(F32),
                plus(a[unit : 2 * unit], b[unit:]),
            ),
            g,
            t,
        )
        hid_mine.append(mine)
        hid_got.append(send)

    hidden_add(g_gate, hid_back[0])
    hidden_add(g_up, hid_back[1])
    down.next()
    hidden_add(g_down, hid_back[2])
    d_mix = order.run(functools.partial(ordered, side), dz_own, dz_other)
    hid_got = [tensor_swap(order.tie(send)) for send in hid_got]
    d_branch, rev_prods, rev_state, back_ends = order.run(
        back_scan, d_mix, wide_o, branch_pre, decay, prods, local_state, incoming
    )
    leave = Entering(order, back_ends, hops, True)
    down.next()
    mine_two, theirs_two = order.run(
        lambda *v: ring_grads(ring, shard, v[:2], v[2:]), d_branch, merged, h_one, d_mix
    )
    theirs_two = core_swap(theirs_two)
    leave.next()
    later = leave.finish()
    down.next()
    d_sig, sig_tail, rim, sums, g_gates = order.run(
        back_mix,
        rev_prods,
        rev_state,
        later,
        prods,
        local_state,
        incoming,
        mixed,
        padded,
        marks,
        params,
        wide_gates,
    )
    rim = from_behind(rim, -1)
    ring_two = Scatter(ring, order, ring_parts(mine_two, theirs_two), shard)
    ring_two.start()

    def with_rim(sig, tail, edge):
        tail = tail + edge * tail_keep[HALO - 8 :].astype(F32)
        return lax.dynamic_update_slice(sig, tail.astype(BF16), (group - 8, 0))

    d_signal = order.run(with_rim, d_sig, sig_tail, rim)

    def d_h_rows(branch, signal, w_b, w_s, at):
        return jnp.dot(
            lax.dynamic_slice_in_dim(branch, at, rows, 0), w_b, preferred_element_type=F32
        ) + jnp.dot(
            lax.dynamic_slice_in_dim(signal, at, rows, 0), w_s, preferred_element_type=F32
        )

    d_h_theirs = order.run(
        functools.partial(d_h_rows, at=theirs_at), d_branch, d_signal, wide_b, wide_s
    )
    d_h_got = tensor_swap(d_h_theirs.astype(BF16))
    d_h_mine = order.run(
        functools.partial(d_h_rows, at=mine_at), d_branch, d_signal, wide_b, wide_s
    )

    def gain_sum(mine, theirs, x, other, g_two):
        def unit(v):
            v = v.astype(F32)
            return v * lax.rsqrt(jnp.mean(v * v, axis=-1, keepdims=True) + EPS)

        return jnp.stack([jnp.sum(mine * unit(x) + theirs * unit(other), axis=0), g_two])

    gains = order.run(gain_sum, d_h_mine, d_h_theirs, block_input, x_other, g_gain_two)
    gains_other = tensor_swap(gains)
    ring_two.next()
    block_output = down.finish(lambda d, x: (x + d).astype(BF16), x_one)

    mine_last, theirs_last = order.run(
        lambda a, b, g: ring_grads(ring, shard, (a,), (b,), g), d_signal, h_one, g_gates
    )
    theirs_last = core_swap(theirs_last)
    n_rows = shard * (CONV + 1) + 2 * n_gain

    def small_rows(total, gain, gain_other):
        gain = gain + gain_other
        return jnp.concatenate(
            [
                total[:CONV].T.reshape(count, shard * CONV),
                total[CONV].reshape(count, shard),
                gain[0].reshape(count, n_gain),
                gain[1].reshape(count, n_gain),
            ],
            axis=1,
        )

    smalls = order.run(small_rows, sums, gains, gains_other)
    smalls_other = core_swap(smalls)

    def input_back(mine, got, d_x):
        _, norm_one_back = jax.vjp(lambda v: normed(v, gain_one), x_val)
        return d_x + norm_one_back(mine + got.astype(F32))[0]

    grad_input = order.run(input_back, d_h_mine, d_h_got, d_x_one)
    ring_two.next()
    smalls = order.run(
        lambda a, b: jnp.pad(a + b, ((0, 0), (0, width - n_rows))), smalls, smalls_other
    )

    def last_part(k, distance):
        at = 2 * ring.chip_at(distance) + ring.core

        def cut(a, b, small):
            big = a[k].astype(F32) + b[k].astype(F32)
            return jnp.concatenate([big, lax.dynamic_slice_in_dim(small, at, 1, 0)])

        return Part(cut, mine_last, theirs_last, smalls)

    ring_last = Scatter(
        ring,
        order,
        [last_part(k, distance) for k, distance in enumerate(ring_distances(ring))],
        (shard + n_gate) // 32 * 16 or shard // 2,
    )
    ring_last.start()
    hid_sums = [
        order.run(lambda a, b: a + b.astype(F32), mine, got)
        for mine, got in zip(hid_mine[:2], hid_got[:2])
    ]
    ring_two.next()
    ring_last.next()
    hid_sums.append(order.run(lambda a, b: a + b.astype(F32), hid_mine[2], hid_got[2]))
    s_gate, s_up, s_down = hid_sums[0].T, hid_sums[1].T, hid_sums[2]
    ring_last.next()
    total_two = ring_two.finish()
    s_branch = total_two[:shard].T
    s_mixout = total_two[shard:]
    ring_last.next()
    last = ring_last.finish()
    s_signal = last[:shard].T
    s_gates = [
        jnp.swapaxes(v.reshape(n_gate, heads_here, BLOCK), 0, 1)
        for v in jnp.split(last[shard : shard + n_gate], 2, axis=1)
    ]
    s_small = last[shard + n_gate]
    s_taps = s_small[: shard * CONV].reshape(shard, CONV)
    s_param = s_small[shard * CONV : shard * (CONV + 1)]
    s_gain_one = s_small[n_rows - 2 * n_gain : n_rows - n_gain]
    s_gain_two = s_small[n_rows - n_gain : n_rows]
    return (
        block_output,
        grad_input,
        s_gain_one,
        s_branch,
        s_signal,
        s_gates[0],
        s_gates[1],
        s_taps,
        s_param,
        s_mixout,
        s_gain_two,
        s_gate,
        s_up,
        s_down,
    )


def solution(mesh):
    placed = (
        P(("dp", "tensor"), None),
        P("dp"),
        P(("dp", "tensor"), None),
        P("dp"),
        P(None, ("tensor", "dp")),
        P(None, ("tensor", "dp")),
        P("tensor", "dp", None),
        P("tensor", "dp", None),
        P(("tensor", "dp"), None),
        P(("tensor", "dp")),
        P(("tensor", "dp"), None),
        P("dp"),
        P(None, ("tensor", "dp")),
        P(None, ("tensor", "dp")),
        P(("tensor", "dp"), None),
    )
    return jax.shard_map(
        per_device,
        mesh=mesh,
        in_specs=placed,
        out_specs=(
            P(("dp", "tensor"), None),
            P(("dp", "tensor"), None),
            P("dp"),
            P(None, ("tensor", "dp")),
            P(None, ("tensor", "dp")),
            P("tensor", "dp", None),
            P("tensor", "dp", None),
            P(("tensor", "dp"), None),
            P(("tensor", "dp")),
            P(("tensor", "dp"), None),
            P("dp"),
            P(None, ("tensor", "dp")),
            P(None, ("tensor", "dp")),
            P(("tensor", "dp"), None),
        ),
        check_vma=False,
    )
```

```python
import functools

import jax
import jax.numpy as jnp
from jax import lax
from jax.experimental import pallas as pl
from jax.experimental.pallas import tpu as pltpu
from jax.sharding import PartitionSpec as P

BLOCK = 256
CONV = 4
MAXLEN = 1024
EPS = 1e-06
HALO = 16
BF16 = jnp.bfloat16
F32 = jnp.float32


def ring_order(chips):
    return list(range(0, chips, 2)) + list(range(chips - 1, 0, -2))


class Ring:
    def __init__(self):
        count = lax.axis_size("dp")
        self.chips = count // 2
        self.reach = self.chips // 2
        order = ring_order(self.chips)
        self.up_route = [
            (order[p] * 2 + c, order[(p + 1) % self.chips] * 2 + c)
            for p in range(self.chips)
            for c in range(2)
        ]
        self.down_route = [(b, a) for a, b in self.up_route]
        me = lax.axis_index("dp")
        chip = me // 2
        self.core = lax.rem(me, 2)
        self.place = jnp.where(
            lax.rem(chip, 2) == 0, chip // 2, self.chips - 1 - chip // 2
        )

    def chip_at(self, distance):
        p = lax.rem(self.place - distance + self.chips, self.chips)
        return jnp.where(p < self.reach, 2 * p, 2 * (self.chips - 1 - p) + 1)

    def up(self, value):
        return lax.ppermute(value, "dp", self.up_route)

    def down(self, value):
        return lax.ppermute(value, "dp", self.down_route)


class Order:
    def __init__(self):
        self.token = None

    def tie(self, *values):
        if self.token is not None:
            values = lax.optimization_barrier((values, self.token))[0]
        return values if len(values) > 1 else values[0]

    def arrive(self, *values):
        values = lax.optimization_barrier((values, self.token))[0]
        self.token = values[-1]
        return values if len(values) > 1 else values[0]

    def run(self, function, *values):
        values = self.tie(*values)
        out = function(*values) if isinstance(values, tuple) else function(values)
        self.token = tuple(jax.tree.leaves(out))
        return out


SHOWN = 4


class Gather:
    def __init__(self, ring, order, value, both_cores=False):
        self.ring, self.order = ring, order
        self.own = value
        self.half = value.shape[0] // 32 * 16 or value.shape[0] // 2
        self.flight = (value, value)
        self.pairs, self.far = [], None
        self.theirs = [] if both_cores else None
        self.settled = False
        self.steps = 0

    def start(self):
        self.send()
        self.swap(self.own)
        for _ in range(self.ring.reach - SHOWN):
            self.next()

    def swap(self, *values):
        if self.theirs is not None:
            self.theirs.append(tuple(core_swap(v) for v in values))

    def send(self):
        self.steps += 1
        u, d = self.order.tie(*self.flight)
        if self.steps == self.ring.reach:
            u, d = u[: self.half], d[self.half :]
        self.flight = (self.ring.up(u), self.ring.down(d))

    def land(self):
        swapped = self.theirs.pop() if self.theirs and not self.settled else ()
        self.settled = False
        landed = self.order.arrive(*swapped, *self.flight)
        self.flight = landed[len(swapped) :]
        if swapped:
            self.theirs.append(landed[: len(swapped)])

    def next(self):
        self.land()
        landed = self.flight
        self.pairs.append(landed)
        self.send()
        self.swap(*landed)

    def settle(self):
        swapped = self.order.arrive(*self.theirs.pop())
        self.theirs.append(swapped)
        self.settled = True

    def finish(self):
        self.land()
        self.far = self.flight
        self.swap(*self.far)


class Scatter:
    def __init__(self, ring, order, parts, half):
        self.ring, self.order = ring, order
        self.parts, self.half = list(parts), half
        self.steps = 0

    def start(self):
        far = self.parts.pop()
        self.flight = self.order.run(
            lambda *v: (far(v, 0, self.half), far(v, self.half, None)), *far.values
        )
        self.send()
        for _ in range(self.ring.reach - SHOWN):
            self.next()

    def send(self):
        self.steps += 1
        u, d = self.order.tie(*self.flight)
        self.flight = (self.ring.down(u), self.ring.up(d))

    def next(self):
        ahead, behind = self.parts.pop(), self.parts.pop()
        half, first = self.half, self.steps == 1

        def add(to_down, to_up, *values):
            u_values, d_values = values[: len(behind.values)], values[len(behind.values) :]
            if first:
                return (
                    jnp.concatenate(
                        [behind(u_values, 0, half, to_down), behind(u_values, half, None)]
                    ),
                    jnp.concatenate(
                        [ahead(d_values, 0, half), ahead(d_values, half, None, to_up)]
                    ),
                )
            return behind(u_values, 0, None, to_down), ahead(d_values, 0, None, to_up)

        self.flight = self.order.run(add, *self.flight, *behind.values, *ahead.values)
        self.send()

    def finish(self, function=None, *more):
        own = self.parts.pop()

        def total(to_down, to_up, *values):
            count = len(own.values)
            out = own(values[:count], 0, None, to_down, to_up, F32)
            return function(out, *values[count:]) if function else out

        return self.order.run(total, *self.flight, *own.values, *more)


class Part:
    def __init__(self, cut, *values):
        self.cut, self.values = cut, values

    def __call__(self, values, first, last, *others):
        dtype = BF16
        if others and others[-1] is F32:
            others, dtype = others[:-1], F32
        total = self.cut(*values)[first:last]
        for other in others:
            total = total + other.astype(F32)
        return total.astype(dtype)


def plain_parts(values):
    return [Part(lambda v: v.astype(F32), value) for value in values]


def plus(a, b):
    return (a.astype(F32) + b.astype(F32)).astype(BF16)


def core_swap(value):
    count = lax.axis_size("dp")
    return lax.ppermute(value, "dp", [(i, i ^ 1) for i in range(count)])


def holder_groups():
    return [
        [(2 * chip + core) * 2 + side for core in range(2) for side in range(2)]
        for chip in range(lax.axis_size("dp") // 2)
    ]


def holders_gather(value):
    return lax.all_gather(
        value, ("dp", "tensor"), axis=0, tiled=True, axis_index_groups=holder_groups()
    )


def holders_sum(value):
    return lax.psum_scatter(
        value,
        ("dp", "tensor"),
        scatter_dimension=0,
        tiled=True,
        axis_index_groups=holder_groups(),
    )


def tensor_swap(value):
    return lax.ppermute(value, "tensor", [(0, 1), (1, 0)])


def from_behind(block, distance):
    devices = range(lax.axis_size("dp"))
    route = [(i - distance, i) for i in devices if i - distance in devices]
    return lax.ppermute(block, "dp", route)


class Entering:
    def __init__(self, order, window, hops, reverse):
        self.order, self.sign = order, (-1 if reverse else 1)
        size = 1
        while 4 * size < hops:
            window = follow(from_behind(window, self.sign * size), window)
            size *= 2
        self.size, self.hops, self.window = size, hops, window
        if size < hops:
            self.behind = from_behind(window, self.sign * size)

    def next(self):
        if 2 * self.size < self.hops:
            self.window = self.order.run(follow, self.behind, self.window)
            self.size *= 2
        self.near = from_behind(self.window, self.sign)
        if self.size < self.hops:
            self.rest = from_behind(self.window, self.sign * (1 + self.size))

    def finish(self):
        if self.size >= self.hops:
            return self.order.arrive(self.near)[1:]
        return self.order.run(lambda n, r: n[:1] * r[1:] + n[1:], self.near, self.rest)


def follow(first, second):
    return jnp.stack([first[0] * second[0], second[0] * first[1] + second[1]])


def normed(value, gain):
    return value * lax.rsqrt(jnp.mean(value * value, axis=-1, keepdims=True) + EPS) * gain


def gelu_tanh(value):
    return jax.nn.gelu(value, approximate=True)


GELU_IN = 0.7978845608028654
GELU_CUBE = 0.044715


def gelu_and_slope(value):
    square = value * value
    t = jnp.tanh(GELU_IN * (value + GELU_CUBE * (square * value)))
    half = 0.5 * (1.0 + t)
    slope = half + 0.5 * value * (1.0 - t * t) * (GELU_IN * (1.0 + 3.0 * GELU_CUBE * square))
    return value * half, slope


def rows_inner(left, right):
    return lax.dot_general(
        left, right, (((0,), (0,)), ((), ())), preferred_element_type=F32
    )


def cols_inner(left, right):
    return lax.dot_general(
        left, right, (((1,), (1,)), ((), ())), preferred_element_type=F32
    )


def scan_rows(reverse, a_ref, b_ref, p_ref, s_ref):
    rows, width = a_ref.shape
    blocks = rows // 8
    row = lax.broadcasted_iota(jnp.int32, (8, width), 0)

    def step(i, carry):
        p_in, s_in = carry
        at = (blocks - 1 - i) if reverse else i
        here = pl.ds(pl.multiple_of(at * 8, 8), 8)
        a = a_ref[here, :]
        b = b_ref[here, :]
        for shift in (1, 2, 4):
            turn = 8 - shift if reverse else shift
            inside = (row < 8 - shift) if reverse else (row >= shift)
            a_prev = jnp.where(inside, pltpu.roll(a, turn, 0), 1.0)
            b_prev = jnp.where(inside, pltpu.roll(b, turn, 0), 0.0)
            b = a * b_prev + b
            a = a * a_prev
        b = b + a * s_in
        a = a * p_in
        p_ref[here, :] = a
        s_ref[here, :] = b
        last = 0 if reverse else 7
        return (a[last : last + 1], b[last : last + 1])

    return lax.fori_loop(
        0, blocks, step, (jnp.ones((1, width), F32), jnp.zeros((1, width), F32))
    )


def lru_gates(mixed, w_ig, w_dg, param):
    gx_pre = jnp.dot(mixed, w_ig, preferred_element_type=F32)
    ga_pre = jnp.dot(mixed, w_dg, preferred_element_type=F32)
    return jax.nn.sigmoid(gx_pre), jax.nn.sigmoid(ga_pre), jax.nn.softplus(param)


def one_minus_square(log_a, e):
    x = 2.0 * log_a
    series = -x * (
        1.0 + x * (1 / 2 + x * (1 / 6 + x * (1 / 24 + x * (1 / 120 + x * (1 / 720)))))
    )
    return jnp.where(x > -0.3, series, 1.0 - e * e)


def mix_body(pad_ref, marks_ref, params_ref, ig_ref, dg_ref, *refs):
    mixed_ref, decay_ref, prods_ref, state_ref, ends_ref, a_scr, b_scr = refs
    block = pl.program_id(0)
    rows = mixed_ref.shape[0]
    pad = pad_ref[...].astype(F32)
    total = params_ref[0:1, :] * pad[HALO:] * marks_ref[:, 0:1]
    for k in range(1, CONV):
        behind = pltpu.roll(pad, k, 0)[HALO:]
        total = total + params_ref[k : k + 1, :] * behind * marks_ref[:, k : k + 1]
    mixed = total.astype(BF16)
    mixed_ref[...] = mixed
    gate_x, gate_a, soft = lru_gates(mixed, ig_ref[...], dg_ref[...], params_ref[CONV : CONV + 1, :])
    reset = marks_ref[:, CONV : CONV + 1]
    keep = 1.0 - reset
    log_a = -8.0 * gate_a * soft
    e = jnp.exp(log_a)
    decay = e * keep
    multiplier = jnp.sqrt(one_minus_square(log_a, e)) * keep + reset
    decay_ref[...] = decay
    here = pl.ds(pl.multiple_of(block * BLOCK, BLOCK), BLOCK)
    a_scr[:, here] = decay
    b_scr[:, here] = gate_x * mixed.astype(F32) * multiplier

    @pl.when(block == pl.num_programs(0) - 1)
    def _():
        p_end, s_end = scan_rows(False, a_scr, b_scr, prods_ref, state_ref)
        ends_ref[0:1, :] = p_end
        ends_ref[1:2, :] = s_end


def back_scan_body(dz_ref, wide_ref, pre_ref, decay_ref, prods_ref, state_ref, in_ref, *refs):
    branch_ref, rev_p_ref, rev_s_ref, ends_ref, a_scr, b_scr, first_scr = refs
    block = pl.program_id(0)
    rows = pre_ref.shape[0]
    d_merged = lax.dot_general(
        dz_ref[...], wide_ref[...], (((1,), (1,)), ((), ())), preferred_element_type=F32
    )
    branch, slope = gelu_and_slope(pre_ref[...])
    state = state_ref[...] + prods_ref[...] * in_ref[...]
    branch_ref[...] = (d_merged * state * slope).astype(BF16)
    decay = decay_ref[...]
    row = lax.broadcasted_iota(jnp.int32, decay.shape, 0)
    ahead = jnp.where(row == rows - 1, 1.0, pltpu.roll(decay, rows - 1, 0))
    here = pl.ds(pl.multiple_of(block * BLOCK, BLOCK), BLOCK)
    a_scr[:, here] = ahead
    b_scr[:, here] = d_merged * branch
    first_scr[:, here] = decay[0:8]

    @pl.when(block == pl.num_programs(0) - 1)
    def _():
        p_end, s_end = scan_rows(True, a_scr, b_scr, rev_p_ref, rev_s_ref)
        first = first_scr[0:1, :]
        ends_ref[0:1, :] = first * p_end
        ends_ref[1:2, :] = first * s_end


def back_mix_body(*refs):
    (rev_p_ref, rev_s_ref, later_ref, prods_ref, state_ref, in_ref) = refs[:6]
    (mixed_ref, pad_ref, marks_ref, params_ref, ig_ref, dg_ref) = refs[6:12]
    sig_ref, tail_ref, rim_ref, sums_ref, gates_ref = refs[12:]
    rows = mixed_ref.shape[0]
    g = rev_s_ref[...] + rev_p_ref[...] * later_ref[...]
    entering_row = in_ref[...]
    state = state_ref[...] + prods_ref[...] * entering_row
    row = lax.broadcasted_iota(jnp.int32, state.shape, 0)
    previous = jnp.where(row == 0, entering_row, pltpu.roll(state, 1, 0))
    mixed = mixed_ref[...]
    mixed_f = mixed.astype(F32)
    param = params_ref[CONV : CONV + 1, :]
    gate_x, gate_a, soft = lru_gates(mixed, ig_ref[...], dg_ref[...], param)
    reset = marks_ref[:, CONV : CONV + 1]
    keep = 1.0 - reset
    log_a = -8.0 * gate_a * soft
    e = jnp.exp(log_a)
    root = jnp.sqrt(one_minus_square(log_a, e))
    multiplier = root * keep + reset
    d_multiplier = g * gate_x * mixed_f
    d_log_a = keep * (g * previous * e - d_multiplier * (e * e) / root)
    d_gate_a = d_log_a * (-8.0 * soft)
    d_param = jnp.sum(d_log_a * (-8.0 * gate_a), axis=0, keepdims=True) * jax.nn.sigmoid(param)
    d_ga = (d_gate_a * gate_a * (1.0 - gate_a)).astype(BF16)
    d_gx = (g * mixed_f * multiplier * gate_x * (1.0 - gate_x)).astype(BF16)
    for half, d_pre in enumerate((d_gx, d_ga)):
        at = (half * pl.num_programs(0) + pl.program_id(0)) * BLOCK
        gates_ref[:, pl.ds(pl.multiple_of(at, BLOCK), BLOCK)] = lax.dot_general(
            mixed, d_pre, (((0,), (0,)), ((), ())), preferred_element_type=F32
        ).astype(BF16)
    d_mixed = (
        g * gate_x * multiplier
        + lax.dot_general(d_gx, ig_ref[...], (((1,), (1,)), ((), ())), preferred_element_type=F32)
        + lax.dot_general(d_ga, dg_ref[...], (((1,), (1,)), ((), ())), preferred_element_type=F32)
    )
    pad = pad_ref[...].astype(F32)
    front = jnp.zeros((HALO, BLOCK), F32)
    d_pad = None
    for k in range(CONV):
        masked = d_mixed * marks_ref[:, k : k + 1]
        behind = pad if k == 0 else pltpu.roll(pad, k, 0)
        sums_ref[k : k + 1, :] = jnp.sum(masked * behind[HALO:], axis=0, keepdims=True)
        term = jnp.concatenate([front, masked * params_ref[k : k + 1, :]])
        if k:
            term = pltpu.roll(term, rows + HALO - k, 0)
        d_pad = term if d_pad is None else d_pad + term
    sums_ref[CONV : CONV + 1, :] = d_param
    sums_ref[CONV + 1 : 8, :] = jnp.zeros((8 - CONV - 1, BLOCK), F32)
    rim_ref[...] = d_pad[HALO - 8 : HALO]
    sig_ref[...] = d_pad[HALO:].astype(BF16)
    tail_ref[...] = d_pad[HALO + rows - 8 :]


def rows_spec(rows):
    return pl.BlockSpec((rows, BLOCK), lambda h: (0, h))


def whole_spec(*shape):
    return pl.BlockSpec(shape, lambda h: (0,) * len(shape))


def gate_specs(heads):
    return [
        pl.BlockSpec((BLOCK, BLOCK), lambda h: (0, h)),
        pl.BlockSpec((BLOCK, BLOCK), lambda h: (0, heads + h)),
    ]


BIG = pltpu.CompilerParams(vmem_limit_bytes=48 << 20)
LIGHT = pl.CostEstimate(flops=0, bytes_accessed=0, transcendentals=0)
HEAVY = pl.CostEstimate(flops=500_000_000_000, bytes_accessed=0, transcendentals=0)


def shaped(rows, width, dtype=F32):
    return jax.ShapeDtypeStruct((rows, width), dtype)


def mix(padded, marks, params, w_gates):
    rows, width = padded.shape[0] - HALO, padded.shape[1]
    return pl.pallas_call(
        mix_body,
        grid=(width // BLOCK,),
        in_specs=[
            rows_spec(rows + HALO),
            whole_spec(rows, 8),
            rows_spec(8),
            *gate_specs(width // BLOCK),
        ],
        out_specs=[
            rows_spec(rows),
            rows_spec(rows),
            whole_spec(rows, width),
            whole_spec(rows, width),
            whole_spec(2, width),
        ],
        out_shape=[
            shaped(rows, width, BF16),
            shaped(rows, width),
            shaped(rows, width),
            shaped(rows, width),
            shaped(2, width),
        ],
        scratch_shapes=[pltpu.VMEM((rows, width), F32)] * 2,
        cost_estimate=LIGHT,
        compiler_params=BIG,
    )(padded, marks, params, w_gates, w_gates)


def back_scan(dz, wide, pre, decay, prods, state, incoming):
    rows, width = pre.shape
    depth = dz.shape[1]
    return pl.pallas_call(
        back_scan_body,
        grid=(width // BLOCK,),
        in_specs=[
            whole_spec(rows, depth),
            pl.BlockSpec((BLOCK, depth), lambda h: (h, 0)),
            rows_spec(rows),
            rows_spec(rows),
            rows_spec(rows),
            rows_spec(rows),
            rows_spec(1),
        ],
        out_specs=[
            rows_spec(rows),
            whole_spec(rows, width),
            whole_spec(rows, width),
            whole_spec(2, width),
        ],
        out_shape=[
            shaped(rows, width, BF16),
            shaped(rows, width),
            shaped(rows, width),
            shaped(2, width),
        ],
        scratch_shapes=[
            pltpu.VMEM((rows, width), F32),
            pltpu.VMEM((rows, width), F32),
            pltpu.VMEM((8, width), F32),
        ],
        cost_estimate=LIGHT,
        compiler_params=BIG,
    )(dz, wide, pre, decay, prods, state, incoming)


def back_mix(rev_p, rev_s, later, prods, state, incoming, mixed, padded, marks, params, w_gates):
    rows, width = mixed.shape
    heads = width // BLOCK
    return pl.pallas_call(
        back_mix_body,
        grid=(heads,),
        in_specs=[
            rows_spec(rows),
            rows_spec(rows),
            rows_spec(1),
            rows_spec(rows),
            rows_spec(rows),
            rows_spec(1),
            rows_spec(rows),
            rows_spec(rows + HALO),
            whole_spec(rows, 8),
            rows_spec(8),
            *gate_specs(heads),
        ],
        out_specs=[
            rows_spec(rows),
            rows_spec(8),
            rows_spec(8),
            rows_spec(8),
            whole_spec(BLOCK, 2 * width),
        ],
        out_shape=[
            shaped(rows, width, BF16),
            shaped(8, width),
            shaped(8, width),
            shaped(8, width),
            shaped(BLOCK, 2 * width, BF16),
        ],
        cost_estimate=HEAVY,
        compiler_params=BIG,
    )(rev_p, rev_s, later, prods, state, incoming, mixed, padded, marks, params, w_gates, w_gates)


def assemble_body(sizes, runs, places, at_ref, *refs):
    count = len(runs)
    chunks = refs[:count]
    outs = refs[count : count + len(sizes)]
    scratch, in_sems, out_sems = refs[count + len(sizes) :]
    loads = [
        pltpu.make_async_copy(
            chunk, scratch.at[slot, pl.ds(first, rows)], in_sems.at[i]
        )
        for i, (chunk, (slot, first, rows)) in enumerate(zip(chunks, runs))
    ]
    for load in loads:
        load.start()
    stores = []
    for slot in range(places):
        for load, run in zip(loads, runs):
            if run[0] == slot:
                load.wait()
        base = 0
        for out, size in zip(outs, sizes):
            target = pl.ds(pl.multiple_of(at_ref[slot] * size, 16), size)
            stores.append(
                pltpu.make_async_copy(
                    scratch.at[slot, pl.ds(base, size)],
                    out.at[target],
                    out_sems.at[len(stores)],
                )
            )
            stores[-1].start()
            base += size
    for store in stores:
        store.wait()


def assemble(ring, sizes, gathered):
    near = [(0, (gathered.own,))]
    for k, (u, d) in enumerate(gathered.pairs, 1):
        near += [(k, (u,)), (-k, (d,))]
    near.append((ring.reach, gathered.far))
    their = [gathered.theirs[0]]
    for pair in gathered.theirs[1:-1]:
        their += [(v,) for v in pair]
    their.append(gathered.theirs[-1])
    rows, width = gathered.own.shape
    slots = []
    for (distance, mine), theirs in zip(near, their):
        chip = ring.chip_at(distance)
        slots += [(2 * chip + ring.core, mine), (2 * chip + 1 - ring.core, theirs)]
    at = jnp.stack([place for place, _ in slots]).astype(jnp.int32)
    places = len(slots)
    if any(size % 16 for size in sizes):
        every = jnp.stack([jnp.concatenate(v) if len(v) > 1 else v[0] for _, v in slots])
        every = jnp.zeros_like(every).at[at].set(every)
        cuts = [sum(sizes[:i]) for i in range(len(sizes) + 1)]
        return [every[:, a:b].reshape(-1, width) for a, b in zip(cuts, cuts[1:])]
    chunks, runs = [], []
    for slot, (_, values) in enumerate(slots):
        first = 0
        for value in values:
            chunks.append(value)
            runs.append((slot, first, value.shape[0]))
            first += value.shape[0]
    anywhere = pl.BlockSpec(memory_space=pl.ANY)
    return pl.pallas_call(
        functools.partial(assemble_body, sizes, runs, places),
        out_shape=[shaped(places * size, width, BF16) for size in sizes],
        in_specs=[pl.BlockSpec(memory_space=pltpu.SMEM)] + [anywhere] * len(chunks),
        out_specs=[anywhere] * len(sizes),
        scratch_shapes=[
            pltpu.VMEM((places, rows, width), BF16),
            pltpu.SemaphoreType.DMA((len(chunks),)),
            pltpu.SemaphoreType.DMA((places * len(sizes),)),
        ],
        cost_estimate=LIGHT,
        compiler_params=BIG,
    )(at, *chunks)


def ring_distances(ring):
    out = [0]
    for k in range(1, ring.reach):
        out += [k, -k]
    return out + [ring.reach]


def ring_grads_body(shard, chips, pairs, extra, at_ref, *refs):
    lefts, rights = refs[:pairs], refs[pairs : 2 * pairs]
    rest = refs[2 * pairs :]
    if extra:
        extra_ref, rest = rest[0], rest[1:]
    mine_ref, theirs_ref, turned, full, sems = rest
    core = at_ref[chips]
    width = full.shape[2]
    copies = []

    def send(source, size, base):
        for slot in range(chips):
            for out, c in ((mine_ref, core), (theirs_ref, 1 - core)):
                first = pl.multiple_of((2 * at_ref[slot] + c) * size, 16)
                copies.append(
                    pltpu.make_async_copy(
                        source.at[pl.ds(first, size)],
                        out.at[slot, pl.ds(base, size)],
                        sems.at[len(copies)],
                    )
                )
                copies[-1].start()

    if extra:
        send(extra_ref, extra, pairs * shard)
    for pair in range(pairs):
        turned[...] = lefts[pair][...].astype(F32).T.astype(BF16)

        def column(n, _):
            here = pl.ds(pl.multiple_of(n * BLOCK, BLOCK), BLOCK)
            full[pair, :, here] = jnp.dot(
                turned[...], rights[pair][:, here], preferred_element_type=F32
            ).astype(BF16)
            return 0

        lax.fori_loop(0, width // BLOCK, column, 0)
        send(full.at[pair], shard, pair * shard)
    for copy in copies:
        copy.wait()


def ring_grads(ring, shard, lefts, rights, extra=None):
    pairs, chips = len(lefts), ring.chips
    rows, channels = lefts[0].shape
    width = rights[0].shape[1]
    more = 0 if extra is None else extra.shape[0] // (2 * chips)
    at = [ring.chip_at(distance) for distance in ring_distances(ring)]
    if shard % 16 or more % 16:
        values = [rows_inner(a, b).astype(BF16) for a, b in zip(lefts, rights)]
        values += [] if extra is None else [extra]
        values = jnp.concatenate([v.reshape(chips, 2, -1, width) for v in values], axis=2)
        values = values[jnp.stack(at)]
        return (
            lax.dynamic_index_in_dim(values, ring.core, 1, False),
            lax.dynamic_index_in_dim(values, 1 - ring.core, 1, False),
        )
    in_vmem = pl.BlockSpec(memory_space=pltpu.VMEM)
    anywhere = pl.BlockSpec(memory_space=pl.ANY)
    out = jax.ShapeDtypeStruct((chips, pairs * shard + more, width), BF16)
    return pl.pallas_call(
        functools.partial(ring_grads_body, shard, chips, pairs, more),
        out_shape=[out, out],
        in_specs=[pl.BlockSpec(memory_space=pltpu.SMEM)]
        + [in_vmem] * (2 * pairs + (extra is not None)),
        out_specs=[anywhere, anywhere],
        scratch_shapes=[
            pltpu.VMEM((channels, rows), BF16),
            pltpu.VMEM((pairs, channels, width), BF16),
            pltpu.SemaphoreType.DMA((2 * chips * (pairs + (extra is not None)),)),
        ],
        cost_estimate=LIGHT,
        compiler_params=BIG,
    )(
        jnp.stack(at + [ring.core]).astype(jnp.int32),
        *lefts,
        *rights,
        *(() if extra is None else (extra,)),
    )


def hidden_grad_body(heights, right_heights, which, *refs):
    count = len(right_heights)
    lefts, rights = refs[: len(heights)], refs[len(heights) : len(heights) + count]
    out_ref, turned, held, made, in_sems, out_sems = refs[-6:]
    parts, _, columns = held.shape
    holders, _, unit, _ = out_ref.shape
    loads, stores = [], []
    for part in range(parts):
        first = 0
        for i, height in enumerate(right_heights):
            loads.append(
                pltpu.make_async_copy(
                    rights[i].at[:, pl.ds(part * columns, columns)],
                    held.at[part, pl.ds(first, height)],
                    in_sems.at[part * count + i],
                )
            )
            loads[-1].start()
            first += height
    first = 0
    for left, height in zip(lefts, heights):
        turned[:, first : first + height] = left[...].astype(F32).T.astype(BF16)
        first += height
    for part in range(parts):
        for load in loads[part * count : (part + 1) * count]:
            load.wait()

        def column(n, _, part=part):
            here = pl.ds(pl.multiple_of(n * BLOCK, BLOCK), BLOCK)
            made[part, :, here] = jnp.dot(
                turned[...], held[part, :, here], preferred_element_type=F32
            ).astype(BF16)
            return 0

        lax.fori_loop(0, columns // BLOCK, column, 0)
        for holder in range(holders):
            stores.append(
                pltpu.make_async_copy(
                    made.at[part, pl.ds(holder * unit, unit)],
                    out_ref.at[holder, which, :, pl.ds(part * columns, columns)],
                    out_sems.at[part * holders + holder],
                )
            )
            stores[-1].start()
    for store in stores:
        store.wait()


def hidden_grad(which, into, lefts, rights):
    heights = [left.shape[0] for left in lefts]
    right_heights = [right.shape[0] for right in rights]
    depth, width = lefts[0].shape[1], rights[0].shape[1]
    unit = depth // 4
    if unit % 16 or any(height % 128 for height in heights):
        grad = rows_inner(jnp.concatenate(lefts), jnp.concatenate(rights)).astype(BF16)
        grad = grad.reshape(4, 1, unit, width)
        return grad if into is None else jnp.concatenate([into, grad], axis=1)
    parts = 2
    in_vmem = pl.BlockSpec(memory_space=pltpu.VMEM)
    anywhere = pl.BlockSpec(memory_space=pl.ANY)
    more = () if into is None else (into,)
    return pl.pallas_call(
        functools.partial(hidden_grad_body, heights, right_heights, which),
        out_shape=jax.ShapeDtypeStruct((4, 3, unit, width), BF16),
        in_specs=[in_vmem] * len(lefts) + [anywhere] * (len(rights) + len(more)),
        out_specs=anywhere,
        input_output_aliases={len(lefts) + len(rights): 0} if more else {},
        scratch_shapes=[
            pltpu.VMEM((depth, sum(heights)), BF16),
            pltpu.VMEM((parts, sum(heights), width // parts), BF16),
            pltpu.VMEM((parts, depth, width // parts), BF16),
            pltpu.SemaphoreType.DMA((parts * len(rights),)),
            pltpu.SemaphoreType.DMA((parts * 4,)),
        ],
        cost_estimate=LIGHT,
        compiler_params=BIG,
    )(*lefts, *rights, *more)


def piece_body(count, cuts, tiles, *refs):
    ins, dys, weights = refs[:count], refs[count : 2 * count], refs[2 * count : 2 * count + 3]
    act_ref, d_gate_ref, d_up_ref = refs[2 * count + 3 : 2 * count + 6]
    outs = refs[2 * count + 6 : 2 * count + 6 + len(cuts)]
    h, dy, w_g, w_u, w_d, total, row_sems, w_sems = refs[2 * count + 6 + len(cuts) :]
    row_loads, w_loads = [], []
    for to, sources in ((h, ins), (dy, dys)):
        first = 0
        for source in sources:
            size = source.shape[0]
            row_loads.append(
                pltpu.make_async_copy(
                    source, to.at[pl.ds(first, size)], row_sems.at[len(row_loads)]
                )
            )
            row_loads[-1].start()
            first += size
    for low, high in tiles:
        here = pl.ds(low, high - low)
        for source, to in zip(weights, (w_g, w_u, w_d)):
            w_loads.append(
                pltpu.make_async_copy(source.at[here], to.at[here], w_sems.at[len(w_loads)])
            )
            w_loads[-1].start()
    for load in row_loads:
        load.wait()
    for i, (low, high) in enumerate(tiles):
        for load in w_loads[3 * i : 3 * i + 3]:
            load.wait()
        gate_act, slope = gelu_and_slope(cols_inner(h[...], w_g[low:high, :]))
        up_val = cols_inner(h[...], w_u[low:high, :])
        d_act = cols_inner(dy[...], w_d[low:high, :])
        d_gate = (d_act * up_val * slope).astype(BF16)
        d_up = (d_act * gate_act).astype(BF16)
        act_ref[:, low:high] = (gate_act * up_val).astype(BF16)
        d_gate_ref[:, low:high] = d_gate
        d_up_ref[:, low:high] = d_up
        part = jnp.dot(d_gate, w_g[low:high, :], preferred_element_type=F32) + jnp.dot(
            d_up, w_u[low:high, :], preferred_element_type=F32
        )
        total[...] = part if i == 0 else total[...] + part
    first = 0
    for out, size in zip(outs, cuts):
        out[...] = total[first : first + size, :].astype(BF16)
        first += size


def piece(hs, dys, cuts, w_g, w_u, w_d):
    depth, width = w_g.shape
    rows = sum(cuts)
    tiles = [(low, min(low + BLOCK, depth)) for low in range(0, depth, BLOCK)]
    in_vmem = pl.BlockSpec(memory_space=pltpu.VMEM)
    anywhere = pl.BlockSpec(memory_space=pl.ANY)
    return pl.pallas_call(
        functools.partial(piece_body, len(hs), cuts, tiles),
        out_shape=[shaped(rows, depth, BF16)] * 3 + [shaped(cut, width, BF16) for cut in cuts],
        in_specs=[anywhere] * (2 * len(hs) + 3),
        out_specs=[in_vmem] * (3 + len(cuts)),
        scratch_shapes=[
            pltpu.VMEM((rows, width), BF16),
            pltpu.VMEM((rows, width), BF16),
            pltpu.VMEM((depth, width), BF16),
            pltpu.VMEM((depth, width), BF16),
            pltpu.VMEM((depth, width), BF16),
            pltpu.VMEM((rows, width), F32),
            pltpu.SemaphoreType.DMA((2 * len(hs),)),
            pltpu.SemaphoreType.DMA((3 * len(tiles),)),
        ],
        cost_estimate=LIGHT,
        compiler_params=BIG,
    )(*hs, *dys, w_g, w_u, w_d)


def widen_body(in_ref, *outs):
    first = 0
    for out in outs:
        size = out.shape[0]
        out[...] = in_ref[first : first + size, :].astype(F32)
        first += size


def widen(value, parts):
    rows, width = value.shape
    if rows // parts % 16:
        return [v.astype(F32) for v in jnp.split(value, parts)]
    columns = 2 * BLOCK
    size = rows // parts
    return pl.pallas_call(
        widen_body,
        grid=(width // columns,),
        in_specs=[pl.BlockSpec((rows, columns), lambda n: (0, n))],
        out_specs=[pl.BlockSpec((size, columns), lambda n: (0, n))] * parts,
        out_shape=[shaped(size, width)] * parts,
        cost_estimate=LIGHT,
        compiler_params=BIG,
    )(value)


def hidden_down_body(count, *refs):
    acts, w_ref, outs = refs[:count], refs[count], refs[count + 1 :]
    columns = 2 * BLOCK

    def column(n, _):
        here = pl.ds(pl.multiple_of(n * columns, columns), columns)
        for act, out in zip(acts, outs):
            out[:, here] = jnp.dot(
                act[...], w_ref[:, here], preferred_element_type=F32
            ).astype(BF16)
        return 0

    lax.fori_loop(0, w_ref.shape[1] // columns, column, 0)


def hidden_down(acts, w_down):
    depth, width = w_down.shape
    if sum(a.shape[0] for a in acts) > 2048:
        return [jnp.dot(a, w_down, preferred_element_type=F32).astype(BF16) for a in acts]
    in_vmem = pl.BlockSpec(memory_space=pltpu.VMEM)
    return pl.pallas_call(
        functools.partial(hidden_down_body, len(acts)),
        out_shape=[shaped(a.shape[0], width, BF16) for a in acts],
        in_specs=[in_vmem] * (len(acts) + 1),
        out_specs=[in_vmem] * len(acts),
        cost_estimate=LIGHT,
        compiler_params=BIG,
    )(*acts, w_down)


def input_back_body(x_ref, mine_ref, got_ref, d_x_ref, gain_ref, out_ref):
    x = x_ref[...].astype(F32)
    scaled = (mine_ref[...] + got_ref[...].astype(F32)) * gain_ref[...]
    r = lax.rsqrt(jnp.mean(x * x, axis=-1, keepdims=True) + EPS)
    along = jnp.mean(scaled * x, axis=-1, keepdims=True)
    out_ref[...] = d_x_ref[...] + r * scaled - (r * r * r) * along * x


def input_back(x, mine, got, d_x, gain):
    in_vmem = pl.BlockSpec(memory_space=pltpu.VMEM)
    return pl.pallas_call(
        input_back_body,
        out_shape=shaped(*x.shape),
        in_specs=[in_vmem] * 5,
        out_specs=in_vmem,
        cost_estimate=LIGHT,
        compiler_params=BIG,
    )(x, mine, got, d_x, gain)


def ring_parts(mine, theirs):
    def part(k):
        return Part(lambda a, b: a[k].astype(F32) + b[k].astype(F32), mine, theirs)

    return [part(k) for k in range(mine.shape[0])]


def ordered(ring_tensor, own, other):
    first = jnp.where(ring_tensor == 0, own, other)
    second = jnp.where(ring_tensor == 0, other, own)
    return jnp.concatenate([first, second])


def per_device(
    block_input,
    starts,
    cotangent,
    gain_mixer,
    w_branch,
    w_signal,
    w_input_gate,
    w_decay_gate,
    conv_taps,
    decay_param,
    w_mixout,
    gain_dense,
    w_gate,
    w_up,
    w_down,
):
    ring = Ring()
    side = lax.axis_index("tensor")
    count = lax.axis_size("dp")
    group = starts.shape[0]
    rows, width = block_input.shape
    shard = w_branch.shape[1]
    channels = shard * count
    lag = CONV - 1
    hops = -(-MAXLEN // group)
    heads_here = w_input_gate.shape[0]

    order = Order()
    mine_at, theirs_at = side * rows, (1 - side) * rows

    small = jnp.concatenate(
        [gain_mixer, gain_dense, conv_taps.reshape(-1), decay_param]
    )
    n_small = small.shape[0]
    small = jnp.pad(small, (0, 16 * width - n_small)).reshape(16, width)
    n_gate = w_input_gate.shape[1]
    gates = jnp.concatenate(
        [jnp.swapaxes(w, 0, 1).reshape(n_gate, channels) for w in (w_input_gate, w_decay_gate)],
        axis=1,
    )
    one = Gather(ring, order, jnp.concatenate([w_signal.T, gates, small]), True)
    order.token = one.own
    one.start()
    x_other = tensor_swap(block_input)
    hid_g, hid_u, hid_d = [holders_gather(w) for w in (w_gate.T, w_up.T, w_down)]
    pack_two = order.run(lambda *w: jnp.concatenate(w), w_branch.T, w_mixout)
    cumulative = jnp.cumsum(starts)
    padded_cum = jnp.concatenate([jnp.zeros((lag,), jnp.int32), cumulative])
    masks = [
        (cumulative - padded_cum[lag - k : lag - k + group] == 0).astype(F32)
        for k in range(CONV)
    ]
    marks = jnp.stack(masks + [starts.astype(F32)] * (8 - CONV), axis=1)
    tail_keep = (cumulative[group - 1] - cumulative[group - HALO :] == 0)[:, None]
    one.next()
    x_low = order.run(functools.partial(ordered, side), block_input, x_other)
    halo = from_behind(x_low[group - HALO :] * tail_keep.astype(BF16), 1)
    one.next()
    one.next()

    two = Gather(ring, order, pack_two, True)
    two.start()
    one.finish()
    wide_s, wide_gates, wide_small = order.run(
        lambda *_: assemble(ring, (shard, n_gate, 16), one), one.theirs[-1][0]
    )
    wide_small = wide_small.reshape(count, 16, width)[:, 0]
    n_gain = gain_mixer.shape[0]
    gain_one = wide_small[:, :n_gain].reshape(width).astype(F32)
    gain_two = wide_small[:, n_gain : 2 * n_gain].reshape(width).astype(F32)
    taps = wide_small[:, 2 * n_gain : 2 * n_gain + shard * CONV]
    taps = taps.reshape(channels, CONV)
    param = wide_small[:, 2 * n_gain + shard * CONV : n_small].reshape(channels, 1)
    params = jnp.concatenate([taps] + [param] * (8 - CONV), axis=1).T.astype(F32)
    h_pad = order.run(
        lambda x, g: normed(x.astype(F32), g).astype(BF16),
        jnp.concatenate([halo, x_low]),
        gain_one,
    )
    h_one = h_pad[HALO:]
    two.next()
    padded = order.run(lambda h, w: cols_inner(h, w).astype(BF16), h_pad, wide_s)
    mixed, decay, prods, local_state, ends = order.run(
        mix, padded, marks, params, wide_gates
    )
    enter = Entering(order, ends, hops, False)
    two.next()
    two.settle()
    enter.next()
    incoming = enter.finish()
    two.next()
    hid_g = order.arrive(hid_g)
    two.finish()
    dy = Gather(ring, order, cotangent)
    dy.start()
    wide_b, wide_o = order.run(
        lambda *_: assemble(ring, (shard, shard), two), two.theirs[-1][0]
    )
    dy.next()

    def merge(h, w, local, p, inc):
        pre = cols_inner(h, w)
        return pre, ((local + p * inc) * gelu_tanh(pre)).astype(BF16)

    branch_pre, merged = order.run(merge, h_one, wide_b, local_state, prods, incoming)

    def mix_out(m, w, at):
        return jnp.dot(
            lax.dynamic_slice_in_dim(m, at, rows, 0), w, preferred_element_type=F32
        )

    mix_theirs = order.run(lambda m, w: mix_out(m, w, theirs_at).astype(BF16), merged, wide_o)
    mix_got = tensor_swap(mix_theirs)
    mix_mine = order.run(lambda m, w: mix_out(m, w, mine_at), merged, wide_o)
    dy.next()
    x_val = block_input.astype(F32)
    x_one = order.run(lambda x, m, t: x + m + t.astype(F32), x_val, mix_mine, mix_got)
    n_two, norm_two_back = jax.vjp(normed, x_one, gain_two)
    h_own = n_two.astype(BF16)

    ff = Gather(ring, order, h_own)
    ff.start()
    acts, d_gates, d_ups, d_hs, h_list, dy_list = [], [], [], [], [], []

    def do_piece(hs, dys, cuts):
        count = len(hs)
        out = order.run(
            lambda *v: piece(v[:count], v[count : 2 * count], cuts, *v[2 * count :]),
            *hs,
            *dys,
            hid_g,
            hid_u,
            hid_d,
        )
        for kept, value in zip((acts, d_gates, d_ups), out):
            kept.append(value)
        d_hs.extend(out[3:])
        h_list.extend(hs)
        dy_list.extend(dys)

    def plain_piece(h_piece, dy_piece, w_g, w_u, w_d):
        gate_pre = cols_inner(h_piece, w_g)
        up_val = cols_inner(h_piece, w_u)
        gate_act, slope = gelu_and_slope(gate_pre)
        act = (gate_act * up_val).astype(BF16)
        d_act = cols_inner(dy_piece, w_d)
        d_gate = (d_act * up_val * slope).astype(BF16)
        d_up = (d_act * gate_act).astype(BF16)
        d_h = jnp.dot(d_gate, w_g, preferred_element_type=F32) + jnp.dot(
            d_up, w_u, preferred_element_type=F32
        )
        return act, d_gate, d_up, d_h.astype(BF16)

    def do_plain(hs, dys):
        h_piece, dy_piece = jnp.concatenate(hs), jnp.concatenate(dys)
        out = order.run(plain_piece, h_piece, dy_piece, hid_g, hid_u, hid_d)
        for kept, value in zip((acts, d_gates, d_ups, h_list, dy_list), (*out[:3], h_piece, dy_piece)):
            kept.append(value)
        parts = [out[3]]
        if h_piece.shape[0] > rows:
            parts = [out[3][:rows], out[3][rows:]]
        d_hs.extend(parts)

    do_piece((h_own,), (cotangent,), (rows,))
    dy.next()
    for step in range(ring.reach - SHOWN, ring.reach - 1):
        ff.next()
        if step == ring.reach - SHOWN:
            first = 0
        else:
            first = step
        if step == ring.reach - 3:
            dy.finish()
        for k in range(first, step + 1):
            do_plain(ff.pairs[k], dy.pairs[k])
    ff.finish()
    do_plain(ff.far, dy.far)

    def chunks(parts):
        out = plain_parts(parts[:1])
        for pair in parts[1:-1]:
            out += [Part(lambda v: v[:rows].astype(F32), pair)]
            out += [Part(lambda v: v[rows:].astype(F32), pair)]
        return out + plain_parts(parts[-1:])

    back = Scatter(ring, order, plain_parts(d_hs), rows // 2)
    back.start()
    def run_grad(which, into, lefts, rights):
        count, every = len(lefts), len(lefts) + len(rights)
        more = () if into is None else (into,)
        return order.run(
            lambda *v: hidden_grad(
                which, v[every] if more else None, v[:count], v[count:every]
            ),
            *lefts,
            *rights,
            *more,
        )

    back.next()
    downs = order.run(lambda *v: hidden_down(v[:-1], v[-1]), *acts, hid_d)
    back.next()
    hid_grads = run_grad(0, None, d_gates, h_list)
    back.next()
    hid_grads = run_grad(1, hid_grads, d_ups, h_list)

    def dense_back(d_h, dy_own):
        d_x, g_gain = norm_two_back(d_h)
        d_x = dy_own.astype(F32) + d_x
        return d_x, g_gain, d_x.astype(BF16)

    d_x_one, g_gain_two, dz_own = back.finish(dense_back, cotangent)
    dz_other = tensor_swap(dz_own)
    down = Scatter(ring, order, chunks(downs), rows // 2)
    down.start()
    hid_grads = run_grad(2, hid_grads, acts, dy_list)
    hid_grads = holders_sum(hid_grads.reshape(-1, width))
    down.next()
    d_mix = order.run(functools.partial(ordered, side), dz_own, dz_other)
    d_branch, rev_prods, rev_state, back_ends = order.run(
        back_scan, d_mix, wide_o, branch_pre, decay, prods, local_state, incoming
    )
    leave = Entering(order, back_ends, hops, True)
    down.next()
    mine_two, theirs_two = order.run(
        lambda *v: ring_grads(ring, shard, v[:2], v[2:]), d_branch, merged, h_one, d_mix
    )
    theirs_two = core_swap(theirs_two)
    down.next()
    leave.next()
    later = leave.finish()
    d_sig, sig_tail, rim, sums, g_gates = order.run(
        back_mix,
        rev_prods,
        rev_state,
        later,
        prods,
        local_state,
        incoming,
        mixed,
        padded,
        marks,
        params,
        wide_gates,
    )
    rim = from_behind(rim, -1)
    ring_two = Scatter(ring, order, ring_parts(mine_two, theirs_two), shard)
    ring_two.start()
    block_output = down.finish(lambda d, x: (x + d).astype(BF16), x_one)

    def with_rim(sig, tail, edge):
        tail = tail + edge * tail_keep[HALO - 8 :].astype(F32)
        return lax.dynamic_update_slice(sig, tail.astype(BF16), (group - 8, 0))

    d_signal = order.run(with_rim, d_sig, sig_tail, rim)

    def d_h_rows(branch, signal, w_b, w_s, at):
        return jnp.dot(
            lax.dynamic_slice_in_dim(branch, at, rows, 0), w_b, preferred_element_type=F32
        ) + jnp.dot(
            lax.dynamic_slice_in_dim(signal, at, rows, 0), w_s, preferred_element_type=F32
        )

    d_h_theirs = order.run(
        functools.partial(d_h_rows, at=theirs_at), d_branch, d_signal, wide_b, wide_s
    )
    d_h_got = tensor_swap(d_h_theirs.astype(BF16))
    ring_two.next()

    mine_last, theirs_last = order.run(
        lambda a, b, g: ring_grads(ring, shard, (a,), (b,), g), d_signal, h_one, g_gates
    )
    theirs_last = core_swap(theirs_last)
    d_h_mine = order.run(
        functools.partial(d_h_rows, at=mine_at), d_branch, d_signal, wide_b, wide_s
    )

    def gain_sum(mine, theirs, x, other, g_two):
        def unit(v):
            v = v.astype(F32)
            return v * lax.rsqrt(jnp.mean(v * v, axis=-1, keepdims=True) + EPS)

        return jnp.stack([jnp.sum(mine * unit(x) + theirs * unit(other), axis=0), g_two])

    gains = order.run(gain_sum, d_h_mine, d_h_theirs, block_input, x_other, g_gain_two)
    gains_other = tensor_swap(gains)
    ring_two.next()

    n_rows = shard * (CONV + 1) + 2 * n_gain

    def small_rows(total, gain, gain_other):
        gain = gain + gain_other
        return jnp.concatenate(
            [
                total[:CONV].T.reshape(count, shard * CONV),
                total[CONV].reshape(count, shard),
                gain[0].reshape(count, n_gain),
                gain[1].reshape(count, n_gain),
            ],
            axis=1,
        )

    smalls = order.run(small_rows, sums, gains, gains_other)
    smalls_other = core_swap(smalls)
    smalls = order.run(
        lambda a, b: jnp.pad(a + b, ((0, 0), (0, width - n_rows))), smalls, smalls_other
    )

    def last_part(k, distance):
        at = 2 * ring.chip_at(distance) + ring.core

        def cut(a, b, small):
            big = a[k].astype(F32) + b[k].astype(F32)
            return jnp.concatenate([big, lax.dynamic_slice_in_dim(small, at, 1, 0)])

        return Part(cut, mine_last, theirs_last, smalls)

    ring_last = Scatter(
        ring,
        order,
        [last_part(k, distance) for k, distance in enumerate(ring_distances(ring))],
        (shard + n_gate) // 32 * 16 or shard // 2,
    )
    grad_input = order.run(
        input_back, block_input, d_h_mine, d_h_got, d_x_one, gain_one[None, :]
    )
    def land_both():
        flight = order.arrive(*ring_two.flight, *ring_last.flight)
        ring_two.flight, ring_last.flight = flight[:2], flight[2:]

    ring_last.start()
    land_both()
    ring_two.next()
    ring_last.next()
    land_both()
    ring_last.next()
    total_two = ring_two.finish()
    s_branch = total_two[:shard].T
    s_mixout = total_two[shard:]
    ring_last.next()
    s_gate, s_up, s_down = order.run(lambda g: widen(g, 3), hid_grads)
    s_gate, s_up = s_gate.T, s_up.T
    last = ring_last.finish()
    s_signal = last[:shard].T
    s_gates = [
        jnp.swapaxes(v.reshape(n_gate, heads_here, BLOCK), 0, 1)
        for v in jnp.split(last[shard : shard + n_gate], 2, axis=1)
    ]
    s_small = last[shard + n_gate]
    s_taps = s_small[: shard * CONV].reshape(shard, CONV)
    s_param = s_small[shard * CONV : shard * (CONV + 1)]
    s_gain_one = s_small[n_rows - 2 * n_gain : n_rows - n_gain]
    s_gain_two = s_small[n_rows - n_gain : n_rows]
    return (
        block_output,
        grad_input,
        s_gain_one,
        s_branch,
        s_signal,
        s_gates[0],
        s_gates[1],
        s_taps,
        s_param,
        s_mixout,
        s_gain_two,
        s_gate,
        s_up,
        s_down,
    )


def solution(mesh):
    placed = (
        P(("dp", "tensor"), None),
        P("dp"),
        P(("dp", "tensor"), None),
        P("dp"),
        P(None, ("tensor", "dp")),
        P(None, ("tensor", "dp")),
        P("tensor", "dp", None),
        P("tensor", "dp", None),
        P(("tensor", "dp"), None),
        P(("tensor", "dp")),
        P(("tensor", "dp"), None),
        P("dp"),
        P(None, ("tensor", "dp")),
        P(None, ("tensor", "dp")),
        P(("tensor", "dp"), None),
    )
    return jax.shard_map(
        per_device,
        mesh=mesh,
        in_specs=placed,
        out_specs=(
            P(("dp", "tensor"), None),
            P(("dp", "tensor"), None),
            P("dp"),
            P(None, ("tensor", "dp")),
            P(None, ("tensor", "dp")),
            P("tensor", "dp", None),
            P("tensor", "dp", None),
            P(("tensor", "dp"), None),
            P(("tensor", "dp")),
            P(("tensor", "dp"), None),
            P("dp"),
            P(None, ("tensor", "dp")),
            P(None, ("tensor", "dp")),
            P(("tensor", "dp"), None),
        ),
        check_vma=False,
    )
```

```python
import functools

import jax
import jax.numpy as jnp
from jax import lax
from jax.experimental import pallas as pl
from jax.experimental.pallas import tpu as pltpu
from jax.sharding import PartitionSpec as P

BLOCK = 256
CONV = 4
MAXLEN = 1024
EPS = 1e-06
HALO = 16
BF16 = jnp.bfloat16
F32 = jnp.float32


def ring_order(chips):
    return list(range(0, chips, 2)) + list(range(chips - 1, 0, -2))


class Ring:
    def __init__(self):
        count = lax.axis_size("dp")
        self.chips = count // 2
        self.reach = self.chips // 2
        order = ring_order(self.chips)
        self.up_route = [
            (order[p] * 2 + c, order[(p + 1) % self.chips] * 2 + c)
            for p in range(self.chips)
            for c in range(2)
        ]
        self.down_route = [(b, a) for a, b in self.up_route]
        me = lax.axis_index("dp")
        chip = me // 2
        self.core = lax.rem(me, 2)
        self.place = jnp.where(
            lax.rem(chip, 2) == 0, chip // 2, self.chips - 1 - chip // 2
        )

    def chip_at(self, distance):
        p = lax.rem(self.place - distance + self.chips, self.chips)
        return jnp.where(p < self.reach, 2 * p, 2 * (self.chips - 1 - p) + 1)

    def up(self, value):
        return lax.ppermute(value, "dp", self.up_route)

    def down(self, value):
        return lax.ppermute(value, "dp", self.down_route)


class Order:
    def __init__(self):
        self.token = None

    def tie(self, *values):
        if self.token is not None:
            values = lax.optimization_barrier((values, self.token))[0]
        return values if len(values) > 1 else values[0]

    def arrive(self, *values):
        values = lax.optimization_barrier((values, self.token))[0]
        self.token = values[-1]
        return values if len(values) > 1 else values[0]

    def run(self, function, *values):
        values = self.tie(*values)
        out = function(*values) if isinstance(values, tuple) else function(values)
        self.token = tuple(jax.tree.leaves(out))
        return out


SHOWN = 4


class Gather:
    def __init__(self, ring, order, value, both_cores=False):
        self.ring, self.order = ring, order
        self.own = value
        self.half = value.shape[0] // 32 * 16 or value.shape[0] // 2
        self.flight = (value, value)
        self.pairs, self.far = [], None
        self.theirs = [] if both_cores else None
        self.settled = False
        self.steps = 0

    def start(self):
        self.send()
        self.swap(self.own)
        for _ in range(self.ring.reach - SHOWN):
            self.next()

    def swap(self, *values):
        if self.theirs is not None:
            self.theirs.append(tuple(core_swap(v) for v in values))

    def send(self):
        self.steps += 1
        u, d = self.order.tie(*self.flight)
        if self.steps == self.ring.reach:
            u, d = u[: self.half], d[self.half :]
        self.flight = (self.ring.up(u), self.ring.down(d))

    def land(self):
        swapped = self.theirs.pop() if self.theirs and not self.settled else ()
        self.settled = False
        landed = self.order.arrive(*swapped, *self.flight)
        self.flight = landed[len(swapped) :]
        if swapped:
            self.theirs.append(landed[: len(swapped)])

    def next(self):
        self.land()
        landed = self.flight
        self.pairs.append(landed)
        self.send()
        self.swap(*landed)

    def settle(self):
        swapped = self.order.arrive(*self.theirs.pop())
        self.theirs.append(swapped)
        self.settled = True

    def finish(self):
        self.land()
        self.far = self.flight
        self.swap(*self.far)


class Scatter:
    def __init__(self, ring, order, parts, half):
        self.ring, self.order = ring, order
        self.parts, self.half = list(parts), half
        self.steps = 0

    def start(self):
        far = self.parts.pop()
        self.flight = self.order.run(
            lambda *v: (far(v, 0, self.half), far(v, self.half, None)), *far.values
        )
        self.send()
        for _ in range(self.ring.reach - SHOWN):
            self.next()

    def send(self):
        self.steps += 1
        u, d = self.order.tie(*self.flight)
        self.flight = (self.ring.down(u), self.ring.up(d))

    def next(self):
        ahead, behind = self.parts.pop(), self.parts.pop()
        half, first = self.half, self.steps == 1

        self.steps += 1
        to_down, to_up = self.flight

        def add_up(got, *values):
            if first:
                return jnp.concatenate(
                    [ahead(values, 0, half), ahead(values, half, None, got)]
                )
            return ahead(values, 0, None, got)

        def add_down(got, *values):
            if first:
                return jnp.concatenate(
                    [behind(values, 0, half, got), behind(values, half, None)]
                )
            return behind(values, 0, None, got)

        up = self.ring.up(self.order.run(add_up, to_up, *ahead.values))
        down = self.ring.down(self.order.run(add_down, to_down, *behind.values))
        self.flight = (down, up)

    def finish(self, function=None, *more):
        own = self.parts.pop()

        def total(to_down, to_up, *values):
            count = len(own.values)
            out = own(values[:count], 0, None, to_down, to_up, F32)
            return function(out, *values[count:]) if function else out

        return self.order.run(total, *self.flight, *own.values, *more)


class Part:
    def __init__(self, cut, *values):
        self.cut, self.values = cut, values

    def __call__(self, values, first, last, *others):
        dtype = BF16
        if others and others[-1] is F32:
            others, dtype = others[:-1], F32
        total = self.cut(*values)[first:last]
        for other in others:
            total = total + other.astype(F32)
        return total.astype(dtype)


def plain_parts(values):
    return [Part(lambda v: v.astype(F32), value) for value in values]


def plus(a, b):
    return (a.astype(F32) + b.astype(F32)).astype(BF16)


def core_swap(value):
    count = lax.axis_size("dp")
    return lax.ppermute(value, "dp", [(i, i ^ 1) for i in range(count)])


def holder_groups():
    return [
        [(2 * chip + core) * 2 + side for core in range(2) for side in range(2)]
        for chip in range(lax.axis_size("dp") // 2)
    ]


def holders_gather(value):
    return lax.all_gather(
        value, ("dp", "tensor"), axis=0, tiled=True, axis_index_groups=holder_groups()
    )


def holders_sum(value):
    return lax.psum_scatter(
        value,
        ("dp", "tensor"),
        scatter_dimension=0,
        tiled=True,
        axis_index_groups=holder_groups(),
    )


def tensor_swap(value):
    return lax.ppermute(value, "tensor", [(0, 1), (1, 0)])


def from_behind(block, distance):
    devices = range(lax.axis_size("dp"))
    route = [(i - distance, i) for i in devices if i - distance in devices]
    return lax.ppermute(block, "dp", route)


class Entering:
    def __init__(self, order, window, hops, reverse):
        self.order, self.sign = order, (-1 if reverse else 1)
        size = 1
        while 4 * size < hops:
            window = follow(from_behind(window, self.sign * size), window)
            size *= 2
        self.size, self.hops, self.window = size, hops, window
        if size < hops:
            self.behind = from_behind(window, self.sign * size)

    def next(self):
        if 2 * self.size < self.hops:
            self.window = self.order.run(follow, self.behind, self.window)
            self.size *= 2
        self.near = from_behind(self.window, self.sign)
        if self.size < self.hops:
            self.rest = from_behind(self.window, self.sign * (1 + self.size))

    def finish(self):
        if self.size >= self.hops:
            return self.order.arrive(self.near)[1:]
        return self.order.run(lambda n, r: n[:1] * r[1:] + n[1:], self.near, self.rest)


def follow(first, second):
    return jnp.stack([first[0] * second[0], second[0] * first[1] + second[1]])


def normed(value, gain):
    return value * lax.rsqrt(jnp.mean(value * value, axis=-1, keepdims=True) + EPS) * gain


def gelu_tanh(value):
    return jax.nn.gelu(value, approximate=True)


GELU_IN = 0.7978845608028654
GELU_CUBE = 0.044715


def gelu_and_slope(value):
    square = value * value
    t = jnp.tanh(GELU_IN * (value + GELU_CUBE * (square * value)))
    half = 0.5 * (1.0 + t)
    slope = half + 0.5 * value * (1.0 - t * t) * (GELU_IN * (1.0 + 3.0 * GELU_CUBE * square))
    return value * half, slope


def rows_inner(left, right):
    return lax.dot_general(
        left, right, (((0,), (0,)), ((), ())), preferred_element_type=F32
    )


def cols_inner(left, right):
    return lax.dot_general(
        left, right, (((1,), (1,)), ((), ())), preferred_element_type=F32
    )


def scan_rows(reverse, a_ref, b_ref, p_ref, s_ref):
    rows, width = a_ref.shape
    blocks = rows // 8
    row = lax.broadcasted_iota(jnp.int32, (8, width), 0)

    def step(i, carry):
        p_in, s_in = carry
        at = (blocks - 1 - i) if reverse else i
        here = pl.ds(pl.multiple_of(at * 8, 8), 8)
        a = a_ref[here, :]
        b = b_ref[here, :]
        for shift in (1, 2, 4):
            turn = 8 - shift if reverse else shift
            inside = (row < 8 - shift) if reverse else (row >= shift)
            a_prev = jnp.where(inside, pltpu.roll(a, turn, 0), 1.0)
            b_prev = jnp.where(inside, pltpu.roll(b, turn, 0), 0.0)
            b = a * b_prev + b
            a = a * a_prev
        b = b + a * s_in
        a = a * p_in
        p_ref[here, :] = a
        s_ref[here, :] = b
        last = 0 if reverse else 7
        return (a[last : last + 1], b[last : last + 1])

    return lax.fori_loop(
        0, blocks, step, (jnp.ones((1, width), F32), jnp.zeros((1, width), F32))
    )


def lru_gates(mixed, w_ig, w_dg, param):
    gx_pre = jnp.dot(mixed, w_ig, preferred_element_type=F32)
    ga_pre = jnp.dot(mixed, w_dg, preferred_element_type=F32)
    return jax.nn.sigmoid(gx_pre), jax.nn.sigmoid(ga_pre), jax.nn.softplus(param)


def one_minus_square(log_a, e):
    x = 2.0 * log_a
    series = -x * (
        1.0 + x * (1 / 2 + x * (1 / 6 + x * (1 / 24 + x * (1 / 120 + x * (1 / 720)))))
    )
    return jnp.where(x > -0.3, series, 1.0 - e * e)


def mix_body(pad_ref, marks_ref, params_ref, ig_ref, dg_ref, *refs):
    mixed_ref, decay_ref, prods_ref, state_ref, ends_ref, a_scr, b_scr = refs
    block = pl.program_id(0)
    rows = mixed_ref.shape[0]
    pad = pad_ref[...].astype(F32)
    total = params_ref[0:1, :] * pad[HALO:] * marks_ref[:, 0:1]
    for k in range(1, CONV):
        behind = pltpu.roll(pad, k, 0)[HALO:]
        total = total + params_ref[k : k + 1, :] * behind * marks_ref[:, k : k + 1]
    mixed = total.astype(BF16)
    mixed_ref[...] = mixed
    gate_x, gate_a, soft = lru_gates(mixed, ig_ref[...], dg_ref[...], params_ref[CONV : CONV + 1, :])
    reset = marks_ref[:, CONV : CONV + 1]
    keep = 1.0 - reset
    log_a = -8.0 * gate_a * soft
    e = jnp.exp(log_a)
    decay = e * keep
    multiplier = jnp.sqrt(one_minus_square(log_a, e)) * keep + reset
    decay_ref[...] = decay
    here = pl.ds(pl.multiple_of(block * BLOCK, BLOCK), BLOCK)
    a_scr[:, here] = decay
    b_scr[:, here] = gate_x * mixed.astype(F32) * multiplier

    @pl.when(block == pl.num_programs(0) - 1)
    def _():
        p_end, s_end = scan_rows(False, a_scr, b_scr, prods_ref, state_ref)
        ends_ref[0:1, :] = p_end
        ends_ref[1:2, :] = s_end


def back_scan_body(dz_ref, wide_ref, pre_ref, decay_ref, prods_ref, state_ref, in_ref, *refs):
    branch_ref, rev_p_ref, rev_s_ref, ends_ref, a_scr, b_scr, first_scr = refs
    block = pl.program_id(0)
    rows = pre_ref.shape[0]
    d_merged = lax.dot_general(
        dz_ref[...], wide_ref[...], (((1,), (1,)), ((), ())), preferred_element_type=F32
    )
    branch, slope = gelu_and_slope(pre_ref[...])
    state = state_ref[...] + prods_ref[...] * in_ref[...]
    branch_ref[...] = (d_merged * state * slope).astype(BF16)
    decay = decay_ref[...]
    row = lax.broadcasted_iota(jnp.int32, decay.shape, 0)
    ahead = jnp.where(row == rows - 1, 1.0, pltpu.roll(decay, rows - 1, 0))
    here = pl.ds(pl.multiple_of(block * BLOCK, BLOCK), BLOCK)
    a_scr[:, here] = ahead
    b_scr[:, here] = d_merged * branch
    first_scr[:, here] = decay[0:8]

    @pl.when(block == pl.num_programs(0) - 1)
    def _():
        p_end, s_end = scan_rows(True, a_scr, b_scr, rev_p_ref, rev_s_ref)
        first = first_scr[0:1, :]
        ends_ref[0:1, :] = first * p_end
        ends_ref[1:2, :] = first * s_end


def back_mix_body(*refs):
    (rev_p_ref, rev_s_ref, later_ref, prods_ref, state_ref, in_ref) = refs[:6]
    (mixed_ref, pad_ref, marks_ref, params_ref, ig_ref, dg_ref) = refs[6:12]
    sig_ref, tail_ref, rim_ref, sums_ref, gates_ref = refs[12:]
    rows = mixed_ref.shape[0]
    g = rev_s_ref[...] + rev_p_ref[...] * later_ref[...]
    entering_row = in_ref[...]
    state = state_ref[...] + prods_ref[...] * entering_row
    row = lax.broadcasted_iota(jnp.int32, state.shape, 0)
    previous = jnp.where(row == 0, entering_row, pltpu.roll(state, 1, 0))
    mixed = mixed_ref[...]
    mixed_f = mixed.astype(F32)
    param = params_ref[CONV : CONV + 1, :]
    gate_x, gate_a, soft = lru_gates(mixed, ig_ref[...], dg_ref[...], param)
    reset = marks_ref[:, CONV : CONV + 1]
    keep = 1.0 - reset
    log_a = -8.0 * gate_a * soft
    e = jnp.exp(log_a)
    root = jnp.sqrt(one_minus_square(log_a, e))
    multiplier = root * keep + reset
    d_multiplier = g * gate_x * mixed_f
    d_log_a = keep * (g * previous * e - d_multiplier * (e * e) / root)
    d_gate_a = d_log_a * (-8.0 * soft)
    d_param = jnp.sum(d_log_a * (-8.0 * gate_a), axis=0, keepdims=True) * jax.nn.sigmoid(param)
    d_ga = (d_gate_a * gate_a * (1.0 - gate_a)).astype(BF16)
    d_gx = (g * mixed_f * multiplier * gate_x * (1.0 - gate_x)).astype(BF16)
    for half, d_pre in enumerate((d_gx, d_ga)):
        at = (half * pl.num_programs(0) + pl.program_id(0)) * BLOCK
        gates_ref[:, pl.ds(pl.multiple_of(at, BLOCK), BLOCK)] = lax.dot_general(
            mixed, d_pre, (((0,), (0,)), ((), ())), preferred_element_type=F32
        ).astype(BF16)
    d_mixed = (
        g * gate_x * multiplier
        + lax.dot_general(d_gx, ig_ref[...], (((1,), (1,)), ((), ())), preferred_element_type=F32)
        + lax.dot_general(d_ga, dg_ref[...], (((1,), (1,)), ((), ())), preferred_element_type=F32)
    )
    pad = pad_ref[...].astype(F32)
    front = jnp.zeros((HALO, BLOCK), F32)
    d_pad = None
    for k in range(CONV):
        masked = d_mixed * marks_ref[:, k : k + 1]
        behind = pad if k == 0 else pltpu.roll(pad, k, 0)
        sums_ref[k : k + 1, :] = jnp.sum(masked * behind[HALO:], axis=0, keepdims=True)
        term = jnp.concatenate([front, masked * params_ref[k : k + 1, :]])
        if k:
            term = pltpu.roll(term, rows + HALO - k, 0)
        d_pad = term if d_pad is None else d_pad + term
    sums_ref[CONV : CONV + 1, :] = d_param
    sums_ref[CONV + 1 : 8, :] = jnp.zeros((8 - CONV - 1, BLOCK), F32)
    rim_ref[...] = d_pad[HALO - 8 : HALO]
    sig_ref[...] = d_pad[HALO:].astype(BF16)
    tail_ref[...] = d_pad[HALO + rows - 8 :]


def rows_spec(rows):
    return pl.BlockSpec((rows, BLOCK), lambda h: (0, h))


def whole_spec(*shape):
    return pl.BlockSpec(shape, lambda h: (0,) * len(shape))


def gate_specs(heads):
    return [
        pl.BlockSpec((BLOCK, BLOCK), lambda h: (0, h)),
        pl.BlockSpec((BLOCK, BLOCK), lambda h: (0, heads + h)),
    ]


BIG = pltpu.CompilerParams(vmem_limit_bytes=48 << 20)
LIGHT = pl.CostEstimate(flops=0, bytes_accessed=0, transcendentals=0)
HEAVY = pl.CostEstimate(flops=500_000_000_000, bytes_accessed=0, transcendentals=0)


def shaped(rows, width, dtype=F32):
    return jax.ShapeDtypeStruct((rows, width), dtype)


def mix(padded, marks, params, w_gates):
    rows, width = padded.shape[0] - HALO, padded.shape[1]
    return pl.pallas_call(
        mix_body,
        grid=(width // BLOCK,),
        in_specs=[
            rows_spec(rows + HALO),
            whole_spec(rows, 8),
            rows_spec(8),
            *gate_specs(width // BLOCK),
        ],
        out_specs=[
            rows_spec(rows),
            rows_spec(rows),
            whole_spec(rows, width),
            whole_spec(rows, width),
            whole_spec(2, width),
        ],
        out_shape=[
            shaped(rows, width, BF16),
            shaped(rows, width),
            shaped(rows, width),
            shaped(rows, width),
            shaped(2, width),
        ],
        scratch_shapes=[pltpu.VMEM((rows, width), F32)] * 2,
        cost_estimate=LIGHT,
        compiler_params=BIG,
    )(padded, marks, params, w_gates, w_gates)


def back_scan(dz, wide, pre, decay, prods, state, incoming):
    rows, width = pre.shape
    depth = dz.shape[1]
    return pl.pallas_call(
        back_scan_body,
        grid=(width // BLOCK,),
        in_specs=[
            whole_spec(rows, depth),
            pl.BlockSpec((BLOCK, depth), lambda h: (h, 0)),
            rows_spec(rows),
            rows_spec(rows),
            rows_spec(rows),
            rows_spec(rows),
            rows_spec(1),
        ],
        out_specs=[
            rows_spec(rows),
            whole_spec(rows, width),
            whole_spec(rows, width),
            whole_spec(2, width),
        ],
        out_shape=[
            shaped(rows, width, BF16),
            shaped(rows, width),
            shaped(rows, width),
            shaped(2, width),
        ],
        scratch_shapes=[
            pltpu.VMEM((rows, width), F32),
            pltpu.VMEM((rows, width), F32),
            pltpu.VMEM((8, width), F32),
        ],
        cost_estimate=LIGHT,
        compiler_params=BIG,
    )(dz, wide, pre, decay, prods, state, incoming)


def back_mix(rev_p, rev_s, later, prods, state, incoming, mixed, padded, marks, params, w_gates):
    rows, width = mixed.shape
    heads = width // BLOCK
    return pl.pallas_call(
        back_mix_body,
        grid=(heads,),
        in_specs=[
            rows_spec(rows),
            rows_spec(rows),
            rows_spec(1),
            rows_spec(rows),
            rows_spec(rows),
            rows_spec(1),
            rows_spec(rows),
            rows_spec(rows + HALO),
            whole_spec(rows, 8),
            rows_spec(8),
            *gate_specs(heads),
        ],
        out_specs=[
            rows_spec(rows),
            rows_spec(8),
            rows_spec(8),
            rows_spec(8),
            whole_spec(BLOCK, 2 * width),
        ],
        out_shape=[
            shaped(rows, width, BF16),
            shaped(8, width),
            shaped(8, width),
            shaped(8, width),
            shaped(BLOCK, 2 * width, BF16),
        ],
        cost_estimate=HEAVY,
        compiler_params=BIG,
    )(rev_p, rev_s, later, prods, state, incoming, mixed, padded, marks, params, w_gates, w_gates)


def assemble_body(sizes, runs, places, at_ref, *refs):
    chunks = refs[: len(runs)]
    outs, (scratch, in_sems, out_sems) = refs[-3 - len(sizes) : -3], refs[-3:]
    loads = [
        pltpu.make_async_copy(
            chunk, scratch.at[slot, pl.ds(first, rows)], in_sems.at[i]
        )
        for i, (chunk, (slot, first, rows)) in enumerate(zip(chunks, runs))
    ]
    for load in loads:
        load.start()
    stores = []
    for slot in range(places):
        for load, run in zip(loads, runs):
            if run[0] == slot:
                load.wait()
        base = 0
        for out, size in zip(outs, sizes):
            target = pl.ds(pl.multiple_of(at_ref[slot] * size, 16), size)
            stores.append(
                pltpu.make_async_copy(
                    scratch.at[slot, pl.ds(base, size)],
                    out.at[target],
                    out_sems.at[len(stores)],
                )
            )
            stores[-1].start()
            base += size
    for store in stores:
        store.wait()


def assemble_whole(ring, sizes, gathered):
    return assemble(ring, sizes, gathered, None, 0, 2 * ring.chips)


def assemble(ring, sizes, gathered, into, low, high):
    near = [(gathered.own,)] + [(v,) for pair in gathered.pairs for v in pair]
    their = [gathered.theirs[0]]
    for pair in gathered.theirs[1 : ring.reach]:
        their += [(v,) for v in pair]
    if gathered.far is not None:
        near.append(gathered.far)
        their.append(gathered.theirs[-1])
    rows, width = gathered.own.shape
    slots = []
    for distance, mine, theirs in zip(ring_distances(ring), near, their):
        chip = ring.chip_at(distance)
        slots += [(2 * chip + ring.core, mine), (2 * chip + 1 - ring.core, theirs)]
    if any(size % 16 for size in sizes):
        if high < 2 * ring.chips:
            return list(slots[0][1])
        at = jnp.stack([place for place, _ in slots]).astype(jnp.int32)
        every = jnp.stack([jnp.concatenate(v) if len(v) > 1 else v[0] for _, v in slots])
        every = jnp.zeros_like(every).at[at].set(every)
        cuts = [sum(sizes[:i]) for i in range(len(sizes) + 1)]
        return [every[:, a:b].reshape(-1, width) for a, b in zip(cuts, cuts[1:])]
    slots = slots[low:high]
    at = jnp.stack([place for place, _ in slots]).astype(jnp.int32)
    places = len(slots)
    chunks, runs = [], []
    for slot, (_, values) in enumerate(slots):
        first = 0
        for value in values:
            chunks.append(value)
            runs.append((slot, first, value.shape[0]))
            first += value.shape[0]
    anywhere = pl.BlockSpec(memory_space=pl.ANY)
    more = [] if into is None else list(into)
    return pl.pallas_call(
        functools.partial(assemble_body, sizes, runs, places),
        out_shape=[shaped(2 * ring.chips * size, width, BF16) for size in sizes],
        in_specs=[pl.BlockSpec(memory_space=pltpu.SMEM)]
        + [anywhere] * (len(chunks) + len(more)),
        out_specs=[anywhere] * len(sizes),
        input_output_aliases={1 + len(chunks) + i: i for i in range(len(more))},
        scratch_shapes=[
            pltpu.VMEM((places, rows, width), BF16),
            pltpu.SemaphoreType.DMA((len(chunks),)),
            pltpu.SemaphoreType.DMA((places * len(sizes),)),
        ],
        cost_estimate=LIGHT,
        compiler_params=BIG,
    )(at, *chunks, *more)


def ring_distances(ring):
    out = [0]
    for k in range(1, ring.reach):
        out += [k, -k]
    return out + [ring.reach]


def ring_grads_body(shard, chips, pairs, extra, at_ref, *refs):
    lefts, rights = refs[:pairs], refs[pairs : 2 * pairs]
    rest = refs[2 * pairs :]
    if extra:
        extra_ref, rest = rest[0], rest[1:]
    mine_ref, theirs_ref, turned, full, sems = rest
    core = at_ref[chips]
    width = full.shape[2]
    copies = []

    def send(source, size, base):
        for slot in range(chips):
            for out, c in ((mine_ref, core), (theirs_ref, 1 - core)):
                first = pl.multiple_of((2 * at_ref[slot] + c) * size, 16)
                copies.append(
                    pltpu.make_async_copy(
                        source.at[pl.ds(first, size)],
                        out.at[slot, pl.ds(base, size)],
                        sems.at[len(copies)],
                    )
                )
                copies[-1].start()

    if extra:
        send(extra_ref, extra, pairs * shard)
    for pair in range(pairs):
        turned[...] = lefts[pair][...].astype(F32).T.astype(BF16)

        def column(n, _):
            here = pl.ds(pl.multiple_of(n * BLOCK, BLOCK), BLOCK)
            full[pair, :, here] = jnp.dot(
                turned[...], rights[pair][:, here], preferred_element_type=F32
            ).astype(BF16)
            return 0

        lax.fori_loop(0, width // BLOCK, column, 0)
        send(full.at[pair], shard, pair * shard)
    for copy in copies:
        copy.wait()


def ring_grads(ring, shard, lefts, rights, extra=None):
    pairs, chips = len(lefts), ring.chips
    rows, channels = lefts[0].shape
    width = rights[0].shape[1]
    more = 0 if extra is None else extra.shape[0] // (2 * chips)
    at = [ring.chip_at(distance) for distance in ring_distances(ring)]
    if shard % 16 or more % 16:
        values = [rows_inner(a, b).astype(BF16) for a, b in zip(lefts, rights)]
        values += [] if extra is None else [extra]
        values = jnp.concatenate([v.reshape(chips, 2, -1, width) for v in values], axis=2)
        values = values[jnp.stack(at)]
        return (
            lax.dynamic_index_in_dim(values, ring.core, 1, False),
            lax.dynamic_index_in_dim(values, 1 - ring.core, 1, False),
        )
    in_vmem = pl.BlockSpec(memory_space=pltpu.VMEM)
    anywhere = pl.BlockSpec(memory_space=pl.ANY)
    out = jax.ShapeDtypeStruct((chips, pairs * shard + more, width), BF16)
    return pl.pallas_call(
        functools.partial(ring_grads_body, shard, chips, pairs, more),
        out_shape=[out, out],
        in_specs=[pl.BlockSpec(memory_space=pltpu.SMEM)]
        + [in_vmem] * (2 * pairs + (extra is not None)),
        out_specs=[anywhere, anywhere],
        scratch_shapes=[
            pltpu.VMEM((channels, rows), BF16),
            pltpu.VMEM((pairs, channels, width), BF16),
            pltpu.SemaphoreType.DMA((2 * chips * (pairs + (extra is not None)),)),
        ],
        cost_estimate=LIGHT,
        compiler_params=BIG,
    )(
        jnp.stack(at + [ring.core]).astype(jnp.int32),
        *lefts,
        *rights,
        *(() if extra is None else (extra,)),
    )


def hidden_grad_body(heights, right_heights, which, *refs):
    count = len(right_heights)
    lefts, rights = refs[: len(heights)], refs[len(heights) : len(heights) + count]
    out_ref, turned, held, made, in_sems, out_sems = refs[-6:]
    parts, _, columns = held.shape
    holders, _, unit, _ = out_ref.shape
    loads, stores = [], []
    for part in range(parts):
        first = 0
        for i, height in enumerate(right_heights):
            loads.append(
                pltpu.make_async_copy(
                    rights[i].at[:, pl.ds(part * columns, columns)],
                    held.at[part, pl.ds(first, height)],
                    in_sems.at[part * count + i],
                )
            )
            loads[-1].start()
            first += height
    first = 0
    for left, height in zip(lefts, heights):
        turned[:, first : first + height] = left[...].astype(F32).T.astype(BF16)
        first += height
    for part in range(parts):
        for load in loads[part * count : (part + 1) * count]:
            load.wait()

        def column(n, _, part=part):
            here = pl.ds(pl.multiple_of(n * BLOCK, BLOCK), BLOCK)
            made[part, :, here] = jnp.dot(
                turned[...], held[part, :, here], preferred_element_type=F32
            ).astype(BF16)
            return 0

        lax.fori_loop(0, columns // BLOCK, column, 0)
        for holder in range(holders):
            stores.append(
                pltpu.make_async_copy(
                    made.at[part, pl.ds(holder * unit, unit)],
                    out_ref.at[holder, which, :, pl.ds(part * columns, columns)],
                    out_sems.at[part * holders + holder],
                )
            )
            stores[-1].start()
    for store in stores:
        store.wait()


def hidden_grad(which, into, lefts, rights):
    heights = [left.shape[0] for left in lefts]
    right_heights = [right.shape[0] for right in rights]
    depth, width = lefts[0].shape[1], rights[0].shape[1]
    unit = depth // 4
    if unit % 16 or any(height % 128 for height in heights):
        grad = rows_inner(jnp.concatenate(lefts), jnp.concatenate(rights)).astype(BF16)
        grad = grad.reshape(4, 1, unit, width)
        return grad if into is None else jnp.concatenate([into, grad], axis=1)
    parts = 2
    in_vmem = pl.BlockSpec(memory_space=pltpu.VMEM)
    anywhere = pl.BlockSpec(memory_space=pl.ANY)
    more = () if into is None else (into,)
    return pl.pallas_call(
        functools.partial(hidden_grad_body, heights, right_heights, which),
        out_shape=jax.ShapeDtypeStruct((4, 3, unit, width), BF16),
        in_specs=[in_vmem] * len(lefts) + [anywhere] * (len(rights) + len(more)),
        out_specs=anywhere,
        input_output_aliases={len(lefts) + len(rights): 0} if more else {},
        scratch_shapes=[
            pltpu.VMEM((depth, sum(heights)), BF16),
            pltpu.VMEM((parts, sum(heights), width // parts), BF16),
            pltpu.VMEM((parts, depth, width // parts), BF16),
            pltpu.SemaphoreType.DMA((parts * len(rights),)),
            pltpu.SemaphoreType.DMA((parts * 4,)),
        ],
        cost_estimate=LIGHT,
        compiler_params=BIG,
    )(*lefts, *rights, *more)


def piece_body(count, cuts, tiles, *refs):
    ins, dys, weights = refs[:count], refs[count : 2 * count], refs[2 * count : 2 * count + 3]
    act_ref, d_gate_ref, d_up_ref = refs[2 * count + 3 : 2 * count + 6]
    outs = refs[2 * count + 6 : 2 * count + 6 + len(cuts)]
    h, dy, w_g, w_u, w_d, total, row_sems, w_sems = refs[2 * count + 6 + len(cuts) :]
    row_loads, w_loads = [], []
    for to, sources in ((h, ins), (dy, dys)):
        first = 0
        for source in sources:
            size = source.shape[0]
            row_loads.append(
                pltpu.make_async_copy(
                    source, to.at[pl.ds(first, size)], row_sems.at[len(row_loads)]
                )
            )
            row_loads[-1].start()
            first += size
    for low, high in tiles:
        here = pl.ds(low, high - low)
        for source, to in zip(weights, (w_g, w_u, w_d)):
            w_loads.append(
                pltpu.make_async_copy(source.at[here], to.at[here], w_sems.at[len(w_loads)])
            )
            w_loads[-1].start()
    for load in row_loads:
        load.wait()
    for i, (low, high) in enumerate(tiles):
        for load in w_loads[3 * i : 3 * i + 3]:
            load.wait()
        gate_act, slope = gelu_and_slope(cols_inner(h[...], w_g[low:high, :]))
        up_val = cols_inner(h[...], w_u[low:high, :])
        d_act = cols_inner(dy[...], w_d[low:high, :])
        d_gate = (d_act * up_val * slope).astype(BF16)
        d_up = (d_act * gate_act).astype(BF16)
        act_ref[:, low:high] = (gate_act * up_val).astype(BF16)
        d_gate_ref[:, low:high] = d_gate
        d_up_ref[:, low:high] = d_up
        part = jnp.dot(d_gate, w_g[low:high, :], preferred_element_type=F32) + jnp.dot(
            d_up, w_u[low:high, :], preferred_element_type=F32
        )
        total[...] = part if i == 0 else total[...] + part
    first = 0
    for out, size in zip(outs, cuts):
        out[...] = total[first : first + size, :].astype(BF16)
        first += size


def piece(hs, dys, cuts, w_g, w_u, w_d):
    depth, width = w_g.shape
    rows = sum(cuts)
    tiles = [(low, min(low + BLOCK, depth)) for low in range(0, depth, BLOCK)]
    in_vmem = pl.BlockSpec(memory_space=pltpu.VMEM)
    anywhere = pl.BlockSpec(memory_space=pl.ANY)
    return pl.pallas_call(
        functools.partial(piece_body, len(hs), cuts, tiles),
        out_shape=[shaped(rows, depth, BF16)] * 3 + [shaped(cut, width, BF16) for cut in cuts],
        in_specs=[anywhere] * (2 * len(hs) + 3),
        out_specs=[in_vmem] * (3 + len(cuts)),
        scratch_shapes=[
            pltpu.VMEM((rows, width), BF16),
            pltpu.VMEM((rows, width), BF16),
            pltpu.VMEM((depth, width), BF16),
            pltpu.VMEM((depth, width), BF16),
            pltpu.VMEM((depth, width), BF16),
            pltpu.VMEM((rows, width), F32),
            pltpu.SemaphoreType.DMA((2 * len(hs),)),
            pltpu.SemaphoreType.DMA((3 * len(tiles),)),
        ],
        cost_estimate=LIGHT,
        compiler_params=BIG,
    )(*hs, *dys, w_g, w_u, w_d)


def widen_body(in_ref, *outs):
    first = 0
    for out in outs:
        size = out.shape[0]
        out[...] = in_ref[first : first + size, :].astype(F32)
        first += size


def widen(value, parts):
    rows, width = value.shape
    if rows // parts % 16:
        return [v.astype(F32) for v in jnp.split(value, parts)]
    columns = 2 * BLOCK
    size = rows // parts
    return pl.pallas_call(
        widen_body,
        grid=(width // columns,),
        in_specs=[pl.BlockSpec((rows, columns), lambda n: (0, n))],
        out_specs=[pl.BlockSpec((size, columns), lambda n: (0, n))] * parts,
        out_shape=[shaped(size, width)] * parts,
        cost_estimate=LIGHT,
        compiler_params=BIG,
    )(value)


def hidden_down_body(count, *refs):
    acts, w_ref, outs = refs[:count], refs[count], refs[count + 1 :]
    columns = 2 * BLOCK

    def column(n, _):
        here = pl.ds(pl.multiple_of(n * columns, columns), columns)
        for act, out in zip(acts, outs):
            out[:, here] = jnp.dot(
                act[...], w_ref[:, here], preferred_element_type=F32
            ).astype(BF16)
        return 0

    lax.fori_loop(0, w_ref.shape[1] // columns, column, 0)


def hidden_down(acts, w_down):
    depth, width = w_down.shape
    if sum(a.shape[0] for a in acts) > 2048:
        return [jnp.dot(a, w_down, preferred_element_type=F32).astype(BF16) for a in acts]
    in_vmem = pl.BlockSpec(memory_space=pltpu.VMEM)
    return pl.pallas_call(
        functools.partial(hidden_down_body, len(acts)),
        out_shape=[shaped(a.shape[0], width, BF16) for a in acts],
        in_specs=[in_vmem] * (len(acts) + 1),
        out_specs=[in_vmem] * len(acts),
        cost_estimate=LIGHT,
        compiler_params=BIG,
    )(*acts, w_down)


def input_back_body(x_ref, mine_ref, got_ref, d_x_ref, gain_ref, out_ref):
    x = x_ref[...].astype(F32)
    scaled = (mine_ref[...] + got_ref[...].astype(F32)) * gain_ref[...]
    r = lax.rsqrt(jnp.mean(x * x, axis=-1, keepdims=True) + EPS)
    along = jnp.mean(scaled * x, axis=-1, keepdims=True)
    out_ref[...] = d_x_ref[...] + r * scaled - (r * r * r) * along * x


def input_back(x, mine, got, d_x, gain):
    in_vmem = pl.BlockSpec(memory_space=pltpu.VMEM)
    return pl.pallas_call(
        input_back_body,
        out_shape=shaped(*x.shape),
        in_specs=[in_vmem] * 5,
        out_specs=in_vmem,
        cost_estimate=LIGHT,
        compiler_params=BIG,
    )(x, mine, got, d_x, gain)


def ring_parts(mine, theirs):
    def part(k):
        return Part(lambda a, b: a[k].astype(F32) + b[k].astype(F32), mine, theirs)

    return [part(k) for k in range(mine.shape[0])]


def ordered(ring_tensor, own, other):
    first = jnp.where(ring_tensor == 0, own, other)
    second = jnp.where(ring_tensor == 0, other, own)
    return jnp.concatenate([first, second])


def per_device(
    block_input,
    starts,
    cotangent,
    gain_mixer,
    w_branch,
    w_signal,
    w_input_gate,
    w_decay_gate,
    conv_taps,
    decay_param,
    w_mixout,
    gain_dense,
    w_gate,
    w_up,
    w_down,
):
    ring = Ring()
    side = lax.axis_index("tensor")
    count = lax.axis_size("dp")
    group = starts.shape[0]
    rows, width = block_input.shape
    shard = w_branch.shape[1]
    channels = shard * count
    lag = CONV - 1
    hops = -(-MAXLEN // group)
    heads_here = w_input_gate.shape[0]

    order = Order()
    mine_at, theirs_at = side * rows, (1 - side) * rows

    small = jnp.concatenate(
        [gain_mixer, gain_dense, conv_taps.reshape(-1), decay_param]
    )
    n_small = small.shape[0]
    small = jnp.pad(small, (0, 16 * width - n_small)).reshape(16, width)
    n_gate = w_input_gate.shape[1]
    gates = jnp.concatenate(
        [jnp.swapaxes(w, 0, 1).reshape(n_gate, channels) for w in (w_input_gate, w_decay_gate)],
        axis=1,
    )
    one = Gather(ring, order, jnp.concatenate([w_signal.T, gates, small]), True)
    order.token = one.own
    one.start()
    x_other = tensor_swap(block_input)
    hid_g, hid_u, hid_d = [holders_gather(w) for w in (w_gate.T, w_up.T, w_down)]
    pack_two = order.run(lambda *w: jnp.concatenate(w), w_branch.T, w_mixout)
    cumulative = jnp.cumsum(starts)
    padded_cum = jnp.concatenate([jnp.zeros((lag,), jnp.int32), cumulative])
    masks = [
        (cumulative - padded_cum[lag - k : lag - k + group] == 0).astype(F32)
        for k in range(CONV)
    ]
    marks = jnp.stack(masks + [starts.astype(F32)] * (8 - CONV), axis=1)
    tail_keep = (cumulative[group - 1] - cumulative[group - HALO :] == 0)[:, None]
    one.next()
    x_low = order.run(functools.partial(ordered, side), block_input, x_other)
    halo = from_behind(x_low[group - HALO :] * tail_keep.astype(BF16), 1)
    one.next()
    one.next()

    two = Gather(ring, order, pack_two, True)
    two.start()
    one.finish()
    wide_s, wide_gates, wide_small = order.run(
        lambda *_: assemble_whole(ring, (shard, n_gate, 16), one), one.theirs[-1][0]
    )
    wide_small = wide_small.reshape(count, 16, width)[:, 0]
    n_gain = gain_mixer.shape[0]
    gain_one = wide_small[:, :n_gain].reshape(width).astype(F32)
    gain_two = wide_small[:, n_gain : 2 * n_gain].reshape(width).astype(F32)
    taps = wide_small[:, 2 * n_gain : 2 * n_gain + shard * CONV]
    taps = taps.reshape(channels, CONV)
    param = wide_small[:, 2 * n_gain + shard * CONV : n_small].reshape(channels, 1)
    params = jnp.concatenate([taps] + [param] * (8 - CONV), axis=1).T.astype(F32)
    h_pad = order.run(
        lambda x, g: normed(x.astype(F32), g).astype(BF16),
        jnp.concatenate([halo, x_low]),
        gain_one,
    )
    h_one = h_pad[HALO:]
    two.next()
    padded = order.run(lambda h, w: cols_inner(h, w).astype(BF16), h_pad, wide_s)
    mixed, decay, prods, local_state, ends = order.run(
        mix, padded, marks, params, wide_gates
    )
    enter = Entering(order, ends, hops, False)
    two.next()
    two.settle()
    enter.next()
    incoming = enter.finish()
    two.next()
    two.settle()
    hid_g = order.arrive(hid_g)
    near_slots = 2 * (ring.chips - 1)
    wide_two = order.run(
        lambda *_: assemble(ring, (shard, shard), two, None, 0, near_slots), two.theirs[-1][0]
    )
    two.finish()
    dy = Gather(ring, order, cotangent)
    dy.start()
    wide_b, wide_o = order.run(
        lambda _, *near: assemble(ring, (shard, shard), two, near, near_slots, near_slots + 2),
        two.theirs[-1][0],
        *wide_two,
    )
    def merge(h, w, local, p, inc):
        pre = cols_inner(h, w)
        return pre, ((local + p * inc) * gelu_tanh(pre)).astype(BF16)

    branch_pre, merged = order.run(merge, h_one, wide_b, local_state, prods, incoming)

    def mix_out(m, w, at):
        return jnp.dot(
            lax.dynamic_slice_in_dim(m, at, rows, 0), w, preferred_element_type=F32
        )

    mix_theirs = order.run(lambda m, w: mix_out(m, w, theirs_at).astype(BF16), merged, wide_o)
    mix_got = tensor_swap(mix_theirs)
    dy.next()
    mix_mine = order.run(lambda m, w: mix_out(m, w, mine_at), merged, wide_o)
    dy.next()
    x_val = block_input.astype(F32)
    x_one = order.run(lambda x, m, t: x + m + t.astype(F32), x_val, mix_mine, mix_got)
    n_two, norm_two_back = jax.vjp(normed, x_one, gain_two)
    h_own = n_two.astype(BF16)

    ff = Gather(ring, order, h_own)
    ff.start()
    acts, d_gates, d_ups, d_hs, h_list, dy_list = [], [], [], [], [], []

    def do_piece(hs, dys, cuts):
        count = len(hs)
        out = order.run(
            lambda *v: piece(v[:count], v[count : 2 * count], cuts, *v[2 * count :]),
            *hs,
            *dys,
            hid_g,
            hid_u,
            hid_d,
        )
        for kept, value in zip((acts, d_gates, d_ups), out):
            kept.append(value)
        d_hs.extend(out[3:])
        h_list.extend(hs)
        dy_list.extend(dys)

    def plain_piece(h_piece, dy_piece, w_g, w_u, w_d):
        gate_pre = cols_inner(h_piece, w_g)
        up_val = cols_inner(h_piece, w_u)
        gate_act, slope = gelu_and_slope(gate_pre)
        act = (gate_act * up_val).astype(BF16)
        d_act = cols_inner(dy_piece, w_d)
        d_gate = (d_act * up_val * slope).astype(BF16)
        d_up = (d_act * gate_act).astype(BF16)
        d_h = jnp.dot(d_gate, w_g, preferred_element_type=F32) + jnp.dot(
            d_up, w_u, preferred_element_type=F32
        )
        return act, d_gate, d_up, d_h.astype(BF16)

    def do_plain(hs, dys):
        h_piece, dy_piece = jnp.concatenate(hs), jnp.concatenate(dys)
        out = order.run(plain_piece, h_piece, dy_piece, hid_g, hid_u, hid_d)
        for kept, value in zip((acts, d_gates, d_ups, h_list, dy_list), (*out[:3], h_piece, dy_piece)):
            kept.append(value)
        parts = [out[3]]
        if h_piece.shape[0] > rows:
            parts = [out[3][:rows], out[3][rows:]]
        d_hs.extend(parts)

    do_piece((h_own,), (cotangent,), (rows,))
    dy.next()
    for step in range(ring.reach - SHOWN, ring.reach - 1):
        ff.next()
        if step == ring.reach - SHOWN:
            first = 0
        else:
            first = step
        if step == ring.reach - 3:
            dy.finish()
        for k in range(first, step + 1):
            do_plain(ff.pairs[k], dy.pairs[k])
    ff.finish()
    do_plain(ff.far, dy.far)

    def chunks(parts):
        out = plain_parts(parts[:1])
        for pair in parts[1:-1]:
            out += [Part(lambda v: v[:rows].astype(F32), pair)]
            out += [Part(lambda v: v[rows:].astype(F32), pair)]
        return out + plain_parts(parts[-1:])

    back = Scatter(ring, order, plain_parts(d_hs), rows // 2)
    back.start()
    def run_grad(which, into, lefts, rights):
        count, every = len(lefts), len(lefts) + len(rights)
        more = () if into is None else (into,)
        return order.run(
            lambda *v: hidden_grad(
                which, v[every] if more else None, v[:count], v[count:every]
            ),
            *lefts,
            *rights,
            *more,
        )

    back.next()
    downs = order.run(lambda *v: hidden_down(v[:-1], v[-1]), *acts, hid_d)
    back.next()
    hid_grads = run_grad(0, None, d_gates, h_list)
    back.next()
    hid_grads = run_grad(1, hid_grads, d_ups, h_list)

    def dense_back(d_h, dy_own):
        d_x, g_gain = norm_two_back(d_h)
        d_x = dy_own.astype(F32) + d_x
        return d_x, g_gain, d_x.astype(BF16)

    d_x_one, g_gain_two, dz_own = back.finish(dense_back, cotangent)
    dz_other = tensor_swap(dz_own)
    down = Scatter(ring, order, chunks(downs), rows // 2)
    down.start()
    hid_grads = run_grad(2, hid_grads, acts, dy_list)
    hid_grads = holders_sum(hid_grads.reshape(-1, width))
    down.next()
    d_mix = order.run(functools.partial(ordered, side), dz_own, dz_other)
    d_branch, rev_prods, rev_state, back_ends = order.run(
        back_scan, d_mix, wide_o, branch_pre, decay, prods, local_state, incoming
    )
    leave = Entering(order, back_ends, hops, True)
    down.next()
    mine_two, theirs_two = order.run(
        lambda *v: ring_grads(ring, shard, v[:2], v[2:]), d_branch, merged, h_one, d_mix
    )
    theirs_two = core_swap(theirs_two)
    down.next()
    leave.next()
    later = leave.finish()
    d_sig, sig_tail, rim, sums, g_gates = order.run(
        back_mix,
        rev_prods,
        rev_state,
        later,
        prods,
        local_state,
        incoming,
        mixed,
        padded,
        marks,
        params,
        wide_gates,
    )
    rim = from_behind(rim, -1)
    ring_two = Scatter(ring, order, ring_parts(mine_two, theirs_two), shard)
    ring_two.start()
    block_output = down.finish(lambda d, x: (x + d).astype(BF16), x_one)

    def with_rim(sig, tail, edge):
        tail = tail + edge * tail_keep[HALO - 8 :].astype(F32)
        return lax.dynamic_update_slice(sig, tail.astype(BF16), (group - 8, 0))

    d_signal = order.run(with_rim, d_sig, sig_tail, rim)

    def d_h_rows(branch, signal, w_b, w_s, at):
        return jnp.dot(
            lax.dynamic_slice_in_dim(branch, at, rows, 0), w_b, preferred_element_type=F32
        ) + jnp.dot(
            lax.dynamic_slice_in_dim(signal, at, rows, 0), w_s, preferred_element_type=F32
        )

    d_h_theirs = order.run(
        functools.partial(d_h_rows, at=theirs_at), d_branch, d_signal, wide_b, wide_s
    )
    d_h_got = tensor_swap(d_h_theirs.astype(BF16))
    ring_two.next()

    mine_last, theirs_last = order.run(
        lambda a, b, g: ring_grads(ring, shard, (a,), (b,), g), d_signal, h_one, g_gates
    )
    theirs_last = core_swap(theirs_last)
    d_h_mine = order.run(
        functools.partial(d_h_rows, at=mine_at), d_branch, d_signal, wide_b, wide_s
    )

    def gain_sum(mine, theirs, x, other, g_two):
        def unit(v):
            v = v.astype(F32)
            return v * lax.rsqrt(jnp.mean(v * v, axis=-1, keepdims=True) + EPS)

        return jnp.stack([jnp.sum(mine * unit(x) + theirs * unit(other), axis=0), g_two])

    gains = order.run(gain_sum, d_h_mine, d_h_theirs, block_input, x_other, g_gain_two)
    gains_other = tensor_swap(gains)
    ring_two.next()

    n_rows = shard * (CONV + 1) + 2 * n_gain

    def small_rows(total, gain, gain_other):
        gain = gain + gain_other
        return jnp.concatenate(
            [
                total[:CONV].T.reshape(count, shard * CONV),
                total[CONV].reshape(count, shard),
                gain[0].reshape(count, n_gain),
                gain[1].reshape(count, n_gain),
            ],
            axis=1,
        )

    smalls = order.run(small_rows, sums, gains, gains_other)
    smalls_other = core_swap(smalls)
    smalls = order.run(
        lambda a, b: jnp.pad(a + b, ((0, 0), (0, width - n_rows))), smalls, smalls_other
    )

    def last_part(k, distance):
        at = 2 * ring.chip_at(distance) + ring.core

        def cut(a, b, small):
            big = a[k].astype(F32) + b[k].astype(F32)
            return jnp.concatenate([big, lax.dynamic_slice_in_dim(small, at, 1, 0)])

        return Part(cut, mine_last, theirs_last, smalls)

    ring_last = Scatter(
        ring,
        order,
        [last_part(k, distance) for k, distance in enumerate(ring_distances(ring))],
        (shard + n_gate) // 32 * 16 or shard // 2,
    )
    grad_input = order.run(
        input_back, block_input, d_h_mine, d_h_got, d_x_one, gain_one[None, :]
    )
    def land_both():
        flight = order.arrive(*ring_two.flight, *ring_last.flight)
        ring_two.flight, ring_last.flight = flight[:2], flight[2:]

    ring_last.start()
    land_both()
    ring_two.next()
    ring_last.next()
    land_both()
    ring_last.next()
    total_two = ring_two.finish()
    s_branch = total_two[:shard].T
    s_mixout = total_two[shard:]
    ring_last.next()
    s_gate, s_up, s_down = order.run(lambda g: widen(g, 3), hid_grads)
    s_gate, s_up = s_gate.T, s_up.T
    last = ring_last.finish()
    s_signal = last[:shard].T
    s_gates = [
        jnp.swapaxes(v.reshape(n_gate, heads_here, BLOCK), 0, 1)
        for v in jnp.split(last[shard : shard + n_gate], 2, axis=1)
    ]
    s_small = last[shard + n_gate]
    s_taps = s_small[: shard * CONV].reshape(shard, CONV)
    s_param = s_small[shard * CONV : shard * (CONV + 1)]
    s_gain_one = s_small[n_rows - 2 * n_gain : n_rows - n_gain]
    s_gain_two = s_small[n_rows - n_gain : n_rows]
    return (
        block_output,
        grad_input,
        s_gain_one,
        s_branch,
        s_signal,
        s_gates[0],
        s_gates[1],
        s_taps,
        s_param,
        s_mixout,
        s_gain_two,
        s_gate,
        s_up,
        s_down,
    )


def solution(mesh):
    placed = (
        P(("dp", "tensor"), None),
        P("dp"),
        P(("dp", "tensor"), None),
        P("dp"),
        P(None, ("tensor", "dp")),
        P(None, ("tensor", "dp")),
        P("tensor", "dp", None),
        P("tensor", "dp", None),
        P(("tensor", "dp"), None),
        P(("tensor", "dp")),
        P(("tensor", "dp"), None),
        P("dp"),
        P(None, ("tensor", "dp")),
        P(None, ("tensor", "dp")),
        P(("tensor", "dp"), None),
    )
    return jax.shard_map(
        per_device,
        mesh=mesh,
        in_specs=placed,
        out_specs=(
            P(("dp", "tensor"), None),
            P(("dp", "tensor"), None),
            P("dp"),
            P(None, ("tensor", "dp")),
            P(None, ("tensor", "dp")),
            P("tensor", "dp", None),
            P("tensor", "dp", None),
            P(("tensor", "dp"), None),
            P(("tensor", "dp")),
            P(("tensor", "dp"), None),
            P("dp"),
            P(None, ("tensor", "dp")),
            P(None, ("tensor", "dp")),
            P(("tensor", "dp"), None),
        ),
        check_vma=False,
    )
```

```python
import functools

import jax
import jax.numpy as jnp
from jax import lax
from jax.experimental import pallas as pl
from jax.experimental.pallas import tpu as pltpu
from jax.sharding import PartitionSpec as P

BLOCK = 256
CONV = 4
MAXLEN = 1024
EPS = 1e-06
HALO = 16
BF16 = jnp.bfloat16
F32 = jnp.float32


def ring_order(chips):
    return list(range(0, chips, 2)) + list(range(chips - 1, 0, -2))


class Ring:
    def __init__(self):
        count = lax.axis_size("dp")
        self.chips = count // 2
        self.reach = self.chips // 2
        order = ring_order(self.chips)
        self.up_route = [
            (order[p] * 2 + c, order[(p + 1) % self.chips] * 2 + c)
            for p in range(self.chips)
            for c in range(2)
        ]
        self.down_route = [(b, a) for a, b in self.up_route]
        me = lax.axis_index("dp")
        chip = me // 2
        self.core = lax.rem(me, 2)
        self.place = jnp.where(
            lax.rem(chip, 2) == 0, chip // 2, self.chips - 1 - chip // 2
        )

    def chip_at(self, distance):
        p = lax.rem(self.place - distance + self.chips, self.chips)
        return jnp.where(p < self.reach, 2 * p, 2 * (self.chips - 1 - p) + 1)

    def up(self, value):
        return lax.ppermute(value, "dp", self.up_route)

    def down(self, value):
        return lax.ppermute(value, "dp", self.down_route)


class Order:
    def __init__(self):
        self.token = None

    def tie(self, *values):
        if self.token is not None:
            values = lax.optimization_barrier((values, self.token))[0]
        return values if len(values) > 1 else values[0]

    def arrive(self, *values):
        values = lax.optimization_barrier((values, self.token))[0]
        self.token = values[-1]
        return values if len(values) > 1 else values[0]

    def run(self, function, *values):
        values = self.tie(*values)
        out = function(*values) if isinstance(values, tuple) else function(values)
        self.token = tuple(jax.tree.leaves(out))
        return out


SHOWN = 4


class Gather:
    def __init__(self, ring, order, value, both_cores=False):
        self.ring, self.order = ring, order
        self.own = value
        self.half = value.shape[0] // 32 * 16 or value.shape[0] // 2
        self.flight = (value, value)
        self.pairs, self.far = [], None
        self.theirs = [] if both_cores else None
        self.settled = False
        self.steps = 0

    def start(self):
        self.send()
        self.swap(self.own)
        for _ in range(self.ring.reach - SHOWN):
            self.next()

    def swap(self, *values):
        if self.theirs is not None:
            self.theirs.append(tuple(core_swap(v) for v in values))

    def send(self):
        self.steps += 1
        u, d = self.order.tie(*self.flight)
        if self.steps == self.ring.reach:
            u, d = u[: self.half], d[self.half :]
        self.flight = (self.ring.up(u), self.ring.down(d))

    def land(self):
        swapped = self.theirs.pop() if self.theirs and not self.settled else ()
        self.settled = False
        landed = self.order.arrive(*swapped, *self.flight)
        self.flight = landed[len(swapped) :]
        if swapped:
            self.theirs.append(landed[: len(swapped)])

    def next(self):
        u, d = self.flight
        swapped = self.theirs.pop() if self.theirs and not self.settled else ()
        self.settled = False
        if swapped:
            *swapped, u = self.order.arrive(*swapped, u)
            self.theirs.append(tuple(swapped))
        else:
            u = self.order.arrive(u)
        self.steps += 1
        final = self.steps == self.ring.reach
        up = self.ring.up(u[: self.half] if final else u)
        d = self.order.arrive(d)
        down = self.ring.down(d[self.half :] if final else d)
        self.pairs.append((u, d))
        self.flight = (up, down)
        self.swap(u, d)

    def settle(self):
        swapped = self.order.arrive(*self.theirs.pop())
        self.theirs.append(swapped)
        self.settled = True

    def finish(self):
        self.land()
        self.far = self.flight
        self.swap(*self.far)


class Scatter:
    def __init__(self, ring, order, parts, half):
        self.ring, self.order = ring, order
        self.parts, self.half = list(parts), half
        self.steps = 0

    def start(self):
        far = self.parts.pop()
        self.flight = self.order.run(
            lambda *v: (far(v, 0, self.half), far(v, self.half, None)), *far.values
        )
        self.send()
        for _ in range(self.ring.reach - SHOWN):
            self.next()

    def send(self):
        self.steps += 1
        u, d = self.order.tie(*self.flight)
        self.flight = (self.ring.down(u), self.ring.up(d))

    def next(self):
        ahead, behind = self.parts.pop(), self.parts.pop()
        half, first = self.half, self.steps == 1

        self.steps += 1
        to_down, to_up = self.flight

        def add_up(got, *values):
            if first:
                return jnp.concatenate(
                    [ahead(values, 0, half), ahead(values, half, None, got)]
                )
            return ahead(values, 0, None, got)

        def add_down(got, *values):
            if first:
                return jnp.concatenate(
                    [behind(values, 0, half, got), behind(values, half, None)]
                )
            return behind(values, 0, None, got)

        up = self.ring.up(self.order.run(add_up, to_up, *ahead.values))
        down = self.ring.down(self.order.run(add_down, to_down, *behind.values))
        self.flight = (down, up)

    def finish(self, function=None, *more):
        own = self.parts.pop()

        def total(to_down, to_up, *values):
            count = len(own.values)
            out = own(values[:count], 0, None, to_down, to_up, F32)
            return function(out, *values[count:]) if function else out

        return self.order.run(total, *self.flight, *own.values, *more)


class Part:
    def __init__(self, cut, *values):
        self.cut, self.values = cut, values

    def __call__(self, values, first, last, *others):
        dtype = BF16
        if others and others[-1] is F32:
            others, dtype = others[:-1], F32
        total = self.cut(*values)[first:last]
        for other in others:
            total = total + other.astype(F32)
        return total.astype(dtype)


def plain_parts(values):
    return [Part(lambda v: v.astype(F32), value) for value in values]


def plus(a, b):
    return (a.astype(F32) + b.astype(F32)).astype(BF16)


def core_swap(value):
    count = lax.axis_size("dp")
    return lax.ppermute(value, "dp", [(i, i ^ 1) for i in range(count)])


def holder_groups():
    return [
        [(2 * chip + core) * 2 + side for core in range(2) for side in range(2)]
        for chip in range(lax.axis_size("dp") // 2)
    ]


def holders_gather(value):
    return lax.all_gather(
        value, ("dp", "tensor"), axis=0, tiled=True, axis_index_groups=holder_groups()
    )


def holders_sum(value):
    return lax.psum_scatter(
        value,
        ("dp", "tensor"),
        scatter_dimension=0,
        tiled=True,
        axis_index_groups=holder_groups(),
    )


def tensor_swap(value):
    return lax.ppermute(value, "tensor", [(0, 1), (1, 0)])


def from_behind(block, distance):
    devices = range(lax.axis_size("dp"))
    route = [(i - distance, i) for i in devices if i - distance in devices]
    return lax.ppermute(block, "dp", route)


class Entering:
    def __init__(self, order, window, hops, reverse):
        self.order, self.sign = order, (-1 if reverse else 1)
        size = 1
        while 4 * size < hops:
            window = follow(from_behind(window, self.sign * size), window)
            size *= 2
        self.size, self.hops, self.window = size, hops, window
        if size < hops:
            self.behind = from_behind(window, self.sign * size)

    def next(self):
        if 2 * self.size < self.hops:
            self.window = self.order.run(follow, self.behind, self.window)
            self.size *= 2
        self.near = from_behind(self.window, self.sign)
        if self.size < self.hops:
            self.rest = from_behind(self.window, self.sign * (1 + self.size))

    def finish(self):
        if self.size >= self.hops:
            return self.order.arrive(self.near)[1:]
        return self.order.run(lambda n, r: n[:1] * r[1:] + n[1:], self.near, self.rest)


def follow(first, second):
    return jnp.stack([first[0] * second[0], second[0] * first[1] + second[1]])


def normed(value, gain):
    return value * lax.rsqrt(jnp.mean(value * value, axis=-1, keepdims=True) + EPS) * gain


def gelu_tanh(value):
    return jax.nn.gelu(value, approximate=True)


GELU_IN = 0.7978845608028654
GELU_CUBE = 0.044715


def gelu_and_slope(value):
    square = value * value
    t = jnp.tanh(GELU_IN * (value + GELU_CUBE * (square * value)))
    half = 0.5 * (1.0 + t)
    slope = half + 0.5 * value * (1.0 - t * t) * (GELU_IN * (1.0 + 3.0 * GELU_CUBE * square))
    return value * half, slope


def rows_inner(left, right):
    return lax.dot_general(
        left, right, (((0,), (0,)), ((), ())), preferred_element_type=F32
    )


def cols_inner(left, right):
    return lax.dot_general(
        left, right, (((1,), (1,)), ((), ())), preferred_element_type=F32
    )


def scan_rows(reverse, a_ref, b_ref, p_ref, s_ref):
    rows, width = a_ref.shape
    blocks = rows // 8
    row = lax.broadcasted_iota(jnp.int32, (8, width), 0)

    def step(i, carry):
        p_in, s_in = carry
        at = (blocks - 1 - i) if reverse else i
        here = pl.ds(pl.multiple_of(at * 8, 8), 8)
        a = a_ref[here, :]
        b = b_ref[here, :]
        for shift in (1, 2, 4):
            turn = 8 - shift if reverse else shift
            inside = (row < 8 - shift) if reverse else (row >= shift)
            a_prev = jnp.where(inside, pltpu.roll(a, turn, 0), 1.0)
            b_prev = jnp.where(inside, pltpu.roll(b, turn, 0), 0.0)
            b = a * b_prev + b
            a = a * a_prev
        b = b + a * s_in
        a = a * p_in
        p_ref[here, :] = a
        s_ref[here, :] = b
        last = 0 if reverse else 7
        return (a[last : last + 1], b[last : last + 1])

    return lax.fori_loop(
        0, blocks, step, (jnp.ones((1, width), F32), jnp.zeros((1, width), F32))
    )


def lru_gates(mixed, w_ig, w_dg, param):
    gx_pre = jnp.dot(mixed, w_ig, preferred_element_type=F32)
    ga_pre = jnp.dot(mixed, w_dg, preferred_element_type=F32)
    return jax.nn.sigmoid(gx_pre), jax.nn.sigmoid(ga_pre), jax.nn.softplus(param)


def one_minus_square(log_a, e):
    x = 2.0 * log_a
    series = -x * (
        1.0 + x * (1 / 2 + x * (1 / 6 + x * (1 / 24 + x * (1 / 120 + x * (1 / 720)))))
    )
    return jnp.where(x > -0.3, series, 1.0 - e * e)


def mix_body(pad_ref, marks_ref, params_ref, ig_ref, dg_ref, *refs):
    mixed_ref, decay_ref, prods_ref, state_ref, ends_ref, a_scr, b_scr = refs
    block = pl.program_id(0)
    rows = mixed_ref.shape[0]
    pad = pad_ref[...].astype(F32)
    total = params_ref[0:1, :] * pad[HALO:] * marks_ref[:, 0:1]
    for k in range(1, CONV):
        behind = pltpu.roll(pad, k, 0)[HALO:]
        total = total + params_ref[k : k + 1, :] * behind * marks_ref[:, k : k + 1]
    mixed = total.astype(BF16)
    mixed_ref[...] = mixed
    gate_x, gate_a, soft = lru_gates(mixed, ig_ref[...], dg_ref[...], params_ref[CONV : CONV + 1, :])
    reset = marks_ref[:, CONV : CONV + 1]
    keep = 1.0 - reset
    log_a = -8.0 * gate_a * soft
    e = jnp.exp(log_a)
    decay = e * keep
    multiplier = jnp.sqrt(one_minus_square(log_a, e)) * keep + reset
    decay_ref[...] = decay
    here = pl.ds(pl.multiple_of(block * BLOCK, BLOCK), BLOCK)
    a_scr[:, here] = decay
    b_scr[:, here] = gate_x * mixed.astype(F32) * multiplier

    @pl.when(block == pl.num_programs(0) - 1)
    def _():
        p_end, s_end = scan_rows(False, a_scr, b_scr, prods_ref, state_ref)
        ends_ref[0:1, :] = p_end
        ends_ref[1:2, :] = s_end


def back_scan_body(dz_ref, wide_ref, pre_ref, decay_ref, prods_ref, state_ref, in_ref, *refs):
    branch_ref, rev_p_ref, rev_s_ref, ends_ref, a_scr, b_scr, first_scr = refs
    block = pl.program_id(0)
    rows = pre_ref.shape[0]
    d_merged = lax.dot_general(
        dz_ref[...], wide_ref[...], (((1,), (1,)), ((), ())), preferred_element_type=F32
    )
    branch, slope = gelu_and_slope(pre_ref[...])
    state = state_ref[...] + prods_ref[...] * in_ref[...]
    branch_ref[...] = (d_merged * state * slope).astype(BF16)
    decay = decay_ref[...]
    row = lax.broadcasted_iota(jnp.int32, decay.shape, 0)
    ahead = jnp.where(row == rows - 1, 1.0, pltpu.roll(decay, rows - 1, 0))
    here = pl.ds(pl.multiple_of(block * BLOCK, BLOCK), BLOCK)
    a_scr[:, here] = ahead
    b_scr[:, here] = d_merged * branch
    first_scr[:, here] = decay[0:8]

    @pl.when(block == pl.num_programs(0) - 1)
    def _():
        p_end, s_end = scan_rows(True, a_scr, b_scr, rev_p_ref, rev_s_ref)
        first = first_scr[0:1, :]
        ends_ref[0:1, :] = first * p_end
        ends_ref[1:2, :] = first * s_end


def back_mix_body(*refs):
    (rev_p_ref, rev_s_ref, later_ref, prods_ref, state_ref, in_ref) = refs[:6]
    (mixed_ref, pad_ref, marks_ref, params_ref, ig_ref, dg_ref) = refs[6:12]
    sig_ref, tail_ref, rim_ref, sums_ref, gates_ref = refs[12:]
    rows = mixed_ref.shape[0]
    g = rev_s_ref[...] + rev_p_ref[...] * later_ref[...]
    entering_row = in_ref[...]
    state = state_ref[...] + prods_ref[...] * entering_row
    row = lax.broadcasted_iota(jnp.int32, state.shape, 0)
    previous = jnp.where(row == 0, entering_row, pltpu.roll(state, 1, 0))
    mixed = mixed_ref[...]
    mixed_f = mixed.astype(F32)
    param = params_ref[CONV : CONV + 1, :]
    gate_x, gate_a, soft = lru_gates(mixed, ig_ref[...], dg_ref[...], param)
    reset = marks_ref[:, CONV : CONV + 1]
    keep = 1.0 - reset
    log_a = -8.0 * gate_a * soft
    e = jnp.exp(log_a)
    root = jnp.sqrt(one_minus_square(log_a, e))
    multiplier = root * keep + reset
    d_multiplier = g * gate_x * mixed_f
    d_log_a = keep * (g * previous * e - d_multiplier * (e * e) / root)
    d_gate_a = d_log_a * (-8.0 * soft)
    d_param = jnp.sum(d_log_a * (-8.0 * gate_a), axis=0, keepdims=True) * jax.nn.sigmoid(param)
    d_ga = (d_gate_a * gate_a * (1.0 - gate_a)).astype(BF16)
    d_gx = (g * mixed_f * multiplier * gate_x * (1.0 - gate_x)).astype(BF16)
    for half, d_pre in enumerate((d_gx, d_ga)):
        at = (half * pl.num_programs(0) + pl.program_id(0)) * BLOCK
        gates_ref[:, pl.ds(pl.multiple_of(at, BLOCK), BLOCK)] = lax.dot_general(
            mixed, d_pre, (((0,), (0,)), ((), ())), preferred_element_type=F32
        ).astype(BF16)
    d_mixed = (
        g * gate_x * multiplier
        + lax.dot_general(d_gx, ig_ref[...], (((1,), (1,)), ((), ())), preferred_element_type=F32)
        + lax.dot_general(d_ga, dg_ref[...], (((1,), (1,)), ((), ())), preferred_element_type=F32)
    )
    pad = pad_ref[...].astype(F32)
    front = jnp.zeros((HALO, BLOCK), F32)
    d_pad = None
    for k in range(CONV):
        masked = d_mixed * marks_ref[:, k : k + 1]
        behind = pad if k == 0 else pltpu.roll(pad, k, 0)
        sums_ref[k : k + 1, :] = jnp.sum(masked * behind[HALO:], axis=0, keepdims=True)
        term = jnp.concatenate([front, masked * params_ref[k : k + 1, :]])
        if k:
            term = pltpu.roll(term, rows + HALO - k, 0)
        d_pad = term if d_pad is None else d_pad + term
    sums_ref[CONV : CONV + 1, :] = d_param
    sums_ref[CONV + 1 : 8, :] = jnp.zeros((8 - CONV - 1, BLOCK), F32)
    rim_ref[...] = d_pad[HALO - 8 : HALO]
    sig_ref[...] = d_pad[HALO:].astype(BF16)
    tail_ref[...] = d_pad[HALO + rows - 8 :]


def rows_spec(rows):
    return pl.BlockSpec((rows, BLOCK), lambda h: (0, h))


def whole_spec(*shape):
    return pl.BlockSpec(shape, lambda h: (0,) * len(shape))


def gate_specs(heads):
    return [
        pl.BlockSpec((BLOCK, BLOCK), lambda h: (0, h)),
        pl.BlockSpec((BLOCK, BLOCK), lambda h: (0, heads + h)),
    ]


BIG = pltpu.CompilerParams(vmem_limit_bytes=48 << 20)
LIGHT = pl.CostEstimate(flops=0, bytes_accessed=0, transcendentals=0)
HEAVY = pl.CostEstimate(flops=500_000_000_000, bytes_accessed=0, transcendentals=0)


def shaped(rows, width, dtype=F32):
    return jax.ShapeDtypeStruct((rows, width), dtype)


def mix(padded, marks, params, w_gates):
    rows, width = padded.shape[0] - HALO, padded.shape[1]
    return pl.pallas_call(
        mix_body,
        grid=(width // BLOCK,),
        in_specs=[
            rows_spec(rows + HALO),
            whole_spec(rows, 8),
            rows_spec(8),
            *gate_specs(width // BLOCK),
        ],
        out_specs=[
            rows_spec(rows),
            rows_spec(rows),
            whole_spec(rows, width),
            whole_spec(rows, width),
            whole_spec(2, width),
        ],
        out_shape=[
            shaped(rows, width, BF16),
            shaped(rows, width),
            shaped(rows, width),
            shaped(rows, width),
            shaped(2, width),
        ],
        scratch_shapes=[pltpu.VMEM((rows, width), F32)] * 2,
        cost_estimate=LIGHT,
        compiler_params=BIG,
    )(padded, marks, params, w_gates, w_gates)


def back_scan(dz, wide, pre, decay, prods, state, incoming):
    rows, width = pre.shape
    depth = dz.shape[1]
    return pl.pallas_call(
        back_scan_body,
        grid=(width // BLOCK,),
        in_specs=[
            whole_spec(rows, depth),
            pl.BlockSpec((BLOCK, depth), lambda h: (h, 0)),
            rows_spec(rows),
            rows_spec(rows),
            rows_spec(rows),
            rows_spec(rows),
            rows_spec(1),
        ],
        out_specs=[
            rows_spec(rows),
            whole_spec(rows, width),
            whole_spec(rows, width),
            whole_spec(2, width),
        ],
        out_shape=[
            shaped(rows, width, BF16),
            shaped(rows, width),
            shaped(rows, width),
            shaped(2, width),
        ],
        scratch_shapes=[
            pltpu.VMEM((rows, width), F32),
            pltpu.VMEM((rows, width), F32),
            pltpu.VMEM((8, width), F32),
        ],
        cost_estimate=LIGHT,
        compiler_params=BIG,
    )(dz, wide, pre, decay, prods, state, incoming)


def back_mix(rev_p, rev_s, later, prods, state, incoming, mixed, padded, marks, params, w_gates):
    rows, width = mixed.shape
    heads = width // BLOCK
    return pl.pallas_call(
        back_mix_body,
        grid=(heads,),
        in_specs=[
            rows_spec(rows),
            rows_spec(rows),
            rows_spec(1),
            rows_spec(rows),
            rows_spec(rows),
            rows_spec(1),
            rows_spec(rows),
            rows_spec(rows + HALO),
            whole_spec(rows, 8),
            rows_spec(8),
            *gate_specs(heads),
        ],
        out_specs=[
            rows_spec(rows),
            rows_spec(8),
            rows_spec(8),
            rows_spec(8),
            whole_spec(BLOCK, 2 * width),
        ],
        out_shape=[
            shaped(rows, width, BF16),
            shaped(8, width),
            shaped(8, width),
            shaped(8, width),
            shaped(BLOCK, 2 * width, BF16),
        ],
        cost_estimate=HEAVY,
        compiler_params=BIG,
    )(rev_p, rev_s, later, prods, state, incoming, mixed, padded, marks, params, w_gates, w_gates)


def assemble_body(sizes, runs, places, at_ref, *refs):
    chunks = refs[: len(runs)]
    outs, (scratch, in_sems, out_sems) = refs[-3 - len(sizes) : -3], refs[-3:]
    loads = [
        pltpu.make_async_copy(
            chunk, scratch.at[slot, pl.ds(first, rows)], in_sems.at[i]
        )
        for i, (chunk, (slot, first, rows)) in enumerate(zip(chunks, runs))
    ]
    for load in loads:
        load.start()
    stores = []
    for slot in range(places):
        for load, run in zip(loads, runs):
            if run[0] == slot:
                load.wait()
        base = 0
        for out, size in zip(outs, sizes):
            target = pl.ds(pl.multiple_of(at_ref[slot] * size, 16), size)
            stores.append(
                pltpu.make_async_copy(
                    scratch.at[slot, pl.ds(base, size)],
                    out.at[target],
                    out_sems.at[len(stores)],
                )
            )
            stores[-1].start()
            base += size
    for store in stores:
        store.wait()


def assemble_whole(ring, sizes, gathered):
    return assemble(ring, sizes, gathered, None, 0, 2 * ring.chips)


def assemble(ring, sizes, gathered, into, low, high):
    near = [(gathered.own,)] + [(v,) for pair in gathered.pairs for v in pair]
    their = [gathered.theirs[0]]
    for pair in gathered.theirs[1 : ring.reach]:
        their += [(v,) for v in pair]
    if gathered.far is not None:
        near.append(gathered.far)
        their.append(gathered.theirs[-1])
    rows, width = gathered.own.shape
    slots = []
    for distance, mine, theirs in zip(ring_distances(ring), near, their):
        chip = ring.chip_at(distance)
        slots += [(2 * chip + ring.core, mine), (2 * chip + 1 - ring.core, theirs)]
    if any(size % 16 for size in sizes):
        if high < 2 * ring.chips:
            return list(slots[0][1])
        at = jnp.stack([place for place, _ in slots]).astype(jnp.int32)
        every = jnp.stack([jnp.concatenate(v) if len(v) > 1 else v[0] for _, v in slots])
        every = jnp.zeros_like(every).at[at].set(every)
        cuts = [sum(sizes[:i]) for i in range(len(sizes) + 1)]
        return [every[:, a:b].reshape(-1, width) for a, b in zip(cuts, cuts[1:])]
    slots = slots[low:high]
    at = jnp.stack([place for place, _ in slots]).astype(jnp.int32)
    places = len(slots)
    chunks, runs = [], []
    for slot, (_, values) in enumerate(slots):
        first = 0
        for value in values:
            chunks.append(value)
            runs.append((slot, first, value.shape[0]))
            first += value.shape[0]
    anywhere = pl.BlockSpec(memory_space=pl.ANY)
    more = [] if into is None else list(into)
    return pl.pallas_call(
        functools.partial(assemble_body, sizes, runs, places),
        out_shape=[shaped(2 * ring.chips * size, width, BF16) for size in sizes],
        in_specs=[pl.BlockSpec(memory_space=pltpu.SMEM)]
        + [anywhere] * (len(chunks) + len(more)),
        out_specs=[anywhere] * len(sizes),
        input_output_aliases={1 + len(chunks) + i: i for i in range(len(more))},
        scratch_shapes=[
            pltpu.VMEM((places, rows, width), BF16),
            pltpu.SemaphoreType.DMA((len(chunks),)),
            pltpu.SemaphoreType.DMA((places * len(sizes),)),
        ],
        cost_estimate=LIGHT,
        compiler_params=BIG,
    )(at, *chunks, *more)


def ring_distances(ring):
    out = [0]
    for k in range(1, ring.reach):
        out += [k, -k]
    return out + [ring.reach]


def ring_grads_body(shard, chips, pairs, extra, at_ref, *refs):
    lefts, rights = refs[:pairs], refs[pairs : 2 * pairs]
    rest = refs[2 * pairs :]
    if extra:
        extra_ref, rest = rest[0], rest[1:]
    mine_ref, theirs_ref, turned, full, sems = rest
    core = at_ref[chips]
    width = full.shape[2]
    copies = []

    def send(source, size, base):
        for slot in range(chips):
            for out, c in ((mine_ref, core), (theirs_ref, 1 - core)):
                first = pl.multiple_of((2 * at_ref[slot] + c) * size, 16)
                copies.append(
                    pltpu.make_async_copy(
                        source.at[pl.ds(first, size)],
                        out.at[slot, pl.ds(base, size)],
                        sems.at[len(copies)],
                    )
                )
                copies[-1].start()

    if extra:
        send(extra_ref, extra, pairs * shard)
    for pair in range(pairs):
        turned[...] = lefts[pair][...].astype(F32).T.astype(BF16)

        def column(n, _):
            here = pl.ds(pl.multiple_of(n * BLOCK, BLOCK), BLOCK)
            full[pair, :, here] = jnp.dot(
                turned[...], rights[pair][:, here], preferred_element_type=F32
            ).astype(BF16)
            return 0

        lax.fori_loop(0, width // BLOCK, column, 0)
        send(full.at[pair], shard, pair * shard)
    for copy in copies:
        copy.wait()


def ring_grads(ring, shard, lefts, rights, extra=None):
    pairs, chips = len(lefts), ring.chips
    rows, channels = lefts[0].shape
    width = rights[0].shape[1]
    more = 0 if extra is None else extra.shape[0] // (2 * chips)
    at = [ring.chip_at(distance) for distance in ring_distances(ring)]
    if shard % 16 or more % 16:
        values = [rows_inner(a, b).astype(BF16) for a, b in zip(lefts, rights)]
        values += [] if extra is None else [extra]
        values = jnp.concatenate([v.reshape(chips, 2, -1, width) for v in values], axis=2)
        values = values[jnp.stack(at)]
        return (
            lax.dynamic_index_in_dim(values, ring.core, 1, False),
            lax.dynamic_index_in_dim(values, 1 - ring.core, 1, False),
        )
    in_vmem = pl.BlockSpec(memory_space=pltpu.VMEM)
    anywhere = pl.BlockSpec(memory_space=pl.ANY)
    out = jax.ShapeDtypeStruct((chips, pairs * shard + more, width), BF16)
    return pl.pallas_call(
        functools.partial(ring_grads_body, shard, chips, pairs, more),
        out_shape=[out, out],
        in_specs=[pl.BlockSpec(memory_space=pltpu.SMEM)]
        + [in_vmem] * (2 * pairs + (extra is not None)),
        out_specs=[anywhere, anywhere],
        scratch_shapes=[
            pltpu.VMEM((channels, rows), BF16),
            pltpu.VMEM((pairs, channels, width), BF16),
            pltpu.SemaphoreType.DMA((2 * chips * (pairs + (extra is not None)),)),
        ],
        cost_estimate=LIGHT,
        compiler_params=BIG,
    )(
        jnp.stack(at + [ring.core]).astype(jnp.int32),
        *lefts,
        *rights,
        *(() if extra is None else (extra,)),
    )


def hidden_grad_body(heights, right_heights, which, *refs):
    count = len(right_heights)
    lefts, rights = refs[: len(heights)], refs[len(heights) : len(heights) + count]
    out_ref, turned, held, made, in_sems, out_sems = refs[-6:]
    parts, _, columns = held.shape
    holders, _, unit, _ = out_ref.shape
    loads, stores = [], []
    for part in range(parts):
        first = 0
        for i, height in enumerate(right_heights):
            loads.append(
                pltpu.make_async_copy(
                    rights[i].at[:, pl.ds(part * columns, columns)],
                    held.at[part, pl.ds(first, height)],
                    in_sems.at[part * count + i],
                )
            )
            loads[-1].start()
            first += height
    first = 0
    for left, height in zip(lefts, heights):
        turned[:, first : first + height] = left[...].astype(F32).T.astype(BF16)
        first += height
    for part in range(parts):
        for load in loads[part * count : (part + 1) * count]:
            load.wait()

        def column(n, _, part=part):
            here = pl.ds(pl.multiple_of(n * BLOCK, BLOCK), BLOCK)
            made[part, :, here] = jnp.dot(
                turned[...], held[part, :, here], preferred_element_type=F32
            ).astype(BF16)
            return 0

        lax.fori_loop(0, columns // BLOCK, column, 0)
        for holder in range(holders):
            stores.append(
                pltpu.make_async_copy(
                    made.at[part, pl.ds(holder * unit, unit)],
                    out_ref.at[holder, which, :, pl.ds(part * columns, columns)],
                    out_sems.at[part * holders + holder],
                )
            )
            stores[-1].start()
    for store in stores:
        store.wait()


def hidden_grad(which, into, lefts, rights):
    heights = [left.shape[0] for left in lefts]
    right_heights = [right.shape[0] for right in rights]
    depth, width = lefts[0].shape[1], rights[0].shape[1]
    unit = depth // 4
    if unit % 16 or any(height % 128 for height in heights):
        grad = rows_inner(jnp.concatenate(lefts), jnp.concatenate(rights)).astype(BF16)
        grad = grad.reshape(4, 1, unit, width)
        return grad if into is None else jnp.concatenate([into, grad], axis=1)
    parts = 2
    in_vmem = pl.BlockSpec(memory_space=pltpu.VMEM)
    anywhere = pl.BlockSpec(memory_space=pl.ANY)
    more = () if into is None else (into,)
    return pl.pallas_call(
        functools.partial(hidden_grad_body, heights, right_heights, which),
        out_shape=jax.ShapeDtypeStruct((4, 3, unit, width), BF16),
        in_specs=[in_vmem] * len(lefts) + [anywhere] * (len(rights) + len(more)),
        out_specs=anywhere,
        input_output_aliases={len(lefts) + len(rights): 0} if more else {},
        scratch_shapes=[
            pltpu.VMEM((depth, sum(heights)), BF16),
            pltpu.VMEM((parts, sum(heights), width // parts), BF16),
            pltpu.VMEM((parts, depth, width // parts), BF16),
            pltpu.SemaphoreType.DMA((parts * len(rights),)),
            pltpu.SemaphoreType.DMA((parts * 4,)),
        ],
        cost_estimate=LIGHT,
        compiler_params=BIG,
    )(*lefts, *rights, *more)


def piece_body(count, cuts, tiles, *refs):
    ins, dys, weights = refs[:count], refs[count : 2 * count], refs[2 * count : 2 * count + 3]
    act_ref, d_gate_ref, d_up_ref = refs[2 * count + 3 : 2 * count + 6]
    outs = refs[2 * count + 6 : 2 * count + 6 + len(cuts)]
    h, dy, w_g, w_u, w_d, total, row_sems, w_sems = refs[2 * count + 6 + len(cuts) :]
    row_loads, w_loads = [], []
    for to, sources in ((h, ins), (dy, dys)):
        first = 0
        for source in sources:
            size = source.shape[0]
            row_loads.append(
                pltpu.make_async_copy(
                    source, to.at[pl.ds(first, size)], row_sems.at[len(row_loads)]
                )
            )
            row_loads[-1].start()
            first += size
    for low, high in tiles:
        here = pl.ds(low, high - low)
        for source, to in zip(weights, (w_g, w_u, w_d)):
            w_loads.append(
                pltpu.make_async_copy(source.at[here], to.at[here], w_sems.at[len(w_loads)])
            )
            w_loads[-1].start()
    for load in row_loads:
        load.wait()
    for i, (low, high) in enumerate(tiles):
        for load in w_loads[3 * i : 3 * i + 3]:
            load.wait()
        gate_act, slope = gelu_and_slope(cols_inner(h[...], w_g[low:high, :]))
        up_val = cols_inner(h[...], w_u[low:high, :])
        d_act = cols_inner(dy[...], w_d[low:high, :])
        d_gate = (d_act * up_val * slope).astype(BF16)
        d_up = (d_act * gate_act).astype(BF16)
        act_ref[:, low:high] = (gate_act * up_val).astype(BF16)
        d_gate_ref[:, low:high] = d_gate
        d_up_ref[:, low:high] = d_up
        part = jnp.dot(d_gate, w_g[low:high, :], preferred_element_type=F32) + jnp.dot(
            d_up, w_u[low:high, :], preferred_element_type=F32
        )
        total[...] = part if i == 0 else total[...] + part
    first = 0
    for out, size in zip(outs, cuts):
        out[...] = total[first : first + size, :].astype(BF16)
        first += size


def piece(hs, dys, cuts, w_g, w_u, w_d):
    depth, width = w_g.shape
    rows = sum(cuts)
    tiles = [(low, min(low + BLOCK, depth)) for low in range(0, depth, BLOCK)]
    in_vmem = pl.BlockSpec(memory_space=pltpu.VMEM)
    anywhere = pl.BlockSpec(memory_space=pl.ANY)
    return pl.pallas_call(
        functools.partial(piece_body, len(hs), cuts, tiles),
        out_shape=[shaped(rows, depth, BF16)] * 3 + [shaped(cut, width, BF16) for cut in cuts],
        in_specs=[anywhere] * (2 * len(hs) + 3),
        out_specs=[in_vmem] * (3 + len(cuts)),
        scratch_shapes=[
            pltpu.VMEM((rows, width), BF16),
            pltpu.VMEM((rows, width), BF16),
            pltpu.VMEM((depth, width), BF16),
            pltpu.VMEM((depth, width), BF16),
            pltpu.VMEM((depth, width), BF16),
            pltpu.VMEM((rows, width), F32),
            pltpu.SemaphoreType.DMA((2 * len(hs),)),
            pltpu.SemaphoreType.DMA((3 * len(tiles),)),
        ],
        cost_estimate=LIGHT,
        compiler_params=BIG,
    )(*hs, *dys, w_g, w_u, w_d)


def widen_body(in_ref, *outs):
    first = 0
    for out in outs:
        size = out.shape[0]
        out[...] = in_ref[first : first + size, :].astype(F32)
        first += size


def widen(value, parts):
    rows, width = value.shape
    if rows // parts % 16:
        return [v.astype(F32) for v in jnp.split(value, parts)]
    columns = 2 * BLOCK
    size = rows // parts
    return pl.pallas_call(
        widen_body,
        grid=(width // columns,),
        in_specs=[pl.BlockSpec((rows, columns), lambda n: (0, n))],
        out_specs=[pl.BlockSpec((size, columns), lambda n: (0, n))] * parts,
        out_shape=[shaped(size, width)] * parts,
        cost_estimate=LIGHT,
        compiler_params=BIG,
    )(value)


def hidden_down_body(count, *refs):
    acts, w_ref, outs = refs[:count], refs[count], refs[count + 1 :]
    columns = 2 * BLOCK

    def column(n, _):
        here = pl.ds(pl.multiple_of(n * columns, columns), columns)
        for act, out in zip(acts, outs):
            out[:, here] = jnp.dot(
                act[...], w_ref[:, here], preferred_element_type=F32
            ).astype(BF16)
        return 0

    lax.fori_loop(0, w_ref.shape[1] // columns, column, 0)


def hidden_down(acts, w_down):
    depth, width = w_down.shape
    if sum(a.shape[0] for a in acts) > 2048:
        return [jnp.dot(a, w_down, preferred_element_type=F32).astype(BF16) for a in acts]
    in_vmem = pl.BlockSpec(memory_space=pltpu.VMEM)
    return pl.pallas_call(
        functools.partial(hidden_down_body, len(acts)),
        out_shape=[shaped(a.shape[0], width, BF16) for a in acts],
        in_specs=[in_vmem] * (len(acts) + 1),
        out_specs=[in_vmem] * len(acts),
        cost_estimate=LIGHT,
        compiler_params=BIG,
    )(*acts, w_down)


def input_back_body(x_ref, mine_ref, got_ref, d_x_ref, gain_ref, out_ref):
    x = x_ref[...].astype(F32)
    scaled = (mine_ref[...] + got_ref[...].astype(F32)) * gain_ref[...]
    r = lax.rsqrt(jnp.mean(x * x, axis=-1, keepdims=True) + EPS)
    along = jnp.mean(scaled * x, axis=-1, keepdims=True)
    out_ref[...] = d_x_ref[...] + r * scaled - (r * r * r) * along * x


def input_back(x, mine, got, d_x, gain):
    in_vmem = pl.BlockSpec(memory_space=pltpu.VMEM)
    return pl.pallas_call(
        input_back_body,
        out_shape=shaped(*x.shape),
        in_specs=[in_vmem] * 5,
        out_specs=in_vmem,
        cost_estimate=LIGHT,
        compiler_params=BIG,
    )(x, mine, got, d_x, gain)


def ring_parts(mine, theirs):
    def part(k):
        return Part(lambda a, b: a[k].astype(F32) + b[k].astype(F32), mine, theirs)

    return [part(k) for k in range(mine.shape[0])]


def ordered(ring_tensor, own, other):
    first = jnp.where(ring_tensor == 0, own, other)
    second = jnp.where(ring_tensor == 0, other, own)
    return jnp.concatenate([first, second])


def per_device(
    block_input,
    starts,
    cotangent,
    gain_mixer,
    w_branch,
    w_signal,
    w_input_gate,
    w_decay_gate,
    conv_taps,
    decay_param,
    w_mixout,
    gain_dense,
    w_gate,
    w_up,
    w_down,
):
    ring = Ring()
    side = lax.axis_index("tensor")
    count = lax.axis_size("dp")
    group = starts.shape[0]
    rows, width = block_input.shape
    shard = w_branch.shape[1]
    channels = shard * count
    lag = CONV - 1
    hops = -(-MAXLEN // group)
    heads_here = w_input_gate.shape[0]

    order = Order()
    mine_at, theirs_at = side * rows, (1 - side) * rows

    small = jnp.concatenate(
        [gain_mixer, gain_dense, conv_taps.reshape(-1), decay_param]
    )
    n_small = small.shape[0]
    small = jnp.pad(small, (0, 16 * width - n_small)).reshape(16, width)
    n_gate = w_input_gate.shape[1]
    gates = jnp.concatenate(
        [jnp.swapaxes(w, 0, 1).reshape(n_gate, channels) for w in (w_input_gate, w_decay_gate)],
        axis=1,
    )
    one = Gather(ring, order, jnp.concatenate([w_signal.T, gates, small]), True)
    order.token = one.own
    one.start()
    x_other = tensor_swap(block_input)
    hid_g, hid_u, hid_d = [holders_gather(w) for w in (w_gate.T, w_up.T, w_down)]
    pack_two = order.run(lambda *w: jnp.concatenate(w), w_branch.T, w_mixout)
    cumulative = jnp.cumsum(starts)
    padded_cum = jnp.concatenate([jnp.zeros((lag,), jnp.int32), cumulative])
    masks = [
        (cumulative - padded_cum[lag - k : lag - k + group] == 0).astype(F32)
        for k in range(CONV)
    ]
    marks = jnp.stack(masks + [starts.astype(F32)] * (8 - CONV), axis=1)
    tail_keep = (cumulative[group - 1] - cumulative[group - HALO :] == 0)[:, None]
    one.next()
    x_low = order.run(functools.partial(ordered, side), block_input, x_other)
    halo = from_behind(x_low[group - HALO :] * tail_keep.astype(BF16), 1)
    one.next()
    one.next()

    two = Gather(ring, order, pack_two, True)
    two.start()
    one.finish()
    wide_s, wide_gates, wide_small = order.run(
        lambda *_: assemble_whole(ring, (shard, n_gate, 16), one), one.theirs[-1][0]
    )
    wide_small = wide_small.reshape(count, 16, width)[:, 0]
    n_gain = gain_mixer.shape[0]
    gain_one = wide_small[:, :n_gain].reshape(width).astype(F32)
    gain_two = wide_small[:, n_gain : 2 * n_gain].reshape(width).astype(F32)
    taps = wide_small[:, 2 * n_gain : 2 * n_gain + shard * CONV]
    taps = taps.reshape(channels, CONV)
    param = wide_small[:, 2 * n_gain + shard * CONV : n_small].reshape(channels, 1)
    params = jnp.concatenate([taps] + [param] * (8 - CONV), axis=1).T.astype(F32)
    h_pad = order.run(
        lambda x, g: normed(x.astype(F32), g).astype(BF16),
        jnp.concatenate([halo, x_low]),
        gain_one,
    )
    h_one = h_pad[HALO:]
    two.next()
    padded = order.run(lambda h, w: cols_inner(h, w).astype(BF16), h_pad, wide_s)
    mixed, decay, prods, local_state, ends = order.run(
        mix, padded, marks, params, wide_gates
    )
    enter = Entering(order, ends, hops, False)
    two.next()
    two.settle()
    enter.next()
    incoming = enter.finish()
    two.next()
    two.settle()
    hid_g = order.arrive(hid_g)
    near_slots = 2 * (ring.chips - 1)
    wide_two = order.run(
        lambda *_: assemble(ring, (shard, shard), two, None, 0, near_slots), two.theirs[-1][0]
    )
    two.finish()
    dy = Gather(ring, order, cotangent)
    dy.start()
    wide_b, wide_o = order.run(
        lambda _, *near: assemble(ring, (shard, shard), two, near, near_slots, near_slots + 2),
        two.theirs[-1][0],
        *wide_two,
    )
    def merge(h, w, local, p, inc):
        pre = cols_inner(h, w)
        return pre, ((local + p * inc) * gelu_tanh(pre)).astype(BF16)

    branch_pre, merged = order.run(merge, h_one, wide_b, local_state, prods, incoming)

    def mix_out(m, w, at):
        return jnp.dot(
            lax.dynamic_slice_in_dim(m, at, rows, 0), w, preferred_element_type=F32
        )

    mix_theirs = order.run(lambda m, w: mix_out(m, w, theirs_at).astype(BF16), merged, wide_o)
    mix_got = tensor_swap(mix_theirs)
    dy.next()
    mix_mine = order.run(lambda m, w: mix_out(m, w, mine_at), merged, wide_o)
    dy.next()
    x_val = block_input.astype(F32)
    x_one = order.run(lambda x, m, t: x + m + t.astype(F32), x_val, mix_mine, mix_got)
    n_two, norm_two_back = jax.vjp(normed, x_one, gain_two)
    h_own = n_two.astype(BF16)

    ff = Gather(ring, order, h_own)
    ff.start()
    acts, d_gates, d_ups, d_hs, h_list, dy_list = [], [], [], [], [], []

    def do_piece(hs, dys, cuts):
        count = len(hs)
        out = order.run(
            lambda *v: piece(v[:count], v[count : 2 * count], cuts, *v[2 * count :]),
            *hs,
            *dys,
            hid_g,
            hid_u,
            hid_d,
        )
        for kept, value in zip((acts, d_gates, d_ups), out):
            kept.append(value)
        d_hs.extend(out[3:])
        h_list.extend(hs)
        dy_list.extend(dys)

    def plain_piece(h_piece, dy_piece, w_g, w_u, w_d):
        gate_pre = cols_inner(h_piece, w_g)
        up_val = cols_inner(h_piece, w_u)
        gate_act, slope = gelu_and_slope(gate_pre)
        act = (gate_act * up_val).astype(BF16)
        d_act = cols_inner(dy_piece, w_d)
        d_gate = (d_act * up_val * slope).astype(BF16)
        d_up = (d_act * gate_act).astype(BF16)
        d_h = jnp.dot(d_gate, w_g, preferred_element_type=F32) + jnp.dot(
            d_up, w_u, preferred_element_type=F32
        )
        return act, d_gate, d_up, d_h.astype(BF16)

    def do_plain(hs, dys):
        h_piece, dy_piece = jnp.concatenate(hs), jnp.concatenate(dys)
        out = order.run(plain_piece, h_piece, dy_piece, hid_g, hid_u, hid_d)
        for kept, value in zip((acts, d_gates, d_ups, h_list, dy_list), (*out[:3], h_piece, dy_piece)):
            kept.append(value)
        parts = [out[3]]
        if h_piece.shape[0] > rows:
            parts = [out[3][:rows], out[3][rows:]]
        d_hs.extend(parts)

    do_piece((h_own,), (cotangent,), (rows,))
    dy.next()
    for step in range(ring.reach - SHOWN, ring.reach - 1):
        ff.next()
        if step == ring.reach - SHOWN:
            first = 0
        else:
            first = step
        if step == ring.reach - 3:
            dy.finish()
        for k in range(first, step + 1):
            do_plain(ff.pairs[k], dy.pairs[k])
    ff.finish()
    do_plain(ff.far, dy.far)

    def chunks(parts):
        out = plain_parts(parts[:1])
        for pair in parts[1:-1]:
            out += [Part(lambda v: v[:rows].astype(F32), pair)]
            out += [Part(lambda v: v[rows:].astype(F32), pair)]
        return out + plain_parts(parts[-1:])

    back = Scatter(ring, order, plain_parts(d_hs), rows // 2)
    back.start()
    def run_grad(which, into, lefts, rights):
        count, every = len(lefts), len(lefts) + len(rights)
        more = () if into is None else (into,)
        return order.run(
            lambda *v: hidden_grad(
                which, v[every] if more else None, v[:count], v[count:every]
            ),
            *lefts,
            *rights,
            *more,
        )

    back.next()
    downs = order.run(lambda *v: hidden_down(v[:-1], v[-1]), *acts, hid_d)
    back.next()
    hid_grads = run_grad(0, None, d_gates, h_list)
    back.next()
    hid_grads = run_grad(1, hid_grads, d_ups, h_list)

    def dense_back(d_h, dy_own):
        d_x, g_gain = norm_two_back(d_h)
        d_x = dy_own.astype(F32) + d_x
        return d_x, g_gain, d_x.astype(BF16)

    d_x_one, g_gain_two, dz_own = back.finish(dense_back, cotangent)
    dz_other = tensor_swap(dz_own)
    down = Scatter(ring, order, chunks(downs), rows // 2)
    down.start()
    hid_grads = run_grad(2, hid_grads, acts, dy_list)
    hid_grads = holders_sum(hid_grads.reshape(-1, width))
    down.next()
    d_mix = order.run(functools.partial(ordered, side), dz_own, dz_other)
    d_branch, rev_prods, rev_state, back_ends = order.run(
        back_scan, d_mix, wide_o, branch_pre, decay, prods, local_state, incoming
    )
    leave = Entering(order, back_ends, hops, True)
    down.next()
    mine_two, theirs_two = order.run(
        lambda *v: ring_grads(ring, shard, v[:2], v[2:]), d_branch, merged, h_one, d_mix
    )
    theirs_two = core_swap(theirs_two)
    down.next()
    leave.next()
    later = leave.finish()
    d_sig, sig_tail, rim, sums, g_gates = order.run(
        back_mix,
        rev_prods,
        rev_state,
        later,
        prods,
        local_state,
        incoming,
        mixed,
        padded,
        marks,
        params,
        wide_gates,
    )
    rim = from_behind(rim, -1)
    ring_two = Scatter(ring, order, ring_parts(mine_two, theirs_two), shard)
    ring_two.start()
    block_output = down.finish(lambda d, x: (x + d).astype(BF16), x_one)

    def with_rim(sig, tail, edge):
        tail = tail + edge * tail_keep[HALO - 8 :].astype(F32)
        return lax.dynamic_update_slice(sig, tail.astype(BF16), (group - 8, 0))

    d_signal = order.run(with_rim, d_sig, sig_tail, rim)

    def d_h_rows(branch, signal, w_b, w_s, at):
        return jnp.dot(
            lax.dynamic_slice_in_dim(branch, at, rows, 0), w_b, preferred_element_type=F32
        ) + jnp.dot(
            lax.dynamic_slice_in_dim(signal, at, rows, 0), w_s, preferred_element_type=F32
        )

    d_h_theirs = order.run(
        functools.partial(d_h_rows, at=theirs_at), d_branch, d_signal, wide_b, wide_s
    )
    d_h_got = tensor_swap(d_h_theirs.astype(BF16))
    ring_two.next()

    mine_last, theirs_last = order.run(
        lambda a, b, g: ring_grads(ring, shard, (a,), (b,), g), d_signal, h_one, g_gates
    )
    theirs_last = core_swap(theirs_last)
    d_h_mine = order.run(
        functools.partial(d_h_rows, at=mine_at), d_branch, d_signal, wide_b, wide_s
    )

    def gain_sum(mine, theirs, x, other, g_two):
        def unit(v):
            v = v.astype(F32)
            return v * lax.rsqrt(jnp.mean(v * v, axis=-1, keepdims=True) + EPS)

        return jnp.stack([jnp.sum(mine * unit(x) + theirs * unit(other), axis=0), g_two])

    gains = order.run(gain_sum, d_h_mine, d_h_theirs, block_input, x_other, g_gain_two)
    gains_other = tensor_swap(gains)
    ring_two.next()

    n_rows = shard * (CONV + 1) + 2 * n_gain

    def small_rows(total, gain, gain_other):
        gain = gain + gain_other
        return jnp.concatenate(
            [
                total[:CONV].T.reshape(count, shard * CONV),
                total[CONV].reshape(count, shard),
                gain[0].reshape(count, n_gain),
                gain[1].reshape(count, n_gain),
            ],
            axis=1,
        )

    smalls = order.run(small_rows, sums, gains, gains_other)
    smalls_other = core_swap(smalls)
    smalls = order.run(
        lambda a, b: jnp.pad(a + b, ((0, 0), (0, width - n_rows))), smalls, smalls_other
    )

    def last_part(k, distance):
        at = 2 * ring.chip_at(distance) + ring.core

        def cut(a, b, small):
            big = a[k].astype(F32) + b[k].astype(F32)
            return jnp.concatenate([big, lax.dynamic_slice_in_dim(small, at, 1, 0)])

        return Part(cut, mine_last, theirs_last, smalls)

    ring_last = Scatter(
        ring,
        order,
        [last_part(k, distance) for k, distance in enumerate(ring_distances(ring))],
        (shard + n_gate) // 32 * 16 or shard // 2,
    )
    grad_input = order.run(
        input_back, block_input, d_h_mine, d_h_got, d_x_one, gain_one[None, :]
    )
    def land_both():
        flight = order.arrive(*ring_two.flight, *ring_last.flight)
        ring_two.flight, ring_last.flight = flight[:2], flight[2:]

    ring_last.start()
    land_both()
    ring_two.next()
    ring_last.next()
    land_both()
    ring_last.next()
    total_two = ring_two.finish()
    s_branch = total_two[:shard].T
    s_mixout = total_two[shard:]
    ring_last.next()
    s_gate, s_up, s_down = order.run(lambda g: widen(g, 3), hid_grads)
    s_gate, s_up = s_gate.T, s_up.T
    last = ring_last.finish()
    s_signal = last[:shard].T
    s_gates = [
        jnp.swapaxes(v.reshape(n_gate, heads_here, BLOCK), 0, 1)
        for v in jnp.split(last[shard : shard + n_gate], 2, axis=1)
    ]
    s_small = last[shard + n_gate]
    s_taps = s_small[: shard * CONV].reshape(shard, CONV)
    s_param = s_small[shard * CONV : shard * (CONV + 1)]
    s_gain_one = s_small[n_rows - 2 * n_gain : n_rows - n_gain]
    s_gain_two = s_small[n_rows - n_gain : n_rows]
    return (
        block_output,
        grad_input,
        s_gain_one,
        s_branch,
        s_signal,
        s_gates[0],
        s_gates[1],
        s_taps,
        s_param,
        s_mixout,
        s_gain_two,
        s_gate,
        s_up,
        s_down,
    )


def solution(mesh):
    placed = (
        P(("dp", "tensor"), None),
        P("dp"),
        P(("dp", "tensor"), None),
        P("dp"),
        P(None, ("tensor", "dp")),
        P(None, ("tensor", "dp")),
        P("tensor", "dp", None),
        P("tensor", "dp", None),
        P(("tensor", "dp"), None),
        P(("tensor", "dp")),
        P(("tensor", "dp"), None),
        P("dp"),
        P(None, ("tensor", "dp")),
        P(None, ("tensor", "dp")),
        P(("tensor", "dp"), None),
    )
    return jax.shard_map(
        per_device,
        mesh=mesh,
        in_specs=placed,
        out_specs=(
            P(("dp", "tensor"), None),
            P(("dp", "tensor"), None),
            P("dp"),
            P(None, ("tensor", "dp")),
            P(None, ("tensor", "dp")),
            P("tensor", "dp", None),
            P("tensor", "dp", None),
            P(("tensor", "dp"), None),
            P(("tensor", "dp")),
            P(("tensor", "dp"), None),
            P("dp"),
            P(None, ("tensor", "dp")),
            P(None, ("tensor", "dp")),
            P(("tensor", "dp"), None),
        ),
        check_vma=False,
    )
```
